32 devices in a mesh: rep: 2 (over x), adp: 16 (over z, y, core).
Axes of the slice: x: 2, y: 2, z: 4, core: 2. Of those that a mesh axis runs over, the one named last changes fastest.
Arguments:
- tokens: bfloat16 [768, 8192], P('rep', 'adp'), parts along dimension 0, may hold values from -6 to 6
- request_adapter: int32 [768, 1], P('rep'), parts along dimension 0, may hold values from 0 to 15
- adapter_storage_slot: int32 [16], replicated, may hold values from 0 to 15, each once
- cache_length: int32 [768], P(('rep', 'adp')), parts along dimension 0, may hold values from 2 to 128, as said below
- query_weight: bfloat16 [8192, 8192], P(None, 'adp'), may hold values from -0.0625 to 0.0625
- adapter_down_maps: bfloat16 [16, 8192, 64], P('adp'), may hold values from -0.0625 to 0.0625
- adapter_up_maps: bfloat16 [16, 8192, 64], P('adp'), may hold values from -0.75 to 0.75
- key_cache: bfloat16 [8, 768, 128, 128], P(None, ('rep', 'adp')), parts along dimension 1, may hold values from -250 to 250
- value_cache: bfloat16 [8, 768, 128, 128], P(None, ('rep', 'adp')), parts along dimension 1, may hold values from -6 to 6
- new_token_key: bfloat16 [768, 1024], P(('rep', 'adp')), parts along dimension 0, may hold values from -6 to 6
- new_token_value: bfloat16 [768, 1024], P(('rep', 'adp')), parts along dimension 0, may hold values from -6 to 6
- output_weight: bfloat16 [8192, 8192], P('adp'), may hold values from -0.09375 to 0.09375
Outputs:
- attn_out: bfloat16 [768, 8192], P('rep', 'adp'), parts along dimension 0
The draws below stay inside these ranges and needn't reach their ends.
There are 2 independent parts, one for each index of `rep`. The reference program is written for one: setup_inputs(seed, part) draws one part's arguments, and reference() takes and returns one part's arrays. A program takes and returns all parts, laid end to end along the dimension named above; an argument that names none is the same for every part. Nothing has to cross between parts.
Inputs may be any that keep to these rules, and one draw needn't show every extreme that they name: `request_adapter`: every adapter is named by some request of a group. `adapter_storage_slot`: each adapter id has its own slot. `cache_length`: some request holds exactly 128 positions.
All inputs are finite; a program needn't handle non-finite values.
Results may differ from the reference program's by a relative error of at most 0.011.
Values may be sent and summed in bfloat16 or wider, within the bound.
No kernel may reach another device: no remote copies, remote signals or barrier semaphores. Data moves between devices by JAX's collectives and lax.ppermute only.
A program may use at most 128 MiB of HBM per device.

```python
import jax
import jax.numpy as jnp
from jax import lax

MODEL_WIDTH = 8192
HEADS = 64
KV_HEADS = 8
HEAD_DIM = 128
ADAPTER_RANK = 64
REQS = 384
CACHE = 128
ADAPTER_TOTAL = 16


def draw_cache_length(key, part):
    key = jax.random.fold_in(key, 5)
    first, second = jax.random.split(key)
    lengths = jax.random.randint(first, (REQS,), 2, CACHE + 1)
    longest = jax.random.randint(second, (), 0, REQS)
    return jnp.where(jnp.arange(REQS) == longest, CACHE, lengths).astype(jnp.int32)


def draw_key_cache(key, part):
    key = jax.random.fold_in(key, 11)
    shape = (KV_HEADS, REQS, CACHE, HEAD_DIM)
    first = jax.random.fold_in(key, 0)
    return jax.random.normal(first, shape, jnp.float32).astype(jnp.bfloat16)


def with_spikes(values, rng, source, target, blocks, factor):
    owner, partner = [(jnp.arange(values.shape[dim]) // (values.shape[dim] // blocks)).reshape([-1 if axis == dim else 1 for axis in range(values.ndim)]) for dim in (source, target)]
    chosen = jax.random.permutation(rng, blocks)[partner]
    strong = (owner == chosen) | (owner == (partner + blocks // 2) % blocks)
    return jnp.where(strong, factor * values, values)


def block_scale(own_key, shape, cuts, low, top_value):
    factor_of = 1.0
    for axis_at, blocks in cuts:
        steps = jax.random.uniform(jax.random.fold_in(jax.random.fold_in(own_key, 6), axis_at), (blocks,), jnp.float32, low / len(cuts), top_value / len(cuts))
        factor_of = factor_of * jnp.repeat(jnp.exp(steps), shape[axis_at] // blocks).reshape((-1,) + (1,) * (len(shape) - 1 - axis_at))
    return factor_of


def choose_distinct(stream_key, rows, count, top, lift):
    order = jax.random.permutation(jax.random.fold_in(stream_key, 1), count)
    pull = order
    for power in range(3):
        pull = pull * pull // count
    pull = pull * lift // count
    tickets = jax.random.randint(jax.random.fold_in(stream_key, 2), (rows, count), 0, 4096) + pull
    holders = jax.random.permutation(jax.random.fold_in(stream_key, 3), rows)[jnp.arange(count) % rows]
    tickets = jnp.where(jnp.arange(rows)[:, None] == holders[None, :], 1 << 14, tickets)
    priority = tickets * count + jnp.arange(count)
    return lax.top_k(priority.astype(jnp.int32), top)[1].astype(jnp.int32)


def noise(own_key, dims, scale, most, cuts=(), held_as=jnp.bfloat16):
    values = jax.random.normal(own_key, dims, jnp.float32) * scale
    if len(cuts) > 0:
        values = block_scale(own_key, dims, cuts, -0.22, 0.18) * values
    return jnp.clip(values, min=-most, max=most).astype(held_as)


def noise_with(stream_key, extent, spread, limit, shards, heavy, kind=jnp.bfloat16):
    values = spread * jax.random.normal(stream_key, extent, jnp.float32)
    if shards:
        values = values * block_scale(stream_key, extent, shards, -0.22, 0.18)
    return jnp.clip(with_spikes(values, jax.random.fold_in(stream_key, 3), *heavy), -limit, limit).astype(kind)


def setup_inputs(seed: int = 0, part: int = 0) -> dict:
    seeds = jax.random.split(jax.random.key(seed), 13)
    part_splits = jax.random.split(jax.random.fold_in(seeds[12], part), 13)
    return {
        "tokens": noise(part_splits[0], (REQS, MODEL_WIDTH), 1.0, 6.0, ((1, 16),)),
        "request_adapter": choose_distinct(part_splits[1], REQS, ADAPTER_TOTAL, 1, 1024),
        "adapter_storage_slot": jax.random.permutation(seeds[2], ADAPTER_TOTAL).astype(jnp.int32),
        "cache_length": draw_cache_length(jax.random.fold_in(jax.random.fold_in(seeds[12], part), 71), part),
        "query_weight": noise(seeds[4], (MODEL_WIDTH, MODEL_WIDTH), MODEL_WIDTH ** -0.5, 0.0625, ((1, 16),)),
        "adapter_down_maps": noise(seeds[5], (ADAPTER_TOTAL, MODEL_WIDTH, ADAPTER_RANK), MODEL_WIDTH ** -0.5, 0.0625, ((0, 16),)),
        "adapter_up_maps": noise(seeds[6], (ADAPTER_TOTAL, MODEL_WIDTH, ADAPTER_RANK), ADAPTER_RANK ** -0.5, 0.75, ((0, 16),)),
        "key_cache": draw_key_cache(jax.random.fold_in(jax.random.fold_in(seeds[12], part), 71), part),
        "value_cache": noise(part_splits[8], (KV_HEADS, REQS, CACHE, HEAD_DIM), 1.0, 6.0, ((1, 16),)),
        "new_token_key": noise(part_splits[9], (REQS, KV_HEADS * HEAD_DIM), 1.0, 6.0, ((0, 16),)),
        "new_token_value": noise(part_splits[10], (REQS, KV_HEADS * HEAD_DIM), 1.0, 6.0, ((0, 16),)),
        "output_weight": noise_with(seeds[11], (MODEL_WIDTH, MODEL_WIDTH), MODEL_WIDTH ** -0.5, 0.09375, ((0, 16),), (0, 1, 16, 2.0)),
    }


def reference(tokens, request_adapter, adapter_storage_slot, cache_length, query_weight, adapter_down_maps, adapter_up_maps, key_cache, value_cache, new_token_key, new_token_value, output_weight):
    ids = request_adapter[:, 0].astype(jnp.int32)
    slot = jnp.take(adapter_storage_slot, ids).astype(jnp.int32)
    base = jnp.dot(tokens, query_weight, preferred_element_type=jnp.float32)

    def one_low(row):
        x_row, position_index = row
        down_matrix = lax.dynamic_index_in_dim(adapter_down_maps, position_index, 0, keepdims=False)
        return jnp.dot(x_row, down_matrix, preferred_element_type=jnp.float32)

    low = lax.map(one_low, (tokens, slot)).astype(jnp.bfloat16)

    def one_delta(row):
        u_row, position_index = row
        up_matrix = lax.dynamic_index_in_dim(adapter_up_maps, position_index, 0, keepdims=False)
        return jnp.dot(up_matrix, u_row, preferred_element_type=jnp.float32)

    delta = lax.map(one_delta, (low, slot))
    query = ((base + delta) * (HEAD_DIM ** -0.5)).astype(jnp.bfloat16)
    group = HEADS // KV_HEADS
    q_heads = query.reshape(REQS, KV_HEADS, group, HEAD_DIM).transpose(1, 0, 2, 3)
    k_new = new_token_key.reshape(REQS, KV_HEADS, HEAD_DIM).transpose(1, 0, 2)
    v_new = new_token_value.reshape(REQS, KV_HEADS, HEAD_DIM).transpose(1, 0, 2)
    live = (jnp.arange(CACHE)[None, :] < cache_length[:, None])[:, None, :]

    def one_head(pieces):
        q_one, k_one, v_one, kn_one, vn_one = pieces
        q_wide = q_one.astype(jnp.float32)
        scores = jnp.einsum("rge,rje->rgj", q_wide, k_one.astype(jnp.float32))
        fresh = jnp.einsum("rge,re->rg", q_wide, kn_one.astype(jnp.float32))
        scores = jnp.where(live, scores, -jnp.inf)
        top = jnp.maximum(jnp.max(scores, axis=2), fresh)
        expd = jnp.where(live, jnp.exp(scores - top[:, :, None]), 0.0)
        expf = jnp.exp(fresh - top)
        total = jnp.sum(expd, axis=2) + expf
        probs = (expd / total[:, :, None]).astype(jnp.bfloat16)
        probf = (expf / total).astype(jnp.bfloat16)
        context = jnp.einsum("rgj,rje->rge", probs.astype(jnp.float32), v_one.astype(jnp.float32))
        context = context + probf.astype(jnp.float32)[:, :, None] * vn_one.astype(jnp.float32)[:, None, :]
        return context.astype(jnp.bfloat16)

    context = lax.map(one_head, (q_heads, key_cache, value_cache, k_new, v_new))
    context = context.transpose(1, 0, 2, 3).reshape(REQS, MODEL_WIDTH)
    return jnp.dot(context, output_weight, preferred_element_type=jnp.float32).astype(jnp.bfloat16)
```

```python
import jax
import jax.numpy as jnp
from jax import lax
from jax.experimental import pallas as pl
from jax.experimental.pallas import tpu as pltpu
from jax.sharding import Mesh
from jax.sharding import PartitionSpec as P

HEADS = 64
HEAD_DIM = 128
ADP = ("chip", "core")
SWAP = ((0, 1), (1, 0))


def project_kernel(core, own, other, w_own, w_other, a_own, a_other, mine, base, low):
    @pl.when(pl.program_id(0) == 0)
    def _():
        base[...] = jnp.zeros_like(base)
        low[...] = jnp.zeros_like(low)

    nt = (((1,), (1,)), ((), ()))
    x, y = own[0], other[0]
    base[...] += jnp.dot(x, w_own[...], preferred_element_type=jnp.float32) + jnp.dot(
        y, w_other[...], preferred_element_type=jnp.float32
    )
    low[...] += lax.dot_general(x, a_own[0], nt, preferred_element_type=jnp.float32)
    low[...] += lax.dot_general(y, a_other[0], nt, preferred_element_type=jnp.float32)

    @pl.when(pl.program_id(0) == pl.num_programs(0) - 1)
    def _():
        low[...] = low[...] * mine[...]


def project(core, own, other, weight, down, mine):
    chips, rows, width = own.shape
    cols, rank = weight.shape[1], down.shape[1]
    piece = pl.BlockSpec((1, rows, width), lambda k, c: (k, 0, 0))
    return pl.pallas_call(
        project_kernel,
        grid_spec=pltpu.PrefetchScalarGridSpec(
            num_scalar_prefetch=1,
            grid=(chips,),
            in_specs=[
                piece,
                piece,
                pl.BlockSpec((width, cols), lambda k, c: (2 * k + c[0], 0)),
                pl.BlockSpec((width, cols), lambda k, c: (2 * k + 1 - c[0], 0)),
                pl.BlockSpec((1, rank, width), lambda k, c: (0, 0, 2 * k + c[0])),
                pl.BlockSpec((1, rank, width), lambda k, c: (0, 0, 2 * k + 1 - c[0])),
                pl.BlockSpec((rows, 1), lambda k, c: (0, 0)),
            ],
            out_specs=[
                pl.BlockSpec((rows, cols), lambda k, c: (0, 0)),
                pl.BlockSpec((rows, rank), lambda k, c: (0, 0)),
            ],
        ),
        out_shape=[
            jax.ShapeDtypeStruct((rows, cols), jnp.float32),
            jax.ShapeDtypeStruct((rows, rank), jnp.float32),
        ],
        compiler_params=pltpu.CompilerParams(vmem_limit_bytes=32 << 20),
        cost_estimate=pl.CostEstimate(
            flops=4 * chips * rows * width * (cols + rank),
            bytes_accessed=4 * chips * width * (rows + cols),
            transcendentals=0,
        ),
    )(core, own, other, weight, weight, down, down, mine)


def output_kernel(core, own, other, w_own, w_other, out):
    total = jnp.dot(own[...], w_own[...], preferred_element_type=jnp.float32)
    total += jnp.dot(other[...], w_other[0], preferred_element_type=jnp.float32)
    out[0] = total.astype(out.dtype)


def output_partial(core, own, other, weight, weight_other):
    rows, depth = own.shape
    chips, _, width = weight_other.shape
    whole = pl.BlockSpec((rows, depth), lambda k, c: (0, 0))
    return pl.pallas_call(
        output_kernel,
        grid_spec=pltpu.PrefetchScalarGridSpec(
            num_scalar_prefetch=1,
            grid=(chips,),
            in_specs=[
                whole,
                whole,
                pl.BlockSpec((depth, width), lambda k, c: (0, 2 * k + c[0])),
                pl.BlockSpec((1, depth, width), lambda k, c: (k, 0, 0)),
            ],
            out_specs=pl.BlockSpec((1, rows, width), lambda k, c: (k, 0, 0)),
        ),
        out_shape=jax.ShapeDtypeStruct((chips, rows, width), jnp.bfloat16),
        compiler_params=pltpu.CompilerParams(vmem_limit_bytes=32 << 20),
        cost_estimate=pl.CostEstimate(
            flops=4 * chips * rows * width * depth,
            bytes_accessed=2 * chips * width * (rows + 2 * depth),
            transcendentals=0,
        ),
    )(core, own, other, weight, weight_other)


def attention(query, cache_length, key_cache, value_cache, k_new, v_new):
    local_reqs = query.shape[0]
    kv_count, _, span, dim = key_cache.shape
    group = HEADS // kv_count
    query = query.reshape(local_reqs, kv_count, group, dim)
    k_new = k_new.reshape(local_reqs, kv_count, dim)
    v_new = v_new.reshape(local_reqs, kv_count, dim)
    live = (jnp.arange(span)[None, :] < cache_length[:, None])[None, :, None, :]
    scores = jnp.einsum("rkge,krje->krgj", query, key_cache, preferred_element_type=jnp.float32)
    fresh = jnp.einsum("rkge,rke->krg", query, k_new, preferred_element_type=jnp.float32)
    scores = jnp.where(live, scores, -jnp.inf)
    top = jnp.maximum(jnp.max(scores, axis=3), fresh)
    expd = jnp.where(live, jnp.exp(scores - top[:, :, :, None]), 0.0)
    expf = jnp.exp(fresh - top)
    total = jnp.sum(expd, axis=3) + expf
    probs = (expd / total[:, :, :, None]).astype(jnp.bfloat16)
    probf = (expf / total).astype(jnp.bfloat16)
    context = jnp.einsum("krgj,krje->rkge", probs, value_cache, preferred_element_type=jnp.float32)
    fresh_part = jnp.einsum("krg,rke->rkge", probf.astype(jnp.float32), v_new.astype(jnp.float32))
    return (context + fresh_part).astype(jnp.bfloat16).reshape(local_reqs, HEADS * dim)


def shards(
    tokens,
    request_adapter,
    adapter_storage_slot,
    cache_length,
    query_weight,
    adapter_down_maps,
    adapter_up_maps,
    key_cache,
    value_cache,
    new_token_key,
    new_token_value,
    output_weight,
):
    chips = lax.axis_size("chip")
    core = lax.axis_index("core")
    core_arg = core.astype(jnp.int32).reshape(1)
    rows, width = tokens.shape
    total_adapters = adapter_storage_slot.shape[0]
    rank = adapter_down_maps.shape[2]

    gathered = lax.all_gather(tokens, "chip", axis=0)
    up = lax.all_to_all(
        jnp.swapaxes(adapter_up_maps, 1, 2)[0], ADP, split_axis=1, concat_axis=0, tiled=True
    )
    weight_pairs = output_weight.reshape(output_weight.shape[0], chips, 2, width)
    weight_sent = lax.dynamic_index_in_dim(weight_pairs, 1 - core, 2, keepdims=False)
    weight_other = lax.ppermute(jnp.swapaxes(weight_sent, 0, 1), "core", SWAP)

    ids = request_adapter[:, 0]
    numbers = jnp.arange(total_adapters, dtype=jnp.int32)
    slot = jnp.sum(
        jnp.where(ids[:, None] == numbers[None, :], adapter_storage_slot[None, :], 0), axis=1
    )
    mine = (slot == lax.axis_index(ADP)).astype(jnp.float32)[:, None]

    other = lax.ppermute(gathered, "core", SWAP)
    base, low = project(
        core_arg, gathered, other, query_weight, jnp.swapaxes(adapter_down_maps, 1, 2), mine
    )
    low = lax.psum(low.astype(jnp.bfloat16), ADP)
    owner = jnp.arange(total_adapters * rank, dtype=jnp.int32) // rank
    spread = jnp.where(
        slot[:, None] == owner[None, :], jnp.tile(low, (1, total_adapters)), 0
    ).astype(jnp.bfloat16)
    delta = jnp.dot(spread, up, preferred_element_type=jnp.float32)
    query = ((base + delta) * HEAD_DIM ** (-0.5)).astype(jnp.bfloat16)
    query_local = lax.all_to_all(query, ADP, split_axis=0, concat_axis=1, tiled=True)

    context = attention(
        query_local, cache_length, key_cache, value_cache, new_token_key, new_token_value
    )
    context = lax.all_to_all(context, ADP, split_axis=1, concat_axis=0, tiled=True)
    context_other = lax.ppermute(context, "core", SWAP)
    partial_out = output_partial(core_arg, context, context_other, output_weight, weight_other)
    return lax.psum_scatter(partial_out, "chip", scatter_dimension=0)


def solution(mesh):
    reps, adp = mesh.shape["rep"], mesh.shape["adp"]
    mesh = Mesh(mesh.devices.reshape(reps, adp // 2, 2), ("rep",) + ADP)
    in_specs = (
        P("rep", ADP),
        P("rep", None),
        P(),
        P(("rep",) + ADP),
        P(None, ADP),
        P(ADP, None, None),
        P(ADP, None, None),
        P(None, ("rep",) + ADP, None, None),
        P(None, ("rep",) + ADP, None, None),
        P(("rep",) + ADP, None),
        P(("rep",) + ADP, None),
        P(ADP, None),
    )
    return jax.shard_map(
        shards, mesh=mesh, in_specs=in_specs, out_specs=P("rep", ADP), check_vma=False
    )
```

```python
import jax
import jax.numpy as jnp
from jax import lax
from jax.experimental import pallas as pl
from jax.experimental.pallas import tpu as pltpu
from jax.sharding import Mesh
from jax.sharding import PartitionSpec as P

HEADS = 64
HEAD_DIM = 128
ADP = ("z", "y", "core")


def project_kernel(places, *refs):
    count = places.shape[0]
    blocks, weights, downs = refs[:count], refs[count : 2 * count], refs[2 * count : 3 * count]
    base_in, low_in, base, low = refs[3 * count :]
    total = base_in[...]
    for block, weight in zip(blocks, weights):
        total += jnp.dot(block[...], weight[...], preferred_element_type=jnp.float32)
    base[...] = total

    @pl.when(pl.program_id(0) == 0)
    def _():
        nt = (((1,), (1,)), ((), ()))
        part = low_in[...]
        for block, down in zip(blocks, downs):
            part += lax.dot_general(block[...], down[0], nt, preferred_element_type=jnp.float32)
        low[...] = part


def project(places, blocks, weight, down, base, low):
    count = len(blocks)
    rows, width = blocks[0].shape
    cols, rank = base.shape[1], low.shape[1]
    tile = cols // 2 if cols % 256 == 0 else cols
    flat = pl.BlockSpec((rows, width), lambda j, p: (0, 0))
    base_spec = pl.BlockSpec((rows, tile), lambda j, p: (0, j))
    low_spec = pl.BlockSpec((rows, rank), lambda j, p: (0, 0))
    return pl.pallas_call(
        project_kernel,
        grid_spec=pltpu.PrefetchScalarGridSpec(
            num_scalar_prefetch=1,
            grid=(cols // tile,),
            in_specs=[flat] * count
            + [pl.BlockSpec((width, tile), lambda j, p, i=i: (p[i], j)) for i in range(count)]
            + [pl.BlockSpec((1, rank, width), lambda j, p, i=i: (0, 0, p[i])) for i in range(count)]
            + [base_spec, low_spec],
            out_specs=[base_spec, low_spec],
        ),
        out_shape=[
            jax.ShapeDtypeStruct((rows, cols), jnp.float32),
            jax.ShapeDtypeStruct((rows, rank), jnp.float32),
        ],
        compiler_params=pltpu.CompilerParams(vmem_limit_bytes=32 << 20),
        cost_estimate=pl.CostEstimate(
            flops=2 * count * rows * width * (cols + rank),
            bytes_accessed=2 * count * width * (rows + cols) + 8 * rows * cols,
            transcendentals=0,
        ),
    )(places, *blocks, *[weight] * count, *[down] * count, base, low)


def slice_kernel(core, weight, out):
    out[0] = weight[...]


def other_columns(core, weight, width):
    depth, cols = weight.shape
    chips = cols // (2 * width)
    return pl.pallas_call(
        slice_kernel,
        grid_spec=pltpu.PrefetchScalarGridSpec(
            num_scalar_prefetch=1,
            grid=(chips,),
            in_specs=[pl.BlockSpec((depth, width), lambda k, c: (0, 2 * k + 1 - c[0]))],
            out_specs=pl.BlockSpec((1, depth, width), lambda k, c: (k, 0, 0)),
        ),
        out_shape=jax.ShapeDtypeStruct((chips, depth, width), weight.dtype),
        cost_estimate=pl.CostEstimate(
            flops=0, bytes_accessed=4 * chips * depth * width, transcendentals=0
        ),
    )(core, weight)


def output_kernel(places, own, other, *refs):
    count = places.shape[0] // 2
    for w_own, w_other, out in zip(refs[:count], refs[count : 2 * count], refs[2 * count :]):
        total = jnp.dot(own[...], w_own[...], preferred_element_type=jnp.float32)
        total += jnp.dot(other[...], w_other[0], preferred_element_type=jnp.float32)
        out[...] = total.astype(out.dtype)


def output_partial(places, own, other, weight, weight_other):
    rows, depth = own.shape
    width = weight_other.shape[2]
    count = places.shape[0] // 2
    tile = width // 2 if width % 256 == 0 else width
    steps = width // tile
    whole = pl.BlockSpec((rows, depth), lambda j, p: (0, 0))
    return pl.pallas_call(
        output_kernel,
        grid_spec=pltpu.PrefetchScalarGridSpec(
            num_scalar_prefetch=1,
            grid=(steps,),
            in_specs=[whole, whole]
            + [
                pl.BlockSpec((depth, tile), lambda j, p, i=i: (0, p[i] * steps + j))
                for i in range(count)
            ]
            + [
                pl.BlockSpec((1, depth, tile), lambda j, p, i=i: (p[count + i], 0, j))
                for i in range(count)
            ],
            out_specs=[pl.BlockSpec((rows, tile), lambda j, p: (0, j))] * count,
        ),
        out_shape=[jax.ShapeDtypeStruct((rows, width), jnp.bfloat16)] * count,
        compiler_params=pltpu.CompilerParams(vmem_limit_bytes=32 << 20),
        cost_estimate=pl.CostEstimate(
            flops=4 * count * rows * width * depth,
            bytes_accessed=2 * count * width * (rows + 2 * depth) + 4 * rows * depth,
            transcendentals=0,
        ),
    )(places, own, other, *[weight] * count, *[weight_other] * count)


def shift(value, axis, by):
    size = lax.axis_size(axis)
    return lax.ppermute(value, axis, [(i, (i + by) % size) for i in range(size)])


def attention(query, cache_length, key_cache, value_cache, k_new, v_new):
    local_reqs = query.shape[0]
    kv_count, _, span, dim = key_cache.shape
    group = HEADS // kv_count
    query = query.reshape(local_reqs, kv_count, group, dim)
    k_new = k_new.reshape(local_reqs, kv_count, dim)
    v_new = v_new.reshape(local_reqs, kv_count, dim)
    live = (jnp.arange(span)[None, :] < cache_length[:, None])[None, :, None, :]
    scores = jnp.einsum("rkge,krje->krgj", query, key_cache, preferred_element_type=jnp.float32)
    fresh = jnp.einsum("rkge,rke->krg", query, k_new, preferred_element_type=jnp.float32)
    scores = jnp.where(live, scores, -jnp.inf)
    top = jnp.maximum(jnp.max(scores, axis=3), fresh)
    expd = jnp.where(live, jnp.exp(scores - top[:, :, :, None]), 0.0)
    expf = jnp.exp(fresh - top)
    total = jnp.sum(expd, axis=3) + expf
    probs = (expd / total[:, :, :, None]).astype(jnp.bfloat16)
    probf = (expf / total).astype(jnp.bfloat16)
    context = jnp.einsum("krgj,krje->rkge", probs, value_cache, preferred_element_type=jnp.float32)
    fresh_part = jnp.einsum("krg,rke->rkge", probf.astype(jnp.float32), v_new.astype(jnp.float32))
    return (context + fresh_part).astype(jnp.bfloat16).reshape(local_reqs, HEADS * dim)


def shards(
    tokens,
    request_adapter,
    adapter_storage_slot,
    cache_length,
    query_weight,
    adapter_down_maps,
    adapter_up_maps,
    key_cache,
    value_cache,
    new_token_key,
    new_token_value,
    output_weight,
):
    layers, sides = lax.axis_size("z"), lax.axis_size("y")
    z, y, core = lax.axis_index("z"), lax.axis_index("y"), lax.axis_index("core")
    core_arg = core.astype(jnp.int32).reshape(1)
    rows, width = tokens.shape
    total_adapters = adapter_storage_slot.shape[0]
    rank = adapter_down_maps.shape[2]

    blocks = []
    for k in range(layers):
        layer = [shift(tokens, "z", k) if k else tokens]
        layer += [shift(layer[0], "y", 1)] if sides == 2 else []
        blocks.append(layer + [shift(block, "core", 1) for block in layer])
    up = lax.all_to_all(
        jnp.swapaxes(adapter_up_maps, 1, 2)[0], ADP, split_axis=1, concat_axis=0, tiled=True
    )
    weight_other = shift(other_columns(core_arg, output_weight, width), "core", 1)

    ids = request_adapter[:, 0]
    numbers = jnp.arange(total_adapters, dtype=jnp.int32)
    slot = jnp.sum(
        jnp.where(ids[:, None] == numbers[None, :], adapter_storage_slot[None, :], 0), axis=1
    )
    mine = (slot == lax.axis_index(ADP))[:, None]

    base = jnp.zeros((rows, query_weight.shape[1]), jnp.float32)
    low = jnp.zeros((rows, rank), jnp.float32)
    down = jnp.swapaxes(adapter_down_maps, 1, 2)
    for k in range(layers):
        layer = ((z - k) % layers) * (2 * sides)
        places = jnp.stack(
            [layer + 2 * ((y + side) % sides) + (core + c) % 2 for c in (0, 1) for side in range(sides)]
        ).astype(jnp.int32)
        base, low = project(places, blocks[k], query_weight, down, base, low)

    low = jnp.where(mine, low, 0).astype(jnp.bfloat16)
    low = low + shift(low, "core", 1)
    if sides == 2:
        low = low + shift(low, "y", 1)
    step = 1
    while step < layers:
        low = low + lax.ppermute(low, "z", [(i, i ^ step) for i in range(layers)])
        step *= 2

    owner = jnp.arange(total_adapters * rank, dtype=jnp.int32) // rank
    spread = jnp.where(
        slot[:, None] == owner[None, :], jnp.tile(low, (1, total_adapters)), 0
    ).astype(jnp.bfloat16)
    delta = jnp.dot(spread, up, preferred_element_type=jnp.float32)
    query = ((base + delta) * HEAD_DIM ** (-0.5)).astype(jnp.bfloat16)
    query_local = lax.all_to_all(query, ADP, split_axis=0, concat_axis=1, tiled=True)

    context = attention(
        query_local, cache_length, key_cache, value_cache, new_token_key, new_token_value
    )
    context = lax.all_to_all(context, ADP, split_axis=1, concat_axis=0, tiled=True)
    context_other = shift(context, "core", 1)

    total = None
    for k in list(range(1, layers)) + [0]:
        layer = ((z + k) % layers) * sides
        chips = [layer + (y + side) % sides for side in range(sides)]
        places = jnp.stack([2 * chip + core for chip in chips] + chips).astype(jnp.int32)
        parts = output_partial(places, context, context_other, output_weight, weight_other)
        part = parts[0].astype(jnp.float32)
        if sides == 2:
            part = part + shift(parts[1], "y", 1).astype(jnp.float32)
        if k:
            part = shift(part.astype(jnp.bfloat16), "z", k).astype(jnp.float32)
        total = part if total is None else total + part
    return total.astype(jnp.bfloat16)


def solution(mesh):
    reps, adp = mesh.shape["rep"], mesh.shape["adp"]
    sides = 2 if adp == 16 else 1
    mesh = Mesh(mesh.devices.reshape(reps, adp // (2 * sides), sides, 2), ("rep",) + ADP)
    in_specs = (
        P("rep", ADP),
        P("rep", None),
        P(),
        P(("rep",) + ADP),
        P(None, ADP),
        P(ADP, None, None),
        P(ADP, None, None),
        P(None, ("rep",) + ADP, None, None),
        P(None, ("rep",) + ADP, None, None),
        P(("rep",) + ADP, None),
        P(("rep",) + ADP, None),
        P(ADP, None),
    )
    return jax.shard_map(
        shards, mesh=mesh, in_specs=in_specs, out_specs=P("rep", ADP), check_vma=False
    )
```

```python
import jax
import jax.numpy as jnp
from jax import lax
from jax.experimental import pallas as pl
from jax.experimental.pallas import tpu as pltpu
from jax.sharding import Mesh
from jax.sharding import PartitionSpec as P

HEADS = 64
HEAD_DIM = 128
ADP = ("z", "y", "core")
NT = (((1,), (1,)), ((), ()))
VMEM_LIMIT = 56 << 20


def slices_kernel(core, query_weight, down, output_weight, query_out, down_out, out_out, sems):
    chips, width = query_out.shape[0], query_out.shape[1]
    copies = []
    for k in range(chips):
        span = pl.ds(pl.multiple_of((2 * k + 1 - core[0]) * width, width), width)
        copies += [
            pltpu.make_async_copy(query_weight.at[span, :], query_out.at[k], sems.at[0, k]),
            pltpu.make_async_copy(down.at[0, :, span], down_out.at[k], sems.at[1, k]),
            pltpu.make_async_copy(output_weight.at[:, span], out_out.at[k], sems.at[2, k]),
        ]
    for copy in copies:
        copy.start()
    for copy in copies:
        copy.wait()


def other_slices(core, query_weight, down, output_weight, chips, width):
    cols, rank, depth = query_weight.shape[1], down.shape[1], output_weight.shape[0]
    shapes = [(chips, width, cols), (chips, rank, width), (chips, depth, width)]
    hbm = pl.BlockSpec(memory_space=pl.ANY)
    return pl.pallas_call(
        slices_kernel,
        in_specs=[pl.BlockSpec(memory_space=pltpu.SMEM), hbm, hbm, hbm],
        out_specs=[hbm] * 3,
        out_shape=[jax.ShapeDtypeStruct(shape, query_weight.dtype) for shape in shapes],
        scratch_shapes=[pltpu.SemaphoreType.DMA((3, chips))],
        cost_estimate=pl.CostEstimate(
            flops=0,
            bytes_accessed=4 * chips * width * (cols + rank + depth),
            transcendentals=0,
        ),
    )(core, query_weight, down, output_weight)


def project_kernel(places, *refs):
    count = places.shape[0] // 2
    blocks, w_own, w_other, a_own, a_other = (refs[i * count : (i + 1) * count] for i in range(5))
    own_out, sent_out = refs[-2:]
    cols = own_out.shape[1]
    first_core = places[0] % 2 == 0
    own = other = low = None
    if len(refs) > 5 * count + 2:
        own = refs[5 * count][...]
        other = refs[5 * count + 1][:, :cols]
        low = refs[5 * count + 1][:, cols:]
    for i in range(count):
        x = blocks[i][...]
        d_own, d_other = a_own[i][0], a_other[i][0]
        pair = jnp.concatenate(
            [jnp.where(first_core, d_own, d_other), jnp.where(first_core, d_other, d_own)], axis=0
        )
        parts = (
            jnp.dot(x, w_own[i][...], preferred_element_type=jnp.float32),
            jnp.dot(x, w_other[i][0], preferred_element_type=jnp.float32),
            lax.dot_general(x, pair, NT, preferred_element_type=jnp.float32),
        )
        own, other, low = parts if own is None else (own + parts[0], other + parts[1], low + parts[2])
    own_out[...] = own
    sent_out[:, :cols] = other
    sent_out[:, cols:] = low


def project(chips, core, blocks, weight, weight_other, down, down_other, sums):
    count = len(blocks)
    rows, width = blocks[0].shape
    cols, rank = weight.shape[1], down.shape[1]
    places = jnp.stack([2 * chip + core for chip in chips] + chips).astype(jnp.int32)
    flat = lambda shape: pl.BlockSpec(shape, lambda j, p: (0, 0))
    sum_shapes = [(rows, cols), (rows, cols + 2 * rank)]
    each = range(count)
    return pl.pallas_call(
        project_kernel,
        grid_spec=pltpu.PrefetchScalarGridSpec(
            num_scalar_prefetch=1,
            grid=(1,),
            in_specs=[flat((rows, width))] * count
            + [pl.BlockSpec((width, cols), lambda j, p, i=i: (p[i], 0)) for i in each]
            + [pl.BlockSpec((1, width, cols), lambda j, p, i=i: (p[count + i], 0, 0)) for i in each]
            + [pl.BlockSpec((1, rank, width), lambda j, p, i=i: (0, 0, p[i])) for i in each]
            + [pl.BlockSpec((1, rank, width), lambda j, p, i=i: (p[count + i], 0, 0)) for i in each]
            + [flat(shape) for shape in sum_shapes[: len(sums)]],
            out_specs=[flat(shape) for shape in sum_shapes],
        ),
        out_shape=[jax.ShapeDtypeStruct(shape, jnp.float32) for shape in sum_shapes],
        compiler_params=pltpu.CompilerParams(vmem_limit_bytes=VMEM_LIMIT),
        cost_estimate=pl.CostEstimate(
            flops=4 * count * rows * width * (cols + rank),
            bytes_accessed=2 * count * width * (rows + 2 * cols) + 8 * rows * cols,
            transcendentals=0,
        ),
    )(
        places,
        *blocks,
        *[weight] * count,
        *[weight_other] * count,
        *[down] * count,
        *[down_other] * count,
        *sums,
    )


def query_kernel(half, own, received, low, slot, up_own, up_other, out):
    step = pl.program_id(0)
    cols, lanes = own.shape[1], low.shape[1]
    rank = lanes // 2
    part = rank // 2
    depth = up_own.shape[0]
    shape = (lanes, depth)
    lane = lax.broadcasted_iota(jnp.int32, shape, 1) % part
    row = lax.broadcasted_iota(jnp.int32, shape, 0)
    owner = lax.broadcasted_iota(jnp.int32, (own.shape[0], depth), 1) // part
    live = slot[...] == owner
    total = own[...] + received[:, :cols]
    for h, up in ((half[0], up_own), (1 - half[0], up_other)):
        copies = (row == lane + rank * step + part * h).astype(jnp.bfloat16)
        spread = jnp.dot(low[...], copies, preferred_element_type=jnp.float32)
        spread = jnp.where(live, spread, 0.0).astype(jnp.bfloat16)
        total += jnp.dot(spread, up[...], preferred_element_type=jnp.float32)
    out[...] = (total * HEAD_DIM ** (-0.5)).astype(out.dtype)


def make_query(half, own, received, low, slot, up_own, up_other):
    rows, cols = own.shape
    tile = rows // 2
    depth = up_own.shape[0]
    by_rows = lambda width: pl.BlockSpec((tile, width), lambda j, h: (j, 0))
    whole = lambda array: pl.BlockSpec(array.shape, lambda j, h: (0, 0))
    return pl.pallas_call(
        query_kernel,
        grid_spec=pltpu.PrefetchScalarGridSpec(
            num_scalar_prefetch=1,
            grid=(2,),
            in_specs=[
                by_rows(cols),
                by_rows(received.shape[1]),
                whole(low),
                by_rows(1),
                whole(up_own),
                whole(up_other),
            ],
            out_specs=by_rows(cols),
        ),
        out_shape=jax.ShapeDtypeStruct((rows, cols), jnp.bfloat16),
        compiler_params=pltpu.CompilerParams(vmem_limit_bytes=VMEM_LIMIT),
        cost_estimate=pl.CostEstimate(
            flops=4 * rows * cols * depth,
            bytes_accessed=rows * cols * 10 + 4 * depth * cols,
            transcendentals=0,
        ),
    )(half, own, received, low, slot, up_own, up_other)


def output_kernel(places, own, other, *refs):
    count = places.shape[0] // 2
    for w_own, w_other, out in zip(refs[:count], refs[count : 2 * count], refs[2 * count :]):
        total = jnp.dot(own[...], w_own[...], preferred_element_type=jnp.float32)
        total += jnp.dot(other[...], w_other[0], preferred_element_type=jnp.float32)
        out[...] = total.astype(out.dtype)


def output_partial(chips, core, own, other, weight, weight_other):
    rows, depth = own.shape
    width = weight_other.shape[2]
    count = len(chips)
    places = jnp.stack([2 * chip + core for chip in chips] + chips).astype(jnp.int32)
    whole = pl.BlockSpec((rows, depth), lambda j, p: (0, 0))
    return pl.pallas_call(
        output_kernel,
        grid_spec=pltpu.PrefetchScalarGridSpec(
            num_scalar_prefetch=1,
            grid=(1,),
            in_specs=[whole, whole]
            + [pl.BlockSpec((depth, width), lambda j, p, i=i: (0, p[i])) for i in range(count)]
            + [
                pl.BlockSpec((1, depth, width), lambda j, p, i=i: (p[count + i], 0, 0))
                for i in range(count)
            ],
            out_specs=[pl.BlockSpec((rows, width), lambda j, p: (0, 0))] * count,
        ),
        out_shape=[jax.ShapeDtypeStruct((rows, width), jnp.bfloat16)] * count,
        compiler_params=pltpu.CompilerParams(vmem_limit_bytes=VMEM_LIMIT),
        cost_estimate=pl.CostEstimate(
            flops=4 * count * rows * width * depth,
            bytes_accessed=2 * count * width * (rows + 2 * depth) + 4 * rows * depth,
            transcendentals=0,
        ),
    )(places, own, other, *[weight] * count, *[weight_other] * count)


def attention(query, cache_length, key_cache, value_cache, k_new, v_new):
    local_reqs = query.shape[0]
    kv_count, _, span, dim = key_cache.shape
    group = HEADS // kv_count
    query = query.reshape(local_reqs, kv_count, group, dim)
    k_new = k_new.reshape(local_reqs, kv_count, dim)
    v_new = v_new.reshape(local_reqs, kv_count, dim)
    live = (jnp.arange(span)[None, :] < cache_length[:, None])[None, :, None, :]
    scores = jnp.einsum("rkge,krje->krgj", query, key_cache, preferred_element_type=jnp.float32)
    fresh = jnp.einsum("rkge,rke->krg", query, k_new, preferred_element_type=jnp.float32)
    scores = jnp.where(live, scores, -jnp.inf)
    top = jnp.maximum(jnp.max(scores, axis=3), fresh)
    expd = jnp.where(live, jnp.exp(scores - top[:, :, :, None]), 0.0)
    expf = jnp.exp(fresh - top)
    total = jnp.sum(expd, axis=3) + expf
    probs = (expd / total[:, :, :, None]).astype(jnp.bfloat16)
    probf = (expf / total).astype(jnp.bfloat16)
    context = jnp.einsum("krgj,krje->rkge", probs, value_cache, preferred_element_type=jnp.float32)
    fresh_part = jnp.einsum("krg,rke->rkge", probf.astype(jnp.float32), v_new.astype(jnp.float32))
    return (context + fresh_part).astype(jnp.bfloat16).reshape(local_reqs, HEADS * dim)


def shift(value, axis, by):
    size = lax.axis_size(axis)
    return lax.ppermute(value, axis, [(i, (i + by) % size) for i in range(size)])


def after(value, *others):
    return lax.optimization_barrier((value, *others))[0]


def gather_layers(tokens):
    layers = lax.axis_size("z")
    if layers != 4:
        return [shift(tokens, "z", k) if k else tokens for k in range(layers)]
    below, above = shift(tokens, "z", 1), shift(tokens, "z", 3)
    two = lax.ppermute(below, "z", [(1, 2), (2, 3)]), lax.ppermute(above, "z", [(2, 1), (1, 0)])
    return [tokens, below, jnp.where(lax.axis_index("z") >= 2, *two), above]


def scatter_layers(parts):
    layers = lax.axis_size("z")
    wide = lambda value: value.astype(jnp.float32)
    narrow = lambda value: value.astype(jnp.bfloat16)
    if layers != 4:
        return sum([wide(shift(narrow(parts[k]), "z", k)) for k in range(1, layers)], parts[0])
    two = narrow(parts[2])
    up = lax.ppermute(two, "z", [(0, 1), (1, 2)])
    down = lax.ppermute(two, "z", [(3, 2), (2, 1)])
    above = shift(narrow(parts[1] + wide(up)), "z", 1)
    below = shift(narrow(parts[3] + wide(down)), "z", 3)
    return parts[0] + wide(above) + wide(below)


def shards(
    tokens,
    request_adapter,
    adapter_storage_slot,
    cache_length,
    query_weight,
    adapter_down_maps,
    adapter_up_maps,
    key_cache,
    value_cache,
    new_token_key,
    new_token_value,
    output_weight,
):
    layers, sides = lax.axis_size("z"), lax.axis_size("y")
    z, y, core = lax.axis_index("z"), lax.axis_index("y"), lax.axis_index("core")
    core_arg = core.astype(jnp.int32).reshape(1)
    rows, width = tokens.shape
    cols = query_weight.shape[1]
    total_adapters = adapter_storage_slot.shape[0]
    rank = adapter_down_maps.shape[2]
    chips_of = lambda layer: [
        (layer % layers) * sides + (y + side) % sides for side in range(sides)
    ]

    blocks = gather_layers(tokens)
    blocks = [
        [block, shift(block, "y", 1)] if sides == 2 else [block] for block in blocks
    ]

    down = jnp.swapaxes(adapter_down_maps, 1, 2)
    sent = other_slices(core_arg, query_weight, down, output_weight, layers * sides, width)
    query_weight_other, down_other, output_weight_other = [shift(s, "core", 1) for s in sent]

    reps = lax.axis_size("rep")
    half = lax.axis_index("rep") % 2
    up = jnp.swapaxes(adapter_up_maps, 1, 2)[0]
    up = lax.dynamic_slice_in_dim(up, half * (rank // 2), rank // 2, 0)
    up = after(up, blocks[1][0], blocks[layers - 1][0])
    up = lax.all_to_all(up, ADP, split_axis=1, concat_axis=0, tiled=True)
    up_other = lax.ppermute(up, "rep", [(i, i ^ 1) for i in range(reps)])

    ids = request_adapter[:, 0]
    numbers = jnp.arange(total_adapters, dtype=jnp.int32)
    slot = jnp.sum(
        jnp.where(ids[:, None] == numbers[None, :], adapter_storage_slot[None, :], 0), axis=1
    )[:, None]

    order = [0, 1, 3, 2] if layers == 4 else list(range(layers))
    sums = []
    for group in (order[:-1], order[-1:]):
        sums = project(
            [chip for k in group for chip in chips_of(z - k)],
            core,
            [block for k in group for block in blocks[k]],
            query_weight,
            query_weight_other,
            down,
            down_other,
            sums,
        )
    own, sent = sums
    received = shift(sent, "core", 1)

    low = sent[:, cols:] + received[:, cols:]
    chip = z * sides + y
    low = jnp.where(slot == 2 * chip, low[:, :rank], 0.0) + jnp.where(
        slot == 2 * chip + 1, low[:, rank:], 0.0
    )
    low = low.astype(jnp.bfloat16)
    low = jnp.concatenate([low[: rows // 2], low[rows // 2 :]], axis=1)
    if sides == 2:
        low = low + shift(low, "y", 1)
    low = sum([shift(low, "z", k) for k in range(1, layers)], low)

    query = make_query(half.astype(jnp.int32).reshape(1), own, received, low, slot, up, up_other)
    query_local = lax.all_to_all(query, ADP, split_axis=0, concat_axis=1, tiled=True)

    context = attention(
        query_local, cache_length, key_cache, value_cache, new_token_key, new_token_value
    )
    context = lax.all_to_all(context, ADP, split_axis=1, concat_axis=0, tiled=True)
    context_other = shift(context, "core", 1)

    parts = [None] * layers
    for k in [2, 1, 3, 0] if layers == 4 else list(range(1, layers)) + [0]:
        made = output_partial(
            chips_of(z + k), core, context, context_other, output_weight, output_weight_other
        )
        parts[k] = made[0].astype(jnp.float32)
        if sides == 2:
            parts[k] = parts[k] + shift(made[1], "y", 1).astype(jnp.float32)
    return scatter_layers(parts).astype(jnp.bfloat16)


def solution(mesh):
    reps, adp = mesh.shape["rep"], mesh.shape["adp"]
    sides = 2 if adp == 16 else 1
    mesh = Mesh(mesh.devices.reshape(reps, adp // (2 * sides), sides, 2), ("rep",) + ADP)
    in_specs = (
        P("rep", ADP),
        P("rep", None),
        P(),
        P(("rep",) + ADP),
        P(None, ADP),
        P(ADP, None, None),
        P(ADP, None, None),
        P(None, ("rep",) + ADP, None, None),
        P(None, ("rep",) + ADP, None, None),
        P(("rep",) + ADP, None),
        P(("rep",) + ADP, None),
        P(ADP, None),
    )
    return jax.shard_map(
        shards, mesh=mesh, in_specs=in_specs, out_specs=P("rep", ADP), check_vma=False
    )
```

```python
import jax
import jax.numpy as jnp
from jax import lax
from jax.experimental import pallas as pl
from jax.experimental.pallas import tpu as pltpu
from jax.sharding import Mesh
from jax.sharding import PartitionSpec as P

HEADS = 64
HEAD_DIM = 128
ADP = ("z", "y", "core")
NT = (((1,), (1,)), ((), ()))
VMEM_LIMIT = 56 << 20


def low_kernel(places, *refs):
    count = places.shape[0] // 2
    blocks, a_own, a_other = (refs[i * count : (i + 1) * count] for i in range(3))
    out = refs[-1]
    out[...] = refs[-2][...] if len(refs) > 3 * count + 1 else jnp.zeros_like(out)
    first_core = places[0] % 2 == 0
    for i in range(count):

        @pl.when(places[count + i] > 0)
        def _():
            own, other = a_own[i][0], a_other[i][0]
            pair = jnp.concatenate(
                [jnp.where(first_core, own, other), jnp.where(first_core, other, own)], axis=0
            )
            out[...] += lax.dot_general(
                blocks[i][...], pair, NT, preferred_element_type=jnp.float32
            )


def add_low(places, blocks, down, down_other, sums):
    count = len(blocks)
    rows, width = blocks[0].shape
    rank = down.shape[1]
    flat = lambda shape: pl.BlockSpec(shape, lambda j, p: (0, 0))
    shape = (rows, 2 * rank)
    maps = [pl.BlockSpec((1, rank, width), lambda j, p, i=i: (0, 0, p[i])) for i in range(count)]
    return pl.pallas_call(
        low_kernel,
        grid_spec=pltpu.PrefetchScalarGridSpec(
            num_scalar_prefetch=1,
            grid=(1,),
            in_specs=[flat((rows, width))] * count + maps * 2 + [flat(shape)] * len(sums),
            out_specs=flat(shape),
        ),
        out_shape=jax.ShapeDtypeStruct(shape, jnp.float32),
        compiler_params=pltpu.CompilerParams(vmem_limit_bytes=VMEM_LIMIT),
        cost_estimate=pl.CostEstimate(
            flops=4 * count * rows * width * rank,
            bytes_accessed=2 * count * width * (rows + 2 * rank),
            transcendentals=0,
        ),
    )(places, *blocks, *[down] * count, *[down_other] * count, *sums)


def project_kernel(places, *refs):
    count = places.shape[0] // 2
    blocks, w_own, w_other = (refs[i * count : (i + 1) * count] for i in range(3))
    outs = refs[-2:]
    for j, (out, weights) in enumerate(zip(outs, (w_own, w_other))):
        out[...] = refs[3 * count + j][...] if len(refs) > 3 * count + 2 else jnp.zeros_like(out)
        for i in range(count):

            @pl.when(places[count + i] > 0)
            def _():
                out[...] += jnp.dot(
                    blocks[i][...], weights[i][...], preferred_element_type=jnp.float32
                )


def project(places, blocks, weight, weight_other, sums):
    count = len(blocks)
    rows, width = blocks[0].shape
    cols = weight.shape[1]
    tile = cols // 2 if cols % 256 == 0 else cols
    sum_spec = pl.BlockSpec((rows, tile), lambda j, p: (0, j))
    weights = [pl.BlockSpec((width, tile), lambda j, p, i=i: (p[i], j)) for i in range(count)]
    return pl.pallas_call(
        project_kernel,
        grid_spec=pltpu.PrefetchScalarGridSpec(
            num_scalar_prefetch=1,
            grid=(cols // tile,),
            in_specs=[pl.BlockSpec((rows, width), lambda j, p: (0, 0))] * count
            + weights * 2
            + [sum_spec] * len(sums),
            out_specs=[sum_spec] * 2,
        ),
        out_shape=[jax.ShapeDtypeStruct((rows, cols), jnp.float32)] * 2,
        compiler_params=pltpu.CompilerParams(vmem_limit_bytes=VMEM_LIMIT),
        cost_estimate=pl.CostEstimate(
            flops=4 * count * rows * width * cols,
            bytes_accessed=2 * count * width * (rows + 2 * cols) + 8 * rows * cols,
            transcendentals=0,
        ),
    )(places, *blocks, *[weight] * count, *[weight_other] * count, *sums)


def query_kernel(half, own, received, low, slot, up_own, up_other, out):
    step = pl.program_id(0)
    cols, lanes = own.shape[1], low.shape[1]
    rank = lanes // 2
    part = rank // 2
    depth = up_own.shape[0]
    shape = (lanes, depth)
    lane = lax.broadcasted_iota(jnp.int32, shape, 1) % part
    row = lax.broadcasted_iota(jnp.int32, shape, 0)
    owner = lax.broadcasted_iota(jnp.int32, (own.shape[0], depth), 1) // part
    live = slot[...] == owner
    total = own[...] + received[:, :cols]
    for h, up in ((half[0], up_own), (1 - half[0], up_other)):
        copies = (row == lane + rank * step + part * h).astype(jnp.bfloat16)
        spread = jnp.dot(low[...], copies, preferred_element_type=jnp.float32)
        spread = jnp.where(live, spread, 0.0).astype(jnp.bfloat16)
        total += jnp.dot(spread, up[...], preferred_element_type=jnp.float32)
    out[...] = (total * HEAD_DIM ** (-0.5)).astype(out.dtype)


def make_query(half, own, received, low, slot, up_own, up_other):
    rows, cols = own.shape
    tile = rows // 2
    depth = up_own.shape[0]
    by_rows = lambda width: pl.BlockSpec((tile, width), lambda j, h: (j, 0))
    whole = lambda array: pl.BlockSpec(array.shape, lambda j, h: (0, 0))
    return pl.pallas_call(
        query_kernel,
        grid_spec=pltpu.PrefetchScalarGridSpec(
            num_scalar_prefetch=1,
            grid=(2,),
            in_specs=[
                by_rows(cols),
                by_rows(received.shape[1]),
                whole(low),
                by_rows(1),
                whole(up_own),
                whole(up_other),
            ],
            out_specs=by_rows(cols),
        ),
        out_shape=jax.ShapeDtypeStruct((rows, cols), jnp.bfloat16),
        compiler_params=pltpu.CompilerParams(vmem_limit_bytes=VMEM_LIMIT),
        cost_estimate=pl.CostEstimate(
            flops=4 * rows * cols * depth,
            bytes_accessed=rows * cols * 10 + 4 * depth * cols,
            transcendentals=0,
        ),
    )(half, own, received, low, slot, up_own, up_other)


def output_kernel(places, own, other, *refs):
    count = places.shape[0]
    for w_own, w_other, out in zip(refs[:count], refs[count : 2 * count], refs[2 * count :]):
        total = jnp.dot(own[...], w_own[...], preferred_element_type=jnp.float32)
        total += jnp.dot(other[...], w_other[...], preferred_element_type=jnp.float32)
        out[...] = total.astype(out.dtype)


def output_partial(chips, core, own, other, weight, weight_other, width):
    rows, depth = own.shape
    count = len(chips)
    tile = width // 2 if width % 256 == 0 else width
    steps = width // tile
    places = jnp.stack([2 * chip + core for chip in chips]).astype(jnp.int32)
    whole = pl.BlockSpec((rows, depth), lambda j, p: (0, 0))
    weights = [
        pl.BlockSpec((depth, tile), lambda j, p, i=i: (0, p[i] * steps + j)) for i in range(count)
    ]
    return pl.pallas_call(
        output_kernel,
        grid_spec=pltpu.PrefetchScalarGridSpec(
            num_scalar_prefetch=1,
            grid=(steps,),
            in_specs=[whole, whole] + weights * 2,
            out_specs=[pl.BlockSpec((rows, tile), lambda j, p: (0, j))] * count,
        ),
        out_shape=[jax.ShapeDtypeStruct((rows, width), jnp.bfloat16)] * count,
        compiler_params=pltpu.CompilerParams(vmem_limit_bytes=VMEM_LIMIT),
        cost_estimate=pl.CostEstimate(
            flops=4 * count * rows * width * depth,
            bytes_accessed=2 * count * width * (rows + 2 * depth) + 4 * rows * depth,
            transcendentals=0,
        ),
    )(places, own, other, *[weight] * count, *[weight_other] * count)


def attention(query, cache_length, key_cache, value_cache, k_new, v_new):
    local_reqs = query.shape[0]
    kv_count, _, span, dim = key_cache.shape
    group = HEADS // kv_count
    query = query.reshape(local_reqs, kv_count, group, dim)
    k_new = k_new.reshape(local_reqs, kv_count, dim)
    v_new = v_new.reshape(local_reqs, kv_count, dim)
    live = (jnp.arange(span)[None, :] < cache_length[:, None])[None, :, None, :]
    scores = jnp.einsum("rkge,krje->krgj", query, key_cache, preferred_element_type=jnp.float32)
    fresh = jnp.einsum("rkge,rke->krg", query, k_new, preferred_element_type=jnp.float32)
    scores = jnp.where(live, scores, -jnp.inf)
    top = jnp.maximum(jnp.max(scores, axis=3), fresh)
    expd = jnp.where(live, jnp.exp(scores - top[:, :, :, None]), 0.0)
    expf = jnp.exp(fresh - top)
    total = jnp.sum(expd, axis=3) + expf
    probs = (expd / total[:, :, :, None]).astype(jnp.bfloat16)
    probf = (expf / total).astype(jnp.bfloat16)
    context = jnp.einsum("krgj,krje->rkge", probs, value_cache, preferred_element_type=jnp.float32)
    fresh_part = jnp.einsum("krg,rke->rkge", probf.astype(jnp.float32), v_new.astype(jnp.float32))
    return (context + fresh_part).astype(jnp.bfloat16).reshape(local_reqs, HEADS * dim)


def shift(value, axis, by):
    size = lax.axis_size(axis)
    return lax.ppermute(value, axis, [(i, (i + by) % size) for i in range(size)])


def after(value, *others):
    return lax.optimization_barrier((value, *others))[0]


def swap_sides(value, layers):
    return lax.ppermute(value, ("z", "y"), [(2 * i + j, 2 * i + 1 - j) for i in layers for j in (0, 1)])


def gather_features(tokens):
    layers, sides = lax.axis_size("z"), lax.axis_size("y")
    z = lax.axis_index("z")
    if layers != 4 or sides != 2:
        entries = []
        for k in range(layers):
            block = shift(tokens, "z", k) if k else tokens
            pair = [block, shift(block, "y", 1)] if sides == 2 else [block]
            entries.append(((z - k) % layers, True, pair))
        return [entries[:-1], entries[-1:]]
    own_side = swap_sides(tokens, range(4))
    below = lax.ppermute(tokens, "z", [(0, 1), (1, 2), (2, 3)])
    above = lax.ppermute(tokens, "z", [(1, 0), (2, 1), (3, 2)])
    below_side = swap_sides(after(below, own_side), (1, 2, 3))
    above_side = swap_sides(above, (0, 1, 2))
    two = lax.ppermute(below, "z", [(1, 2), (2, 3)]), lax.ppermute(above, "z", [(2, 1), (1, 0)])
    far = lax.ppermute(after(tokens, below, above), "z", [(0, 3), (3, 0)])
    two = jnp.where(z >= 2, *two)
    two_side = swap_sides(two, range(4))
    far_side = swap_sides(far, (0, 3))
    return [
        [
            (z, True, [tokens, own_side]),
            ((z - 1) % 4, z >= 1, [below, below_side]),
            ((z + 1) % 4, z <= 2, [above, above_side]),
        ],
        [((z + 2) % 4, True, [two, two_side]), (3 - z, (z == 0) | (z == 3), [far, far_side])],
    ]


def scatter_layers(parts):
    layers = lax.axis_size("z")
    wide = lambda value: value.astype(jnp.float32)
    narrow = lambda value: value.astype(jnp.bfloat16)
    if layers != 4:
        return sum([wide(shift(narrow(parts[k]), "z", k)) for k in range(1, layers)], parts[0])
    two = narrow(parts[2])
    up = lax.ppermute(two, "z", [(0, 1), (1, 2)])
    down = lax.ppermute(two, "z", [(3, 2), (2, 1)])
    above = shift(narrow(parts[1] + wide(up)), "z", 1)
    below = shift(narrow(parts[3] + wide(down)), "z", 3)
    return parts[0] + wide(above) + wide(below)


def shards(
    tokens,
    request_adapter,
    adapter_storage_slot,
    cache_length,
    query_weight,
    adapter_down_maps,
    adapter_up_maps,
    key_cache,
    value_cache,
    new_token_key,
    new_token_value,
    output_weight,
):
    layers, sides = lax.axis_size("z"), lax.axis_size("y")
    z, y, core = lax.axis_index("z"), lax.axis_index("y"), lax.axis_index("core")
    rows, width = tokens.shape
    total_adapters = adapter_storage_slot.shape[0]
    rank = adapter_down_maps.shape[2]
    chips_of = lambda layer: [
        (layer % layers) * sides + (y + side) % sides for side in range(sides)
    ]

    down = jnp.swapaxes(adapter_down_maps, 1, 2)
    down_other = shift(down, "core", 1)
    query_weight_other = shift(query_weight, "core", 1)
    output_weight_other = shift(output_weight, "core", 1)

    ids = request_adapter[:, 0]
    numbers = jnp.arange(total_adapters, dtype=jnp.int32)
    slot = jnp.sum(
        jnp.where(ids[:, None] == numbers[None, :], adapter_storage_slot[None, :], 0), axis=1
    )[:, None]

    groups = []
    for entries in gather_features(tokens):
        chips = [chip for layer, _, _ in entries for chip in chips_of(layer)]
        valid = [flag for _, flag, pair in entries for _ in pair]
        places = [2 * chip + core for chip in chips] + valid
        places = jnp.stack([jnp.asarray(place, jnp.int32) for place in places])
        groups.append((places, [block for _, _, pair in entries for block in pair]))

    reps = lax.axis_size("rep")
    half = lax.axis_index("rep") % 2
    up = jnp.swapaxes(adapter_up_maps, 1, 2)[0]
    up = lax.dynamic_slice_in_dim(up, half * (rank // 2), rank // 2, 0)
    up = after(up, groups[0][1][2])
    up = lax.all_to_all(up, ADP, split_axis=1, concat_axis=0, tiled=True)
    up_other = lax.ppermute(up, "rep", [(i, i ^ 1) for i in range(reps)])

    sums, low = [], []
    for index, (places, blocks) in enumerate(groups):
        if index == 0:
            places = after(places, up)
        low = [add_low(places, blocks, down, down_other, low)]
        if index:
            low_other = shift(low[0], "core", 1)
        sums = project(places, blocks, query_weight, query_weight_other, sums)
    own, sent = sums
    received = shift(sent, "core", 1)

    low = low[0] + low_other
    chip = z * sides + y
    low = jnp.where(slot == 2 * chip, low[:, :rank], 0.0) + jnp.where(
        slot == 2 * chip + 1, low[:, rank:], 0.0
    )
    low = low.astype(jnp.bfloat16)
    low = jnp.concatenate([low[: rows // 2], low[rows // 2 :]], axis=1)
    if sides == 2:
        low = low + shift(low, "y", 1)
    low = sum([shift(low, "z", k) for k in range(1, layers)], low)

    query = make_query(half.astype(jnp.int32).reshape(1), own, received, low, slot, up, up_other)
    query_local = lax.all_to_all(query, ADP, split_axis=0, concat_axis=1, tiled=True)

    context = attention(
        query_local, cache_length, key_cache, value_cache, new_token_key, new_token_value
    )
    context = lax.all_to_all(context, ADP, split_axis=1, concat_axis=0, tiled=True)
    context_other = shift(context, "core", 1)

    made = {}
    order = [2, 1, 3, 0] if layers == 4 else list(range(1, layers)) + [0]
    for group in (order[:1], order[1:]):
        outs = output_partial(
            [chip for k in group for chip in chips_of(z + k)],
            core,
            context,
            context_other,
            output_weight,
            output_weight_other,
            width,
        )
        for index, k in enumerate(group):
            made[k] = outs[index * sides : (index + 1) * sides]
    other_side = {k: shift(made[k][1], "y", 1) for k in order if sides == 2}
    parts = [None] * layers
    for k in order:
        parts[k] = after(made[k][0], made[order[-1]][0]).astype(jnp.float32)
        if sides == 2:
            parts[k] = parts[k] + other_side[k].astype(jnp.float32)
    return scatter_layers(parts).astype(jnp.bfloat16)


def solution(mesh):
    reps, adp = mesh.shape["rep"], mesh.shape["adp"]
    sides = 2 if adp == 16 else 1
    mesh = Mesh(mesh.devices.reshape(reps, adp // (2 * sides), sides, 2), ("rep",) + ADP)
    in_specs = (
        P("rep", ADP),
        P("rep", None),
        P(),
        P(("rep",) + ADP),
        P(None, ADP),
        P(ADP, None, None),
        P(ADP, None, None),
        P(None, ("rep",) + ADP, None, None),
        P(None, ("rep",) + ADP, None, None),
        P(("rep",) + ADP, None),
        P(("rep",) + ADP, None),
        P(ADP, None),
    )
    return jax.shard_map(
        shards, mesh=mesh, in_specs=in_specs, out_specs=P("rep", ADP), check_vma=False
    )
```

```python
import jax
import jax.numpy as jnp
from jax import lax
from jax.experimental import pallas as pl
from jax.experimental.pallas import tpu as pltpu
from jax.sharding import Mesh
from jax.sharding import PartitionSpec as P

HEADS = 64
HEAD_DIM = 128
ADP = ("z", "y", "core")
NT = (((1,), (1,)), ((), ()))
VMEM_LIMIT = 56 << 20


def project_kernel(places, *refs):
    count = places.shape[0]
    blocks, w_own, w_other, a_own, a_other = (refs[i * count : (i + 1) * count] for i in range(5))
    ins, outs = refs[5 * count : -3], refs[-3:]
    first_core = places[0] % 2 == 0
    sums = [ref[...] for ref in ins]
    for i in range(count):
        x = blocks[i][...]
        own, other = a_own[i][0], a_other[i][0]
        pair = jnp.concatenate(
            [jnp.where(first_core, own, other), jnp.where(first_core, other, own)], axis=0
        )
        parts = (
            jnp.dot(x, w_own[i][...], preferred_element_type=jnp.float32),
            jnp.dot(x, w_other[i][...], preferred_element_type=jnp.float32),
            lax.dot_general(x, pair, NT, preferred_element_type=jnp.float32),
        )
        sums = [total + part for total, part in zip(sums, parts)] if sums else parts
    for out, total in zip(outs, sums):
        out[...] = total


def project(places, blocks, weight, weight_other, down, down_other, sums):
    count = len(blocks)
    rows, width = blocks[0].shape
    cols, rank = weight.shape[1], down.shape[1]
    flat = lambda shape: pl.BlockSpec(shape, lambda j, p: (0, 0))
    shapes = [(rows, cols), (rows, cols), (rows, 2 * rank)]
    weights = [pl.BlockSpec((width, cols), lambda j, p, i=i: (p[i], 0)) for i in range(count)]
    maps = [pl.BlockSpec((1, rank, width), lambda j, p, i=i: (0, 0, p[i])) for i in range(count)]
    return pl.pallas_call(
        project_kernel,
        grid_spec=pltpu.PrefetchScalarGridSpec(
            num_scalar_prefetch=1,
            grid=(1,),
            in_specs=[flat((rows, width))] * count
            + weights * 2
            + maps * 2
            + [flat(shape) for shape in shapes[: len(sums)]],
            out_specs=[flat(shape) for shape in shapes],
        ),
        out_shape=[jax.ShapeDtypeStruct(shape, jnp.float32) for shape in shapes],
        compiler_params=pltpu.CompilerParams(vmem_limit_bytes=VMEM_LIMIT),
        cost_estimate=pl.CostEstimate(
            flops=4 * count * rows * width * (cols + rank),
            bytes_accessed=2 * count * width * (rows + 2 * cols) + 8 * rows * cols,
            transcendentals=0,
        ),
    )(
        places,
        *blocks,
        *[weight] * count,
        *[weight_other] * count,
        *[down] * count,
        *[down_other] * count,
        *sums,
    )


def query_kernel(half, own, received, low, slot, up_own, up_other, out):
    step = pl.program_id(0)
    cols, lanes = own.shape[1], low.shape[1]
    rank = lanes // 2
    part = rank // 2
    depth = up_own.shape[0]
    shape = (lanes, depth)
    lane = lax.broadcasted_iota(jnp.int32, shape, 1) % part
    row = lax.broadcasted_iota(jnp.int32, shape, 0)
    owner = lax.broadcasted_iota(jnp.int32, (own.shape[0], depth), 1) // part
    live = slot[...] == owner
    total = own[...] + received[:, :cols]
    for h, up in ((half[0], up_own), (1 - half[0], up_other)):
        copies = (row == lane + rank * step + part * h).astype(jnp.bfloat16)
        spread = jnp.dot(low[...], copies, preferred_element_type=jnp.float32)
        spread = jnp.where(live, spread, 0.0).astype(jnp.bfloat16)
        total += jnp.dot(spread, up[...], preferred_element_type=jnp.float32)
    out[...] = (total * HEAD_DIM ** (-0.5)).astype(out.dtype)


def make_query(half, own, received, low, slot, up_own, up_other):
    rows, cols = own.shape
    tile = rows // 2
    depth = up_own.shape[0]
    by_rows = lambda width: pl.BlockSpec((tile, width), lambda j, h: (j, 0))
    whole = lambda array: pl.BlockSpec(array.shape, lambda j, h: (0, 0))
    return pl.pallas_call(
        query_kernel,
        grid_spec=pltpu.PrefetchScalarGridSpec(
            num_scalar_prefetch=1,
            grid=(2,),
            in_specs=[
                by_rows(cols),
                by_rows(received.shape[1]),
                whole(low),
                by_rows(1),
                whole(up_own),
                whole(up_other),
            ],
            out_specs=by_rows(cols),
        ),
        out_shape=jax.ShapeDtypeStruct((rows, cols), jnp.bfloat16),
        compiler_params=pltpu.CompilerParams(vmem_limit_bytes=VMEM_LIMIT),
        cost_estimate=pl.CostEstimate(
            flops=4 * rows * cols * depth,
            bytes_accessed=rows * cols * 10 + 4 * depth * cols,
            transcendentals=0,
        ),
    )(half, own, received, low, slot, up_own, up_other)


def output_kernel(places, own, other, *refs):
    count = places.shape[0]
    for w_own, w_other, out in zip(refs[:count], refs[count : 2 * count], refs[2 * count :]):
        total = jnp.dot(own[...], w_own[...], preferred_element_type=jnp.float32)
        total += jnp.dot(other[...], w_other[...], preferred_element_type=jnp.float32)
        out[...] = total.astype(out.dtype)


def output_partial(chips, core, own, other, weight, weight_other, width):
    rows, depth = own.shape
    count = len(chips)
    tile = width // 2 if width % 256 == 0 else width
    steps = width // tile
    places = jnp.stack([2 * chip + core for chip in chips]).astype(jnp.int32)
    whole = pl.BlockSpec((rows, depth), lambda j, p: (0, 0))
    weights = [
        pl.BlockSpec((depth, tile), lambda j, p, i=i: (0, p[i] * steps + j)) for i in range(count)
    ]
    return pl.pallas_call(
        output_kernel,
        grid_spec=pltpu.PrefetchScalarGridSpec(
            num_scalar_prefetch=1,
            grid=(steps,),
            in_specs=[whole, whole] + weights * 2,
            out_specs=[pl.BlockSpec((rows, tile), lambda j, p: (0, j))] * count,
        ),
        out_shape=[jax.ShapeDtypeStruct((rows, width), jnp.bfloat16)] * count,
        compiler_params=pltpu.CompilerParams(vmem_limit_bytes=VMEM_LIMIT),
        cost_estimate=pl.CostEstimate(
            flops=4 * count * rows * width * depth,
            bytes_accessed=2 * count * width * (rows + 2 * depth) + 4 * rows * depth,
            transcendentals=0,
        ),
    )(places, own, other, *[weight] * count, *[weight_other] * count)


def attention(query, cache_length, key_cache, value_cache, k_new, v_new):
    local_reqs = query.shape[0]
    kv_count, _, span, dim = key_cache.shape
    group = HEADS // kv_count
    query = query.reshape(local_reqs, kv_count, group, dim)
    k_new = k_new.reshape(local_reqs, kv_count, dim)
    v_new = v_new.reshape(local_reqs, kv_count, dim)
    live = (jnp.arange(span)[None, :] < cache_length[:, None])[None, :, None, :]
    scores = jnp.einsum("rkge,krje->krgj", query, key_cache, preferred_element_type=jnp.float32)
    fresh = jnp.einsum("rkge,rke->krg", query, k_new, preferred_element_type=jnp.float32)
    scores = jnp.where(live, scores, -jnp.inf)
    top = jnp.maximum(jnp.max(scores, axis=3), fresh)
    expd = jnp.where(live, jnp.exp(scores - top[:, :, :, None]), 0.0)
    expf = jnp.exp(fresh - top)
    total = jnp.sum(expd, axis=3) + expf
    probs = (expd / total[:, :, :, None]).astype(jnp.bfloat16)
    probf = (expf / total).astype(jnp.bfloat16)
    context = jnp.einsum("krgj,krje->rkge", probs, value_cache, preferred_element_type=jnp.float32)
    fresh_part = jnp.einsum("krg,rke->rkge", probf.astype(jnp.float32), v_new.astype(jnp.float32))
    return (context + fresh_part).astype(jnp.bfloat16).reshape(local_reqs, HEADS * dim)


def shift(value, axis, by):
    size = lax.axis_size(axis)
    return lax.ppermute(value, axis, [(i, (i + by) % size) for i in range(size)])


def after(value, *others):
    return lax.optimization_barrier((value, *others))[0]


def gather_features(tokens):
    layers, sides = lax.axis_size("z"), lax.axis_size("y")
    z = lax.axis_index("z")
    if layers != 4 or sides != 2:
        entries = []
        for k in range(layers):
            block = shift(tokens, "z", k) if k else tokens
            entries.append(((z - k) % layers, [block, shift(block, "y", 1)][:sides]))
        return entries
    side = shift(tokens, "y", 1)
    below, above = shift(tokens, "z", 1), shift(tokens, "z", 3)
    from_below = lax.ppermute(below, "z", [(1, 2), (2, 3)])
    from_above = lax.ppermute(above, "z", [(2, 1), (1, 0)])
    below_side = shift(after(below, side), "y", 1)
    above_side = shift(after(above, side), "y", 1)
    two = jnp.where(z >= 2, from_below, from_above)
    two = after(two, below_side, above_side)
    two_side = shift(two, "y", 1)
    return [
        (z, [tokens, side]),
        ((z - 1) % 4, [below, below_side]),
        ((z + 1) % 4, [above, above_side]),
        ((z + 2) % 4, [two, two_side]),
    ]


def scatter_layers(parts):
    layers = lax.axis_size("z")
    wide = lambda value: value.astype(jnp.float32)
    narrow = lambda value: value.astype(jnp.bfloat16)
    if layers != 4:
        return sum([wide(shift(narrow(parts[k]), "z", k)) for k in range(1, layers)], parts[0])
    two = narrow(parts[2])
    up = lax.ppermute(two, "z", [(0, 1), (1, 2)])
    down = lax.ppermute(two, "z", [(3, 2), (2, 1)])
    above = shift(narrow(parts[1] + wide(up)), "z", 1)
    below = shift(narrow(parts[3] + wide(down)), "z", 3)
    return parts[0] + wide(above) + wide(below)


def shards(
    tokens,
    request_adapter,
    adapter_storage_slot,
    cache_length,
    query_weight,
    adapter_down_maps,
    adapter_up_maps,
    key_cache,
    value_cache,
    new_token_key,
    new_token_value,
    output_weight,
):
    layers, sides = lax.axis_size("z"), lax.axis_size("y")
    z, y, core = lax.axis_index("z"), lax.axis_index("y"), lax.axis_index("core")
    rows, width = tokens.shape
    total_adapters = adapter_storage_slot.shape[0]
    rank = adapter_down_maps.shape[2]
    chips_of = lambda layer: [
        (layer % layers) * sides + (y + side) % sides for side in range(sides)
    ]

    down = jnp.swapaxes(adapter_down_maps, 1, 2)
    down_other = shift(down, "core", 1)
    query_weight_other = shift(query_weight, "core", 1)
    output_weight_other = shift(output_weight, "core", 1)

    ids = request_adapter[:, 0]
    numbers = jnp.arange(total_adapters, dtype=jnp.int32)
    slot = jnp.sum(
        jnp.where(ids[:, None] == numbers[None, :], adapter_storage_slot[None, :], 0), axis=1
    )[:, None]

    entries = gather_features(tokens)

    reps = lax.axis_size("rep")
    half = lax.axis_index("rep") % 2
    up = jnp.swapaxes(adapter_up_maps, 1, 2)[0]
    up = lax.dynamic_slice_in_dim(up, half * (rank // 2), rank // 2, 0)
    up = after(up, entries[-1][1][0])
    up = lax.all_to_all(up, ADP, split_axis=1, concat_axis=0, tiled=True)
    up_other = lax.ppermute(up, "rep", [(i, i ^ 1) for i in range(reps)])

    sums = []
    for group in (entries[:-1], entries[-1:]):
        chips = [chip for layer, _ in group for chip in chips_of(layer)]
        places = jnp.stack([2 * chip + core for chip in chips]).astype(jnp.int32)
        blocks = [block for _, pair in group for block in pair]
        if sums:
            places = after(places, up)
        sums = project(
            places, blocks, query_weight, query_weight_other, down, down_other, sums
        )
    own, sent, low = sums
    low_other = shift(low, "core", 1)
    received = shift(sent, "core", 1)

    low = low + low_other
    chip = z * sides + y
    low = jnp.where(slot == 2 * chip, low[:, :rank], 0.0) + jnp.where(
        slot == 2 * chip + 1, low[:, rank:], 0.0
    )
    low = low.astype(jnp.bfloat16)
    low = jnp.concatenate([low[: rows // 2], low[rows // 2 :]], axis=1)
    if sides == 2:
        low = low + shift(low, "y", 1)
    low = sum([shift(low, "z", k) for k in range(1, layers)], low)

    query = make_query(half.astype(jnp.int32).reshape(1), own, received, low, slot, up, up_other)
    query_local = lax.all_to_all(query, ADP, split_axis=0, concat_axis=1, tiled=True)

    context = attention(
        query_local, cache_length, key_cache, value_cache, new_token_key, new_token_value
    )
    context = lax.all_to_all(context, ADP, split_axis=1, concat_axis=0, tiled=True)
    context_other = shift(context, "core", 1)

    order = [2, 1, 3, 0] if layers == 4 else list(range(1, layers)) + [0]
    keys = [(k, side) for k in order for side in reversed(range(sides))]
    made = {}
    for group in (keys[:1], keys[1:]):
        outs = output_partial(
            [chips_of(z + k)[side] for k, side in group],
            core,
            context,
            context_other,
            output_weight,
            output_weight_other,
            width,
        )
        made.update(zip(group, outs))
    other_side = {k: shift(made[k, 1], "y", 1) for k in order if sides == 2}
    parts = [None] * layers
    for k in order:
        parts[k] = after(made[k, 0], made[keys[-1]]).astype(jnp.float32)
        if sides == 2:
            parts[k] = parts[k] + other_side[k].astype(jnp.float32)
    return scatter_layers(parts).astype(jnp.bfloat16)


def solution(mesh):
    reps, adp = mesh.shape["rep"], mesh.shape["adp"]
    sides = 2 if adp == 16 else 1
    mesh = Mesh(mesh.devices.reshape(reps, adp // (2 * sides), sides, 2), ("rep",) + ADP)
    in_specs = (
        P("rep", ADP),
        P("rep", None),
        P(),
        P(("rep",) + ADP),
        P(None, ADP),
        P(ADP, None, None),
        P(ADP, None, None),
        P(None, ("rep",) + ADP, None, None),
        P(None, ("rep",) + ADP, None, None),
        P(("rep",) + ADP, None),
        P(("rep",) + ADP, None),
        P(ADP, None),
    )
    return jax.shard_map(
        shards, mesh=mesh, in_specs=in_specs, out_specs=P("rep", ADP), check_vma=False
    )
```

```python
import jax
import jax.numpy as jnp
from jax import lax
from jax.experimental import pallas as pl
from jax.experimental.pallas import tpu as pltpu
from jax.sharding import Mesh
from jax.sharding import PartitionSpec as P

HEADS = 64
HEAD_DIM = 128
ADP = ("z", "y", "core")
NT = (((1,), (1,)), ((), ()))
VMEM_LIMIT = 56 << 20


def project_kernel(places, *refs):
    count = places.shape[0]
    blocks, w_own, w_other, a_own, a_other = (refs[i * count : (i + 1) * count] for i in range(5))
    ins, outs = refs[5 * count : -3], refs[-3:]
    first_core = places[0] % 2 == 0
    sums = [ref[...] for ref in ins]
    for i in range(count):
        x = blocks[i][...]
        own, other = a_own[i][0], a_other[i][0]
        pair = jnp.concatenate(
            [jnp.where(first_core, own, other), jnp.where(first_core, other, own)], axis=0
        )
        parts = (
            jnp.dot(x, w_own[i][...], preferred_element_type=jnp.float32),
            jnp.dot(x, w_other[i][...], preferred_element_type=jnp.float32),
            lax.dot_general(x, pair, NT, preferred_element_type=jnp.float32),
        )
        sums = [total + part for total, part in zip(sums, parts)] if sums else parts
    for out, total in zip(outs, sums):
        out[...] = total


def project(places, blocks, weight, weight_other, down, down_other, sums):
    count = len(blocks)
    rows, width = blocks[0].shape
    cols, rank = weight.shape[1], down.shape[1]
    flat = lambda shape: pl.BlockSpec(shape, lambda j, p: (0, 0))
    shapes = [(rows, cols), (rows, cols), (rows, 2 * rank)]
    weights = [pl.BlockSpec((width, cols), lambda j, p, i=i: (p[i], 0)) for i in range(count)]
    maps = [pl.BlockSpec((1, rank, width), lambda j, p, i=i: (0, 0, p[i])) for i in range(count)]
    return pl.pallas_call(
        project_kernel,
        grid_spec=pltpu.PrefetchScalarGridSpec(
            num_scalar_prefetch=1,
            grid=(1,),
            in_specs=[flat((rows, width))] * count
            + weights * 2
            + maps * 2
            + [flat(shape) for shape in shapes[: len(sums)]],
            out_specs=[flat(shape) for shape in shapes],
        ),
        out_shape=[jax.ShapeDtypeStruct(shape, jnp.float32) for shape in shapes],
        compiler_params=pltpu.CompilerParams(vmem_limit_bytes=VMEM_LIMIT),
        cost_estimate=pl.CostEstimate(
            flops=4 * count * rows * width * (cols + rank),
            bytes_accessed=2 * count * width * (rows + 2 * cols) + 8 * rows * cols,
            transcendentals=0,
        ),
    )(
        places,
        *blocks,
        *[weight] * count,
        *[weight_other] * count,
        *[down] * count,
        *[down_other] * count,
        *sums,
    )


def query_kernel(half, own, received, low, slot, up_own, up_other, out):
    step = pl.program_id(0)
    cols, lanes = own.shape[1], low.shape[1]
    rank = lanes // 2
    part = rank // 2
    depth = up_own.shape[0]
    shape = (lanes, depth)
    lane = lax.broadcasted_iota(jnp.int32, shape, 1) % part
    row = lax.broadcasted_iota(jnp.int32, shape, 0)
    owner = lax.broadcasted_iota(jnp.int32, (own.shape[0], depth), 1) // part
    live = slot[...] == owner
    total = own[...] + received[:, :cols]
    for h, up in ((half[0], up_own), (1 - half[0], up_other)):
        copies = (row == lane + rank * step + part * h).astype(jnp.bfloat16)
        spread = jnp.dot(low[...], copies, preferred_element_type=jnp.float32)
        spread = jnp.where(live, spread, 0.0).astype(jnp.bfloat16)
        total += jnp.dot(spread, up[...], preferred_element_type=jnp.float32)
    out[...] = (total * HEAD_DIM ** (-0.5)).astype(out.dtype)


def make_query(half, own, received, low, slot, up_own, up_other):
    rows, cols = own.shape
    tile = rows // 2
    depth = up_own.shape[0]
    by_rows = lambda width: pl.BlockSpec((tile, width), lambda j, h: (j, 0))
    whole = lambda array: pl.BlockSpec(array.shape, lambda j, h: (0, 0))
    return pl.pallas_call(
        query_kernel,
        grid_spec=pltpu.PrefetchScalarGridSpec(
            num_scalar_prefetch=1,
            grid=(2,),
            in_specs=[
                by_rows(cols),
                by_rows(received.shape[1]),
                whole(low),
                by_rows(1),
                whole(up_own),
                whole(up_other),
            ],
            out_specs=by_rows(cols),
        ),
        out_shape=jax.ShapeDtypeStruct((rows, cols), jnp.bfloat16),
        compiler_params=pltpu.CompilerParams(vmem_limit_bytes=VMEM_LIMIT),
        cost_estimate=pl.CostEstimate(
            flops=4 * rows * cols * depth,
            bytes_accessed=rows * cols * 10 + 4 * depth * cols,
            transcendentals=0,
        ),
    )(half, own, received, low, slot, up_own, up_other)


def output_kernel(places, own, other, *refs):
    count = places.shape[0]
    for w_own, w_other, out in zip(refs[:count], refs[count : 2 * count], refs[2 * count :]):
        total = jnp.dot(own[...], w_own[...], preferred_element_type=jnp.float32)
        total += jnp.dot(other[...], w_other[...], preferred_element_type=jnp.float32)
        out[...] = total.astype(out.dtype)


def output_partial(chips, core, own, other, weight, weight_other, width):
    rows, depth = own.shape
    count = len(chips)
    tile = width // 2 if width % 256 == 0 else width
    steps = width // tile
    places = jnp.stack([2 * chip + core for chip in chips]).astype(jnp.int32)
    whole = pl.BlockSpec((rows, depth), lambda j, p: (0, 0))
    weights = [
        pl.BlockSpec((depth, tile), lambda j, p, i=i: (0, p[i] * steps + j)) for i in range(count)
    ]
    return pl.pallas_call(
        output_kernel,
        grid_spec=pltpu.PrefetchScalarGridSpec(
            num_scalar_prefetch=1,
            grid=(steps,),
            in_specs=[whole, whole] + weights * 2,
            out_specs=[pl.BlockSpec((rows, tile), lambda j, p: (0, j))] * count,
        ),
        out_shape=[jax.ShapeDtypeStruct((rows, width), jnp.bfloat16)] * count,
        compiler_params=pltpu.CompilerParams(vmem_limit_bytes=VMEM_LIMIT),
        cost_estimate=pl.CostEstimate(
            flops=4 * count * rows * width * depth,
            bytes_accessed=2 * count * width * (rows + 2 * depth) + 4 * rows * depth,
            transcendentals=0,
        ),
    )(places, own, other, *[weight] * count, *[weight_other] * count)


def attention(query, cache_length, key_cache, value_cache, k_new, v_new):
    local_reqs = query.shape[0]
    kv_count, _, span, dim = key_cache.shape
    group = HEADS // kv_count
    query = query.reshape(local_reqs, kv_count, group, dim)
    k_new = k_new.reshape(local_reqs, kv_count, dim)
    v_new = v_new.reshape(local_reqs, kv_count, dim)
    live = (jnp.arange(span)[None, :] < cache_length[:, None])[None, :, None, :]
    scores = jnp.einsum("rkge,krje->krgj", query, key_cache, preferred_element_type=jnp.float32)
    fresh = jnp.einsum("rkge,rke->krg", query, k_new, preferred_element_type=jnp.float32)
    scores = jnp.where(live, scores, -jnp.inf)
    top = jnp.maximum(jnp.max(scores, axis=3), fresh)
    expd = jnp.where(live, jnp.exp(scores - top[:, :, :, None]), 0.0)
    expf = jnp.exp(fresh - top)
    total = jnp.sum(expd, axis=3) + expf
    probs = (expd / total[:, :, :, None]).astype(jnp.bfloat16)
    probf = (expf / total).astype(jnp.bfloat16)
    context = jnp.einsum("krgj,krje->rkge", probs, value_cache, preferred_element_type=jnp.float32)
    fresh_part = jnp.einsum("krg,rke->rkge", probf.astype(jnp.float32), v_new.astype(jnp.float32))
    return (context + fresh_part).astype(jnp.bfloat16).reshape(local_reqs, HEADS * dim)


def shift(value, axis, by):
    size = lax.axis_size(axis)
    return lax.ppermute(value, axis, [(i, (i + by) % size) for i in range(size)])


def after(value, *others):
    return lax.optimization_barrier((value, *others))[0]


def gather_features(tokens):
    layers, sides = lax.axis_size("z"), lax.axis_size("y")
    z = lax.axis_index("z")
    if layers != 4 or sides != 2:
        entries = []
        for k in range(layers):
            block = shift(tokens, "z", k) if k else tokens
            entries.append(((z - k) % layers, [block, shift(block, "y", 1)][:sides]))
        return entries
    side = shift(tokens, "y", 1)
    below, above = shift(tokens, "z", 1), shift(tokens, "z", 3)
    from_below = lax.ppermute(below, "z", [(1, 2), (2, 3)])
    from_above = lax.ppermute(above, "z", [(2, 1), (1, 0)])
    below_side = shift(after(below, side), "y", 1)
    above_side = shift(after(above, side), "y", 1)
    two = jnp.where(z >= 2, from_below, from_above)
    two = after(two, below_side, above_side)
    two_side = shift(two, "y", 1)
    return [
        (z, [tokens, side]),
        ((z - 1) % 4, [below, below_side]),
        ((z + 1) % 4, [above, above_side]),
        ((z + 2) % 4, [two, two_side]),
    ]


def scatter_layers(parts):
    layers = lax.axis_size("z")
    wide = lambda value: value.astype(jnp.float32)
    narrow = lambda value: value.astype(jnp.bfloat16)
    if layers != 4:
        return sum([wide(shift(narrow(parts[k]), "z", k)) for k in range(1, layers)], parts[0])
    two = narrow(parts[2])
    up = lax.ppermute(two, "z", [(0, 1), (1, 2)])
    down = lax.ppermute(two, "z", [(3, 2), (2, 1)])
    above = shift(narrow(parts[1] + wide(up)), "z", 1)
    below = shift(narrow(parts[3] + wide(down)), "z", 3)
    return parts[0] + wide(above) + wide(below)


def shards(
    tokens,
    request_adapter,
    adapter_storage_slot,
    cache_length,
    query_weight,
    adapter_down_maps,
    adapter_up_maps,
    key_cache,
    value_cache,
    new_token_key,
    new_token_value,
    output_weight,
):
    layers, sides = lax.axis_size("z"), lax.axis_size("y")
    z, y, core = lax.axis_index("z"), lax.axis_index("y"), lax.axis_index("core")
    rows, width = tokens.shape
    total_adapters = adapter_storage_slot.shape[0]
    rank = adapter_down_maps.shape[2]
    depth = output_weight.shape[0]
    chips_of = lambda layer: [
        (layer % layers) * sides + (y + side) % sides for side in range(sides)
    ]

    down = jnp.swapaxes(adapter_down_maps, 1, 2)
    down_other = shift(down, "core", 1)
    query_weight_other = shift(query_weight, "core", 1)
    output_weight_other = shift(output_weight, "core", 1)

    ids = request_adapter[:, 0]
    numbers = jnp.arange(total_adapters, dtype=jnp.int32)
    slot = jnp.sum(
        jnp.where(ids[:, None] == numbers[None, :], adapter_storage_slot[None, :], 0), axis=1
    )[:, None]

    entries = gather_features(tokens)

    sums = []
    for group in (entries[:-1], entries[-1:]):
        chips = [chip for layer, _ in group for chip in chips_of(layer)]
        places = jnp.stack([2 * chip + core for chip in chips]).astype(jnp.int32)
        blocks = [block for _, pair in group for block in pair]
        sums = project(
            places, blocks, query_weight, query_weight_other, down, down_other, sums
        )
        first_sums = sums if len(group) > 1 else first_sums

    reps = lax.axis_size("rep")
    half = lax.axis_index("rep") % 2
    up = jnp.swapaxes(adapter_up_maps, 1, 2)[0]
    up = lax.dynamic_slice_in_dim(up, half * (rank // 2), rank // 2, 0)
    up = after(up, first_sums[2])
    up = lax.all_to_all(up, ADP, split_axis=1, concat_axis=0, tiled=True)
    up_other = lax.ppermute(up, "rep", [(i, i ^ 1) for i in range(reps)])

    own, sent, low = sums
    low_other = shift(low, "core", 1)
    received = shift(sent, "core", 1)

    low = low + low_other
    chip = z * sides + y
    low = jnp.where(slot == 2 * chip, low[:, :rank], 0.0) + jnp.where(
        slot == 2 * chip + 1, low[:, rank:], 0.0
    )
    low = low.astype(jnp.bfloat16)
    low = jnp.concatenate([low[: rows // 2], low[rows // 2 :]], axis=1)
    if sides == 2:
        low = low + shift(low, "y", 1)
    low = sum([shift(low, "z", k) for k in range(1, layers)], low)

    query = make_query(half.astype(jnp.int32).reshape(1), own, received, low, slot, up, up_other)
    query_local = lax.all_to_all(query, ADP, split_axis=0, concat_axis=1, tiled=True)

    context = attention(
        query_local, cache_length, key_cache, value_cache, new_token_key, new_token_value
    )
    context = jnp.swapaxes(context.reshape(context.shape[0], -1, depth), 0, 1)
    context = lax.all_to_all(context, ADP, split_axis=0, concat_axis=0, tiled=True)
    context = context.reshape(rows, depth)
    context_other = shift(context, "core", 1)

    order = [2, 1, 3, 0] if layers == 4 else list(range(1, layers)) + [0]
    keys = [(k, side) for k in order for side in reversed(range(sides))]
    made = {}
    for group in (keys[:1], keys[1:]):
        outs = output_partial(
            [chips_of(z + k)[side] for k, side in group],
            core,
            context,
            context_other,
            output_weight,
            output_weight_other,
            width,
        )
        made.update(zip(group, outs))
    other_side = {k: shift(made[k, 1], "y", 1) for k in order if sides == 2}
    parts = [None] * layers
    for k in order:
        parts[k] = after(made[k, 0], made[keys[-1]]).astype(jnp.float32)
        if sides == 2:
            parts[k] = parts[k] + other_side[k].astype(jnp.float32)
    return scatter_layers(parts).astype(jnp.bfloat16)


def solution(mesh):
    reps, adp = mesh.shape["rep"], mesh.shape["adp"]
    sides = 2 if adp == 16 else 1
    mesh = Mesh(mesh.devices.reshape(reps, adp // (2 * sides), sides, 2), ("rep",) + ADP)
    in_specs = (
        P("rep", ADP),
        P("rep", None),
        P(),
        P(("rep",) + ADP),
        P(None, ADP),
        P(ADP, None, None),
        P(ADP, None, None),
        P(None, ("rep",) + ADP, None, None),
        P(None, ("rep",) + ADP, None, None),
        P(("rep",) + ADP, None),
        P(("rep",) + ADP, None),
        P(ADP, None),
    )
    return jax.shard_map(
        shards, mesh=mesh, in_specs=in_specs, out_specs=P("rep", ADP), check_vma=False
    )
```

```python
import jax
import jax.numpy as jnp
from jax import lax
from jax.experimental import pallas as pl
from jax.experimental.pallas import tpu as pltpu
from jax.sharding import Mesh
from jax.sharding import PartitionSpec as P

HEADS = 64
HEAD_DIM = 128
ADP = ("z", "y", "core")
NT = (((1,), (1,)), ((), ()))
VMEM_LIMIT = 60 << 20
QUICK = pl.CostEstimate(flops=1, bytes_accessed=1, transcendentals=0)


def adapter_pair(first_core, own, other):
    own, other = own[0], other[0]
    return jnp.concatenate(
        [jnp.where(first_core, own, other), jnp.where(first_core, other, own)], axis=0
    )


def low_kernel(places, first, count, *refs):
    blocks, a_own, a_other = (refs[i * count : (i + 1) * count] for i in range(3))
    rest, out = refs[3 * count : -1], refs[-1]
    first_core = places[0] % 2 == 0
    total = None
    for i in range(count):
        pair = adapter_pair(first_core, a_own[i], a_other[i])
        part = lax.dot_general(blocks[i][...], pair, NT, preferred_element_type=jnp.float32)
        total = part if total is None else total + part
    if not rest:
        out[...] = total
        return
    low_in, slot = rest
    total += low_in[...]
    rank = total.shape[1] // 2
    mine = places[0] - places[0] % 2
    low = jnp.where(slot[...] == mine, total[:, :rank], 0.0)
    low += jnp.where(slot[...] == mine + 1, total[:, rank:], 0.0)
    half = low.shape[0] // 2
    out[...] = jnp.concatenate([low[:half], low[half:]], axis=1)


def add_low(places, first, blocks, down, down_other, rest):
    count = len(blocks)
    rows, width = blocks[0].shape
    rank = down.shape[1]
    flat = lambda shape: pl.BlockSpec(shape, lambda j, p: (0, 0))
    maps = [
        pl.BlockSpec((1, rank, width), lambda j, p, i=i: (0, 0, p[first + i])) for i in range(count)
    ]
    shape = (rows // 2, 2 * rank) if rest else (rows, 2 * rank)

    def kernel(places, *refs):
        low_kernel(places, first, count, *refs)

    return pl.pallas_call(
        kernel,
        grid_spec=pltpu.PrefetchScalarGridSpec(
            num_scalar_prefetch=1,
            grid=(1,),
            in_specs=[flat((rows, width))] * count + maps * 2 + [flat(r.shape) for r in rest],
            out_specs=flat(shape),
        ),
        out_shape=jax.ShapeDtypeStruct(shape, jnp.float32),
        compiler_params=pltpu.CompilerParams(vmem_limit_bytes=VMEM_LIMIT),
        cost_estimate=QUICK,
    )(places, *blocks, *[down] * count, *[down_other] * count, *rest)


def base_kernel(places, count, *refs):
    blocks, w_own, w_other = (refs[i * count : (i + 1) * count] for i in range(3))
    ins, outs = refs[3 * count : -2], refs[-2:]
    for j, (out, weights) in enumerate(zip(outs, (w_own, w_other))):
        total = ins[j][...] if ins else None
        for block, weight in zip(blocks, weights):
            part = jnp.dot(block[...], weight[...], preferred_element_type=jnp.float32)
            total = part if total is None else total + part
        out[...] = total


def add_base(places, first, blocks, weight, weight_other, sums):
    count = len(blocks)
    rows, width = blocks[0].shape
    cols = weight.shape[1]
    tile = cols // 2 if cols % 256 == 0 else cols
    sum_spec = pl.BlockSpec((rows, tile), lambda j, p: (0, j))
    weights = [
        pl.BlockSpec((width, tile), lambda j, p, i=i: (p[first + i], j)) for i in range(count)
    ]

    def kernel(places, *refs):
        base_kernel(places, count, *refs)

    return pl.pallas_call(
        kernel,
        grid_spec=pltpu.PrefetchScalarGridSpec(
            num_scalar_prefetch=1,
            grid=(cols // tile,),
            in_specs=[pl.BlockSpec((rows, width), lambda j, p: (0, 0))] * count
            + weights * 2
            + [sum_spec] * len(sums),
            out_specs=[sum_spec] * 2,
        ),
        out_shape=[jax.ShapeDtypeStruct((rows, cols), jnp.float32)] * 2,
        compiler_params=pltpu.CompilerParams(vmem_limit_bytes=VMEM_LIMIT),
        cost_estimate=QUICK,
    )(places, *blocks, *[weight] * count, *[weight_other] * count, *sums)


def query_kernel(half, own, received, low, slot, owners, up_own, up_other, out):
    step = pl.program_id(0)
    lanes = low.shape[1]
    rank = lanes // 2
    part = rank // 2
    depth = up_own.shape[0]
    shape = (lanes, depth)
    lane = lax.broadcasted_iota(jnp.int32, shape, 1) % part
    row = lax.broadcasted_iota(jnp.int32, shape, 0)
    live = slot[...] == owners[...]
    total = own[...] + received[...]
    for h, up in ((half[0], up_own), (1 - half[0], up_other)):
        copies = (row == lane + rank * step + part * h).astype(jnp.bfloat16)
        spread = jnp.dot(low[...], copies, preferred_element_type=jnp.float32)
        spread = jnp.where(live, spread, 0.0).astype(jnp.bfloat16)
        total += jnp.dot(spread, up[...], preferred_element_type=jnp.float32)
    out[...] = (total * HEAD_DIM ** (-0.5)).astype(out.dtype)


def make_query(half, own, received, low, slot, owners, up_own, up_other):
    rows, cols = own.shape
    tile = rows // 2
    depth = up_own.shape[0]
    by_rows = lambda width: pl.BlockSpec((tile, width), lambda j, h: (j, 0))
    whole = lambda array: pl.BlockSpec(array.shape, lambda j, h: (0, 0))
    return pl.pallas_call(
        query_kernel,
        grid_spec=pltpu.PrefetchScalarGridSpec(
            num_scalar_prefetch=1,
            grid=(2,),
            in_specs=[
                by_rows(cols),
                by_rows(received.shape[1]),
                whole(low),
                by_rows(1),
                whole(owners),
                whole(up_own),
                whole(up_other),
            ],
            out_specs=by_rows(cols),
        ),
        out_shape=jax.ShapeDtypeStruct((rows, cols), jnp.bfloat16),
        compiler_params=pltpu.CompilerParams(vmem_limit_bytes=VMEM_LIMIT),
        cost_estimate=QUICK,
    )(half, own, received, low, slot, owners, up_own, up_other)


def output_kernel(places, count, own, other, *refs):
    for w_own, w_other, out in zip(refs[:count], refs[count : 2 * count], refs[2 * count :]):
        total = jnp.dot(own[...], w_own[...], preferred_element_type=jnp.float32)
        total += jnp.dot(other[...], w_other[...], preferred_element_type=jnp.float32)
        out[...] = total.astype(out.dtype)


def output_partial(places, first, count, own, other, weight, weight_other, width):
    rows, depth = own.shape
    tile = width // 2 if width % 256 == 0 else width
    steps = width // tile
    whole = pl.BlockSpec((rows, depth), lambda j, p: (0, 0))
    weights = [
        pl.BlockSpec((depth, tile), lambda j, p, i=i: (0, p[first + i] * steps + j))
        for i in range(count)
    ]

    def kernel(places, *refs):
        output_kernel(places, count, *refs)

    return pl.pallas_call(
        kernel,
        grid_spec=pltpu.PrefetchScalarGridSpec(
            num_scalar_prefetch=1,
            grid=(steps,),
            in_specs=[whole, whole] + weights * 2,
            out_specs=[pl.BlockSpec((rows, tile), lambda j, p: (0, j))] * count,
        ),
        out_shape=[jax.ShapeDtypeStruct((rows, width), jnp.bfloat16)] * count,
        compiler_params=pltpu.CompilerParams(vmem_limit_bytes=VMEM_LIMIT),
        cost_estimate=QUICK,
    )(places, own, other, *[weight] * count, *[weight_other] * count)


def attention(query, cache_length, key_cache, value_cache, k_new, v_new):
    local_reqs = query.shape[0]
    kv_count, _, span, dim = key_cache.shape
    group = HEADS // kv_count
    query = query.reshape(local_reqs, kv_count, group, dim)
    k_new = k_new.reshape(local_reqs, kv_count, dim)
    v_new = v_new.reshape(local_reqs, kv_count, dim)
    live = (jnp.arange(span)[None, :] < cache_length[:, None])[None, :, None, :]
    scores = jnp.einsum("rkge,krje->krgj", query, key_cache, preferred_element_type=jnp.float32)
    fresh = jnp.einsum("rkge,rke->krg", query, k_new, preferred_element_type=jnp.float32)
    scores = jnp.where(live, scores, -jnp.inf)
    top = jnp.maximum(jnp.max(scores, axis=3), fresh)
    expd = jnp.where(live, jnp.exp(scores - top[:, :, :, None]), 0.0)
    expf = jnp.exp(fresh - top)
    total = jnp.sum(expd, axis=3) + expf
    probs = (expd / total[:, :, :, None]).astype(jnp.bfloat16)
    probf = (expf / total).astype(jnp.bfloat16)
    context = jnp.einsum("krgj,krje->rkge", probs, value_cache, preferred_element_type=jnp.float32)
    fresh_part = jnp.einsum("krg,rke->rkge", probf.astype(jnp.float32), v_new.astype(jnp.float32))
    return (context + fresh_part).astype(jnp.bfloat16).reshape(local_reqs, HEADS * dim)


def shift(value, axis, by):
    size = lax.axis_size(axis)
    return lax.ppermute(value, axis, [(i, (i + by) % size) for i in range(size)])


def after(value, *others):
    return lax.optimization_barrier((value, *others))[0]


def swap_sides(value, layers):
    return lax.ppermute(value, ("z", "y"), [(2 * i + j, 2 * i + 1 - j) for i in layers for j in (0, 1)])


def gather_features(tokens, down_other, query_weight_other):
    layers, sides = lax.axis_size("z"), lax.axis_size("y")
    z = lax.axis_index("z")
    if layers != 4 or sides != 2:
        entries = []
        for k in range(layers):
            block = shift(tokens, "z", k) if k else tokens
            entries.append(((z - k) % layers, [block, shift(block, "y", 1)][:sides]))
        return entries[:-1], entries[-1:], down_other, query_weight_other
    side = swap_sides(tokens, range(4))
    below = lax.ppermute(tokens, "z", [(0, 1), (1, 2), (2, 3)])
    above = lax.ppermute(tokens, "z", [(1, 0), (2, 1), (3, 2)])
    below, above, side, down_other = lax.optimization_barrier((below, above, side, down_other))
    from_below = lax.ppermute(below, "z", [(1, 2), (2, 3)])
    from_above = lax.ppermute(above, "z", [(2, 1), (1, 0)])
    below_side = swap_sides(below, (1, 2, 3))
    above_side = swap_sides(above, (0, 1, 2))
    from_below, from_above, query_weight_other, below_side = lax.optimization_barrier(
        (from_below, from_above, query_weight_other, below_side)
    )
    far = lax.ppermute(after(tokens, from_below), "z", [(0, 3), (3, 0)])
    two = jnp.where(z >= 2, from_below, from_above)
    two_side = swap_sides(two, range(4))
    far_side = swap_sides(far, (0, 3))
    early = [
        (z, [tokens, side]),
        ((z - 1) % 4, [below, below_side]),
        ((z + 1) % 4, [above, above_side]),
    ]
    late = [((z + 2) % 4, [two, two_side]), (3 - z, [far, far_side])]
    return early, late, down_other, query_weight_other


def spread_up_maps(maps, half, width, early):
    layers, sides = lax.axis_size("z"), lax.axis_size("y")
    z, y, core = lax.axis_index("z"), lax.axis_index("y"), lax.axis_index("core")
    part = maps.shape[0] // 2
    if layers != 4 or sides != 2:
        maps = lax.dynamic_slice_in_dim(maps, half * part, part, 0)
        up = lax.all_to_all(maps, ADP, split_axis=1, concat_axis=0, tiled=True)
        return up, (jnp.arange(up.shape[0], dtype=jnp.int32) // part)[None, :]
    span = 4 * width
    maps = after(maps, early)
    pieces = []
    for k in range(4):
        piece = lax.dynamic_slice(maps, (half * part, (z + k) % 4 * span), (part, span))
        pieces.append(shift(piece, "z", k) if k else piece)
    pieces = jnp.stack(pieces)
    for axis, index in (("y", y), ("core", core)):
        span //= 2
        kept = lax.dynamic_slice_in_dim(pieces, index * span, span, 2)
        sent = lax.dynamic_slice_in_dim(pieces, (1 - index) * span, span, 2)
        pieces = jnp.concatenate([kept, shift(sent, axis, 1)])
    index = jnp.arange(16 * part, dtype=jnp.int32) // part
    layer = (z - index % 4) % 4
    owners = (layer * 2 + (y + index // 4) % 2) * 2 + (core + index // 8) % 2
    return pieces.reshape(16 * part, width), owners.astype(jnp.int32)[None, :]


def scatter_layers(parts):
    layers = lax.axis_size("z")
    wide = lambda value: value.astype(jnp.float32)
    narrow = lambda value: value.astype(jnp.bfloat16)
    if layers != 4:
        return sum([wide(shift(narrow(parts[k]), "z", k)) for k in range(1, layers)], parts[0])
    two = narrow(parts[2])
    up = lax.ppermute(two, "z", [(0, 1), (1, 2)])
    down = lax.ppermute(two, "z", [(3, 2), (2, 1)])
    above = shift(narrow(parts[1] + wide(up)), "z", 1)
    below = shift(narrow(parts[3] + wide(down)), "z", 3)
    return parts[0] + wide(above) + wide(below)


def shards(
    tokens,
    request_adapter,
    adapter_storage_slot,
    cache_length,
    query_weight,
    adapter_down_maps,
    adapter_up_maps,
    key_cache,
    value_cache,
    new_token_key,
    new_token_value,
    output_weight,
):
    layers, sides = lax.axis_size("z"), lax.axis_size("y")
    z, y, core = lax.axis_index("z"), lax.axis_index("y"), lax.axis_index("core")
    rows, width = tokens.shape
    total_adapters = adapter_storage_slot.shape[0]
    rank = adapter_down_maps.shape[2]
    depth = output_weight.shape[0]
    chips_of = lambda layer: [
        (layer % layers) * sides + (y + side) % sides for side in range(sides)
    ]

    down = jnp.swapaxes(adapter_down_maps, 1, 2)
    down_other = shift(down, "core", 1)
    query_weight_other = shift(query_weight, "core", 1)

    ids = request_adapter[:, 0]
    numbers = jnp.arange(total_adapters, dtype=jnp.int32)
    slot = jnp.sum(
        jnp.where(ids[:, None] == numbers[None, :], adapter_storage_slot[None, :], 0), axis=1
    )[:, None]

    early, late, down_other, query_weight_other = gather_features(
        tokens, down_other, query_weight_other
    )
    half = lax.axis_index("rep") % 2
    up, owners = spread_up_maps(jnp.swapaxes(adapter_up_maps, 1, 2)[0], half, width, late[-1][1][0])
    up_other = lax.ppermute(up, "rep", [(i, i ^ 1) for i in range(lax.axis_size("rep"))])
    out_order = [2, 1, 3, 0] if layers == 4 else list(range(1, layers)) + [0]
    out_keys = [(k, side) for k in out_order for side in reversed(range(sides))]
    chips = [chip for layer, _ in early + late for chip in chips_of(layer)]
    chips += [chips_of(z + k)[side] for k, side in out_keys]
    places = jnp.stack([2 * chip + core for chip in chips]).astype(jnp.int32)
    out_first = len(chips) - len(out_keys)
    early, late = ([block for _, pair in group for block in pair] for group in (early, late))

    weights, downs = (query_weight, query_weight_other), (down, down_other)
    base = add_base(after(places, late[0]), 0, early, *weights, ())
    low = add_low(after(places, base[0]), 0, early, *downs, ())
    count = len(late) // 2
    base = add_base(places, len(early), late[:count], *weights, base) if count else base
    low = add_low(after(places, base[0]), len(early), late, *downs, (low, slot))
    low = (low + shift(low, "core", 1)).astype(jnp.bfloat16)
    if sides == 2:
        low = low + shift(low, "y", 1)
    own, sent = add_base(
        after(places, low, up), len(early) + count, late[count:], *weights, base
    )
    received = shift(sent, "core", 1)
    output_weight_other = shift(after(output_weight, received), "core", 1)
    low = sum([shift(low, "z", k) for k in range(1, layers)], low)

    query = make_query(half.astype(jnp.int32).reshape(1), own, received, low, slot, owners, up, up_other)
    query_local = lax.all_to_all(query, ADP, split_axis=0, concat_axis=1, tiled=True)

    context = attention(
        query_local, cache_length, key_cache, value_cache, new_token_key, new_token_value
    )
    context = jnp.swapaxes(context.reshape(context.shape[0], -1, depth), 0, 1)
    context = lax.all_to_all(context, ADP, split_axis=0, concat_axis=0, tiled=True)
    context = context.reshape(rows, depth)
    context_other = shift(context, "core", 1)

    made = {}
    for first, count in ((0, 1), (1, len(out_keys) - 1)):
        outs = output_partial(
            places,
            out_first + first,
            count,
            context,
            context_other,
            output_weight,
            output_weight_other,
            width,
        )
        made.update(zip(out_keys[first : first + count], outs))
    other_side = {k: shift(made[k, 1], "y", 1) for k in out_order if sides == 2}
    parts = [None] * layers
    for k in out_order:
        parts[k] = after(made[k, 0], made[out_keys[-1]]).astype(jnp.float32)
        if sides == 2:
            parts[k] = parts[k] + other_side[k].astype(jnp.float32)
    return scatter_layers(parts).astype(jnp.bfloat16)


def solution(mesh):
    reps, adp = mesh.shape["rep"], mesh.shape["adp"]
    sides = 2 if adp == 16 else 1
    mesh = Mesh(mesh.devices.reshape(reps, adp // (2 * sides), sides, 2), ("rep",) + ADP)
    in_specs = (
        P("rep", ADP),
        P("rep", None),
        P(),
        P(("rep",) + ADP),
        P(None, ADP),
        P(ADP, None, None),
        P(ADP, None, None),
        P(None, ("rep",) + ADP, None, None),
        P(None, ("rep",) + ADP, None, None),
        P(("rep",) + ADP, None),
        P(("rep",) + ADP, None),
        P(ADP, None),
    )
    return jax.shard_map(
        shards, mesh=mesh, in_specs=in_specs, out_specs=P("rep", ADP), check_vma=False
    )
```

```python
import jax
import jax.numpy as jnp
from jax import lax
from jax.experimental import pallas as pl
from jax.experimental.pallas import tpu as pltpu
from jax.sharding import Mesh
from jax.sharding import PartitionSpec as P

HEADS = 64
HEAD_DIM = 128
ADP = ("z", "y", "core")
NT = (((1,), (1,)), ((), ()))
VMEM_LIMIT = 56 << 20
QUICK = pl.CostEstimate(flops=1, bytes_accessed=1, transcendentals=0)


def project_kernel(places, first, count, *refs):
    blocks, w_own, w_other, a_own, a_other = (refs[i * count : (i + 1) * count] for i in range(5))
    ins, outs = refs[5 * count : -3], refs[-3:]
    first_core = places[0] % 2 == 0
    sums = [ref[...] for ref in ins[:3]]
    for i in range(count):
        x = blocks[i][...]
        own, other = a_own[i][0], a_other[i][0]
        pair = jnp.concatenate(
            [jnp.where(first_core, own, other), jnp.where(first_core, other, own)], axis=0
        )
        parts = (
            jnp.dot(x, w_own[i][...], preferred_element_type=jnp.float32),
            jnp.dot(x, w_other[i][...], preferred_element_type=jnp.float32),
            lax.dot_general(x, pair, NT, preferred_element_type=jnp.float32),
        )
        sums = [total + part for total, part in zip(sums, parts)] if sums else parts
    outs[0][...], outs[1][...] = sums[:2]
    low = sums[2]
    if ins:
        slot = ins[3][...]
        rank = low.shape[1] // 2
        mine = places[0] - places[0] % 2
        low = jnp.where(slot == mine, low[:, :rank], 0.0) + jnp.where(
            slot == mine + 1, low[:, rank:], 0.0
        )
        half = low.shape[0] // 2
        low = jnp.concatenate([low[:half], low[half:]], axis=1)
    outs[2][...] = low


def project(places, first, blocks, weight, weight_other, down, down_other, rest):
    count = len(blocks)
    rows, width = blocks[0].shape
    cols, rank = weight.shape[1], down.shape[1]
    flat = lambda shape: pl.BlockSpec(shape, lambda j, p: (0, 0))
    low_rows = rows // 2 if rest else rows
    shapes = [(rows, cols), (rows, cols), (low_rows, 2 * rank)]
    weights = [pl.BlockSpec((width, cols), lambda j, p, i=i: (p[first + i], 0)) for i in range(count)]
    maps = [
        pl.BlockSpec((1, rank, width), lambda j, p, i=i: (0, 0, p[first + i])) for i in range(count)
    ]

    def kernel(places, *refs):
        project_kernel(places, first, count, *refs)

    return pl.pallas_call(
        kernel,
        grid_spec=pltpu.PrefetchScalarGridSpec(
            num_scalar_prefetch=1,
            grid=(1,),
            in_specs=[flat((rows, width))] * count
            + weights * 2
            + maps * 2
            + [flat(array.shape) for array in rest],
            out_specs=[flat(shape) for shape in shapes],
        ),
        out_shape=[jax.ShapeDtypeStruct(shape, jnp.float32) for shape in shapes],
        compiler_params=pltpu.CompilerParams(vmem_limit_bytes=VMEM_LIMIT),
        cost_estimate=QUICK,
    )(
        places,
        *blocks,
        *[weight] * count,
        *[weight_other] * count,
        *[down] * count,
        *[down_other] * count,
        *rest,
    )


def query_kernel(half, own, received, low, slot, up_own, up_other, out):
    step = pl.program_id(0)
    lanes = low.shape[1]
    rank = lanes // 2
    part = rank // 2
    depth = up_own.shape[0]
    shape = (lanes, depth)
    lane = lax.broadcasted_iota(jnp.int32, shape, 1) % part
    row = lax.broadcasted_iota(jnp.int32, shape, 0)
    owner = lax.broadcasted_iota(jnp.int32, (own.shape[0], depth), 1) // part
    live = slot[...] == owner
    total = own[...] + received[...]
    for h, up in ((half[0], up_own), (1 - half[0], up_other)):
        copies = (row == lane + rank * step + part * h).astype(jnp.bfloat16)
        spread = jnp.dot(low[...], copies, preferred_element_type=jnp.float32)
        spread = jnp.where(live, spread, 0.0).astype(jnp.bfloat16)
        total += jnp.dot(spread, up[...], preferred_element_type=jnp.float32)
    out[...] = (total * HEAD_DIM ** (-0.5)).astype(out.dtype)


def make_query(half, own, received, low, slot, up_own, up_other):
    rows, cols = own.shape
    tile = rows // 2
    depth = up_own.shape[0]
    by_rows = lambda width: pl.BlockSpec((tile, width), lambda j, h: (j, 0))
    whole = lambda array: pl.BlockSpec(array.shape, lambda j, h: (0, 0))
    return pl.pallas_call(
        query_kernel,
        grid_spec=pltpu.PrefetchScalarGridSpec(
            num_scalar_prefetch=1,
            grid=(2,),
            in_specs=[
                by_rows(cols),
                by_rows(received.shape[1]),
                whole(low),
                by_rows(1),
                whole(up_own),
                whole(up_other),
            ],
            out_specs=by_rows(cols),
        ),
        out_shape=jax.ShapeDtypeStruct((rows, cols), jnp.bfloat16),
        compiler_params=pltpu.CompilerParams(vmem_limit_bytes=VMEM_LIMIT),
        cost_estimate=QUICK,
    )(half, own, received, low, slot, up_own, up_other)


def output_kernel(places, count, own, other, *refs):
    for w_own, w_other, out in zip(refs[:count], refs[count : 2 * count], refs[2 * count :]):
        total = jnp.dot(own[...], w_own[...], preferred_element_type=jnp.float32)
        total += jnp.dot(other[...], w_other[...], preferred_element_type=jnp.float32)
        out[...] = total.astype(out.dtype)


def output_partial(places, first, count, own, other, weight, weight_other, width):
    rows, depth = own.shape
    tile = width // 2 if width % 256 == 0 else width
    steps = width // tile
    whole = pl.BlockSpec((rows, depth), lambda j, p: (0, 0))
    weights = [
        pl.BlockSpec((depth, tile), lambda j, p, i=i: (0, p[first + i] * steps + j))
        for i in range(count)
    ]

    def kernel(places, *refs):
        output_kernel(places, count, *refs)

    return pl.pallas_call(
        kernel,
        grid_spec=pltpu.PrefetchScalarGridSpec(
            num_scalar_prefetch=1,
            grid=(steps,),
            in_specs=[whole, whole] + weights * 2,
            out_specs=[pl.BlockSpec((rows, tile), lambda j, p: (0, j))] * count,
        ),
        out_shape=[jax.ShapeDtypeStruct((rows, width), jnp.bfloat16)] * count,
        compiler_params=pltpu.CompilerParams(vmem_limit_bytes=VMEM_LIMIT),
        cost_estimate=QUICK,
    )(places, own, other, *[weight] * count, *[weight_other] * count)


def attention(query, cache_length, key_cache, value_cache, k_new, v_new):
    local_reqs = query.shape[0]
    kv_count, _, span, dim = key_cache.shape
    group = HEADS // kv_count
    query = query.reshape(local_reqs, kv_count, group, dim)
    k_new = k_new.reshape(local_reqs, kv_count, dim)
    v_new = v_new.reshape(local_reqs, kv_count, dim)
    live = (jnp.arange(span)[None, :] < cache_length[:, None])[None, :, None, :]
    scores = jnp.einsum("rkge,krje->krgj", query, key_cache, preferred_element_type=jnp.float32)
    fresh = jnp.einsum("rkge,rke->krg", query, k_new, preferred_element_type=jnp.float32)
    scores = jnp.where(live, scores, -jnp.inf)
    top = jnp.maximum(jnp.max(scores, axis=3), fresh)
    expd = jnp.where(live, jnp.exp(scores - top[:, :, :, None]), 0.0)
    expf = jnp.exp(fresh - top)
    total = jnp.sum(expd, axis=3) + expf
    probs = (expd / total[:, :, :, None]).astype(jnp.bfloat16)
    probf = (expf / total).astype(jnp.bfloat16)
    context = jnp.einsum("krgj,krje->rkge", probs, value_cache, preferred_element_type=jnp.float32)
    fresh_part = jnp.einsum("krg,rke->rkge", probf.astype(jnp.float32), v_new.astype(jnp.float32))
    return (context + fresh_part).astype(jnp.bfloat16).reshape(local_reqs, HEADS * dim)


def shift(value, axis, by):
    size = lax.axis_size(axis)
    return lax.ppermute(value, axis, [(i, (i + by) % size) for i in range(size)])


def after(value, *others):
    return lax.optimization_barrier((value, *others))[0]


def gather_features(tokens, down_other, up):
    layers, sides = lax.axis_size("z"), lax.axis_size("y")
    z = lax.axis_index("z")
    if layers != 4 or sides != 2:
        entries = []
        for k in range(layers):
            block = shift(tokens, "z", k) if k else tokens
            entries.append(((z - k) % layers, [block, shift(block, "y", 1)][:sides]))
        return entries, down_other
    side = shift(tokens, "y", 1)
    below, above = shift(tokens, "z", 1), shift(tokens, "z", 3)
    below, side, down_other = lax.optimization_barrier((below, side, down_other))
    below_side = shift(below, "y", 1)
    from_below = lax.ppermute(below, "z", [(1, 2), (2, 3)])
    above_side = shift(above, "y", 1)
    from_above = lax.ppermute(above, "z", [(2, 1), (1, 0)])
    two = jnp.where(z >= 2, from_below, from_above)
    two = after(two, below_side, up)
    two_side = shift(two, "y", 1)
    return [
        (z, [tokens, side]),
        ((z - 1) % 4, [below, below_side]),
        ((z + 1) % 4, [above, above_side]),
        ((z + 2) % 4, [two, two_side]),
    ], down_other


def scatter_layers(parts):
    layers = lax.axis_size("z")
    wide = lambda value: value.astype(jnp.float32)
    narrow = lambda value: value.astype(jnp.bfloat16)
    if layers != 4:
        return sum([wide(shift(narrow(parts[k]), "z", k)) for k in range(1, layers)], parts[0])
    two = narrow(parts[2])
    up = lax.ppermute(two, "z", [(0, 1), (1, 2)])
    down = lax.ppermute(two, "z", [(3, 2), (2, 1)])
    above = shift(narrow(parts[1] + wide(up)), "z", 1)
    below = shift(narrow(parts[3] + wide(down)), "z", 3)
    return parts[0] + wide(above) + wide(below)


def shards(
    tokens,
    request_adapter,
    adapter_storage_slot,
    cache_length,
    query_weight,
    adapter_down_maps,
    adapter_up_maps,
    key_cache,
    value_cache,
    new_token_key,
    new_token_value,
    output_weight,
):
    layers, sides = lax.axis_size("z"), lax.axis_size("y")
    z, y, core = lax.axis_index("z"), lax.axis_index("y"), lax.axis_index("core")
    rows, width = tokens.shape
    total_adapters = adapter_storage_slot.shape[0]
    rank = adapter_down_maps.shape[2]
    depth = output_weight.shape[0]
    chips_of = lambda layer: [
        (layer % layers) * sides + (y + side) % sides for side in range(sides)
    ]

    down = jnp.swapaxes(adapter_down_maps, 1, 2)
    down_other = shift(down, "core", 1)
    query_weight_other = shift(query_weight, "core", 1)

    ids = request_adapter[:, 0]
    numbers = jnp.arange(total_adapters, dtype=jnp.int32)
    slot = jnp.sum(
        jnp.where(ids[:, None] == numbers[None, :], adapter_storage_slot[None, :], 0), axis=1
    )[:, None]

    half = lax.axis_index("rep") % 2
    up = jnp.swapaxes(adapter_up_maps, 1, 2)[0]
    up = lax.dynamic_slice_in_dim(up, half * (rank // 2), rank // 2, 0)
    up = lax.all_to_all(up, ADP, split_axis=1, concat_axis=0, tiled=True)
    up_other = lax.ppermute(up, "rep", [(i, i ^ 1) for i in range(lax.axis_size("rep"))])

    entries, down_other = gather_features(tokens, down_other, up)
    out_order = [2, 1, 3, 0] if layers == 4 else list(range(1, layers)) + [0]
    out_keys = [(k, side) for k in out_order for side in reversed(range(sides))]
    chips = [chip for layer, _ in entries for chip in chips_of(layer)]
    chips += [chips_of(z + k)[side] for k, side in out_keys]
    places = jnp.stack([2 * chip + core for chip in chips]).astype(jnp.int32)
    out_first = len(chips) - len(out_keys)

    blocks = [block for _, pair in entries for block in pair]
    last = len(blocks) - sides
    weights = query_weight, query_weight_other, down, down_other
    sums = project(places, 0, blocks[:last], *weights, ())
    own, sent, low = project(places, last, blocks[last:], *weights, (*sums, slot))

    low = (low + shift(low, "core", 1)).astype(jnp.bfloat16)
    received = shift(sent, "core", 1)
    if sides == 2:
        low = low + shift(low, "y", 1)
    low = sum([shift(low, "z", k) for k in range(1, layers)], low)
    output_weight_other = shift(after(output_weight, low), "core", 1)

    query = make_query(half.astype(jnp.int32).reshape(1), own, received, low, slot, up, up_other)
    query_local = lax.all_to_all(query, ADP, split_axis=0, concat_axis=1, tiled=True)

    context = attention(
        query_local, cache_length, key_cache, value_cache, new_token_key, new_token_value
    )
    context = jnp.swapaxes(context.reshape(context.shape[0], -1, depth), 0, 1)
    context = lax.all_to_all(context, ADP, split_axis=0, concat_axis=0, tiled=True)
    context = context.reshape(rows, depth)
    context_other = shift(context, "core", 1)

    made = {}
    for first, count in ((0, 1), (1, len(out_keys) - 1)):
        outs = output_partial(
            places,
            out_first + first,
            count,
            context,
            context_other,
            output_weight,
            output_weight_other,
            width,
        )
        made.update(zip(out_keys[first : first + count], outs))
    other_side = {k: shift(made[k, 1], "y", 1) for k in out_order if sides == 2}
    parts = [None] * layers
    for k in out_order:
        parts[k] = after(made[k, 0], made[out_keys[-1]]).astype(jnp.float32)
        if sides == 2:
            parts[k] = parts[k] + other_side[k].astype(jnp.float32)
    return scatter_layers(parts).astype(jnp.bfloat16)


def solution(mesh):
    reps, adp = mesh.shape["rep"], mesh.shape["adp"]
    sides = 2 if adp == 16 else 1
    mesh = Mesh(mesh.devices.reshape(reps, adp // (2 * sides), sides, 2), ("rep",) + ADP)
    in_specs = (
        P("rep", ADP),
        P("rep", None),
        P(),
        P(("rep",) + ADP),
        P(None, ADP),
        P(ADP, None, None),
        P(ADP, None, None),
        P(None, ("rep",) + ADP, None, None),
        P(None, ("rep",) + ADP, None, None),
        P(("rep",) + ADP, None),
        P(("rep",) + ADP, None),
        P(ADP, None),
    )
    return jax.shard_map(
        shards, mesh=mesh, in_specs=in_specs, out_specs=P("rep", ADP), check_vma=False
    )
```

```python
import jax
import jax.numpy as jnp
from jax import lax
from jax.experimental import pallas as pl
from jax.experimental.pallas import tpu as pltpu
from jax.sharding import Mesh
from jax.sharding import PartitionSpec as P

HEADS = 64
HEAD_DIM = 128
ADP = ("z", "y", "core")
GATHERED = ((0, 0), (0, 1), (3, 0), (1, 0), (3, 1), (1, 1), (2, 0), (2, 1))
NT = (((1,), (1,)), ((), ()))
VMEM_LIMIT = 56 << 20
QUICK = pl.CostEstimate(flops=1, bytes_accessed=1, transcendentals=0)


def project_kernel(places, first, count, *refs):
    blocks, w_own, w_other, a_own, a_other = (refs[i * count : (i + 1) * count] for i in range(5))
    ins, outs = refs[5 * count : -3], refs[-3:]
    first_core = places[0] % 2 == 0
    sums = [ref[...] for ref in ins[:3]]
    for i in range(count):
        x = blocks[i][...]
        own, other = a_own[i][0], a_other[i][0]
        pair = jnp.concatenate(
            [jnp.where(first_core, own, other), jnp.where(first_core, other, own)], axis=0
        )
        parts = (
            jnp.dot(x, w_own[i][...], preferred_element_type=jnp.float32),
            jnp.dot(x, w_other[i][...], preferred_element_type=jnp.float32),
            lax.dot_general(x, pair, NT, preferred_element_type=jnp.float32),
        )
        sums = [total + part for total, part in zip(sums, parts)] if sums else parts
    outs[0][...], outs[1][...] = sums[:2]
    low = sums[2]
    if ins:
        slot = ins[3][...]
        rank = low.shape[1] // 2
        mine = places[0] - places[0] % 2
        low = jnp.where(slot == mine, low[:, :rank], 0.0) + jnp.where(
            slot == mine + 1, low[:, rank:], 0.0
        )
        half = low.shape[0] // 2
        low = jnp.concatenate([low[:half], low[half:]], axis=1)
    outs[2][...] = low


def project(places, first, blocks, weight, weight_other, down, down_other, rest):
    count = len(blocks)
    rows, width = blocks[0].shape
    cols, rank = weight.shape[1], down.shape[1]
    flat = lambda shape: pl.BlockSpec(shape, lambda j, p: (0, 0))
    low_rows = rows // 2 if rest else rows
    shapes = [(rows, cols), (rows, cols), (low_rows, 2 * rank)]
    weights = [pl.BlockSpec((width, cols), lambda j, p, i=i: (p[first + i], 0)) for i in range(count)]
    maps = [
        pl.BlockSpec((1, rank, width), lambda j, p, i=i: (0, 0, p[first + i])) for i in range(count)
    ]

    def kernel(places, *refs):
        project_kernel(places, first, count, *refs)

    return pl.pallas_call(
        kernel,
        grid_spec=pltpu.PrefetchScalarGridSpec(
            num_scalar_prefetch=1,
            grid=(1,),
            in_specs=[flat((rows, width))] * count
            + weights * 2
            + maps * 2
            + [flat(array.shape) for array in rest],
            out_specs=[flat(shape) for shape in shapes],
        ),
        out_shape=[jax.ShapeDtypeStruct(shape, jnp.float32) for shape in shapes],
        compiler_params=pltpu.CompilerParams(vmem_limit_bytes=VMEM_LIMIT),
        cost_estimate=QUICK,
    )(
        places,
        *blocks,
        *[weight] * count,
        *[weight_other] * count,
        *[down] * count,
        *[down_other] * count,
        *rest,
    )


def query_kernel(half, own, received, low, slot, up_own, up_other, out):
    step = pl.program_id(0)
    lanes = low.shape[1]
    rank = lanes // 2
    part = rank // 2
    depth = up_own.shape[0]
    shape = (lanes, depth)
    lane = lax.broadcasted_iota(jnp.int32, shape, 1) % part
    row = lax.broadcasted_iota(jnp.int32, shape, 0)
    owner = lax.broadcasted_iota(jnp.int32, (own.shape[0], depth), 1) // part
    live = slot[...] == owner
    total = own[...] + received[...]
    for h, up in ((half[0], up_own), (1 - half[0], up_other)):
        copies = (row == lane + rank * step + part * h).astype(jnp.bfloat16)
        spread = jnp.dot(low[...], copies, preferred_element_type=jnp.float32)
        spread = jnp.where(live, spread, 0.0).astype(jnp.bfloat16)
        total += jnp.dot(spread, up[...], preferred_element_type=jnp.float32)
    out[...] = (total * HEAD_DIM ** (-0.5)).astype(out.dtype)


def make_query(half, own, received, low, slot, up_own, up_other):
    rows, cols = own.shape
    tile = rows // 2
    depth = up_own.shape[0]
    by_rows = lambda width: pl.BlockSpec((tile, width), lambda j, h: (j, 0))
    whole = lambda array: pl.BlockSpec(array.shape, lambda j, h: (0, 0))
    return pl.pallas_call(
        query_kernel,
        grid_spec=pltpu.PrefetchScalarGridSpec(
            num_scalar_prefetch=1,
            grid=(2,),
            in_specs=[
                by_rows(cols),
                by_rows(received.shape[1]),
                whole(low),
                by_rows(1),
                whole(up_own),
                whole(up_other),
            ],
            out_specs=by_rows(cols),
        ),
        out_shape=jax.ShapeDtypeStruct((rows, cols), jnp.bfloat16),
        compiler_params=pltpu.CompilerParams(vmem_limit_bytes=VMEM_LIMIT),
        cost_estimate=QUICK,
    )(half, own, received, low, slot, up_own, up_other)


def output_kernel(places, count, own, other, *refs):
    for w_own, w_other, out in zip(refs[:count], refs[count : 2 * count], refs[2 * count :]):
        total = jnp.dot(own[...], w_own[...], preferred_element_type=jnp.float32)
        total += jnp.dot(other[...], w_other[...], preferred_element_type=jnp.float32)
        out[...] = total.astype(out.dtype)


def output_partial(places, first, count, own, other, weight, weight_other, width):
    rows, depth = own.shape
    tile = width // 2 if width % 256 == 0 else width
    steps = width // tile
    whole = pl.BlockSpec((rows, depth), lambda j, p: (0, 0))
    weights = [
        pl.BlockSpec((depth, tile), lambda j, p, i=i: (0, p[first + i] * steps + j))
        for i in range(count)
    ]

    def kernel(places, *refs):
        output_kernel(places, count, *refs)

    return pl.pallas_call(
        kernel,
        grid_spec=pltpu.PrefetchScalarGridSpec(
            num_scalar_prefetch=1,
            grid=(steps,),
            in_specs=[whole, whole] + weights * 2,
            out_specs=[pl.BlockSpec((rows, tile), lambda j, p: (0, j))] * count,
        ),
        out_shape=[jax.ShapeDtypeStruct((rows, width), jnp.bfloat16)] * count,
        compiler_params=pltpu.CompilerParams(vmem_limit_bytes=VMEM_LIMIT),
        cost_estimate=QUICK,
    )(places, own, other, *[weight] * count, *[weight_other] * count)


def attention(query, cache_length, key_cache, value_cache, k_new, v_new):
    local_reqs = query.shape[0]
    kv_count, _, span, dim = key_cache.shape
    group = HEADS // kv_count
    query = query.reshape(local_reqs, kv_count, group, dim)
    k_new = k_new.reshape(local_reqs, kv_count, dim)
    v_new = v_new.reshape(local_reqs, kv_count, dim)
    live = (jnp.arange(span)[None, :] < cache_length[:, None])[None, :, None, :]
    scores = jnp.einsum("rkge,krje->krgj", query, key_cache, preferred_element_type=jnp.float32)
    fresh = jnp.einsum("rkge,rke->krg", query, k_new, preferred_element_type=jnp.float32)
    scores = jnp.where(live, scores, -jnp.inf)
    top = jnp.maximum(jnp.max(scores, axis=3), fresh)
    expd = jnp.where(live, jnp.exp(scores - top[:, :, :, None]), 0.0)
    expf = jnp.exp(fresh - top)
    total = jnp.sum(expd, axis=3) + expf
    probs = (expd / total[:, :, :, None]).astype(jnp.bfloat16)
    probf = (expf / total).astype(jnp.bfloat16)
    context = jnp.einsum("krgj,krje->rkge", probs, value_cache, preferred_element_type=jnp.float32)
    fresh_part = jnp.einsum("krg,rke->rkge", probf.astype(jnp.float32), v_new.astype(jnp.float32))
    return (context + fresh_part).astype(jnp.bfloat16).reshape(local_reqs, HEADS * dim)


def shift(value, axis, by):
    size = lax.axis_size(axis)
    return lax.ppermute(value, axis, [(i, (i + by) % size) for i in range(size)])


def after(value, *others):
    return lax.optimization_barrier((value, *others))[0]


def gathered_chips():
    layers, sides = lax.axis_size("z"), lax.axis_size("y")
    z, y = lax.axis_index("z"), lax.axis_index("y")
    steps = GATHERED
    if layers != 4 or sides != 2:
        steps = [(-k, side) for k in range(layers) for side in range(sides)]
    return [((z + k) % layers) * sides + (y + side) % sides for k, side in steps]


def gather_features(tokens, down_other, up, begin):
    layers, sides = lax.axis_size("z"), lax.axis_size("y")
    z = lax.axis_index("z")
    if layers != 4 or sides != 2:
        blocks = [shift(tokens, "z", k) if k else tokens for k in range(layers)]
        blocks = [[block, shift(block, "y", 1)][:sides] for block in blocks]
        blocks = [block for pair in blocks for block in pair]
        return begin(blocks[:-1]), blocks[-1:], up
    side = shift(tokens, "y", 1)
    below, above = shift(tokens, "z", 1), shift(tokens, "z", 3)
    below, side, _ = lax.optimization_barrier((below, side, down_other))
    below_side = shift(below, "y", 1)
    from_below = lax.ppermute(below, "z", [(1, 2), (2, 3)])
    above = after(above, below_side)
    above_side = shift(above, "y", 1)
    from_above = lax.ppermute(above, "z", [(2, 1), (1, 0)])
    sums = begin([tokens, side, below, above])
    from_above, from_below, up, sums = lax.optimization_barrier((from_above, from_below, up, sums))
    two = jnp.where(z >= 2, from_below, from_above)
    return sums, [below_side, above_side, two, shift(two, "y", 1)], up


def scatter_layers(parts):
    layers = lax.axis_size("z")
    wide = lambda value: value.astype(jnp.float32)
    narrow = lambda value: value.astype(jnp.bfloat16)
    if layers != 4:
        return sum([wide(shift(narrow(parts[k]), "z", k)) for k in range(1, layers)], parts[0])
    two = narrow(parts[2])
    up = lax.ppermute(two, "z", [(0, 1), (1, 2)])
    down = lax.ppermute(two, "z", [(3, 2), (2, 1)])
    above = shift(narrow(parts[1] + wide(up)), "z", 1)
    below = shift(narrow(parts[3] + wide(down)), "z", 3)
    return parts[0] + wide(above) + wide(below)


def shards(
    tokens,
    request_adapter,
    adapter_storage_slot,
    cache_length,
    query_weight,
    adapter_down_maps,
    adapter_up_maps,
    key_cache,
    value_cache,
    new_token_key,
    new_token_value,
    output_weight,
):
    layers, sides = lax.axis_size("z"), lax.axis_size("y")
    z, y, core = lax.axis_index("z"), lax.axis_index("y"), lax.axis_index("core")
    rows, width = tokens.shape
    total_adapters = adapter_storage_slot.shape[0]
    rank = adapter_down_maps.shape[2]
    depth = output_weight.shape[0]
    chips_of = lambda layer: [
        (layer % layers) * sides + (y + side) % sides for side in range(sides)
    ]

    down = jnp.swapaxes(adapter_down_maps, 1, 2)
    down_other = shift(down, "core", 1)
    query_weight_other = shift(query_weight, "core", 1)

    ids = request_adapter[:, 0]
    numbers = jnp.arange(total_adapters, dtype=jnp.int32)
    slot = jnp.sum(
        jnp.where(ids[:, None] == numbers[None, :], adapter_storage_slot[None, :], 0), axis=1
    )[:, None]

    half = lax.axis_index("rep") % 2
    up = jnp.swapaxes(adapter_up_maps, 1, 2)[0]
    up = lax.dynamic_slice_in_dim(up, half * (rank // 2), rank // 2, 0)
    up = lax.all_to_all(up, ADP, split_axis=1, concat_axis=0, tiled=True)
    out_order = [2, 1, 3, 0] if layers == 4 else list(range(1, layers)) + [0]
    out_keys = [(k, side) for k in out_order for side in reversed(range(sides))]
    chips = gathered_chips()
    out_first = len(chips)
    chips += [chips_of(z + k)[side] for k, side in out_keys]
    places = jnp.stack([2 * chip + core for chip in chips]).astype(jnp.int32)

    weights = query_weight, query_weight_other, down, down_other
    sums, blocks, up = gather_features(
        tokens, down_other, up, lambda blocks: project(places, 0, blocks, *weights, ())
    )
    up_other = lax.ppermute(up, "rep", [(i, i ^ 1) for i in range(lax.axis_size("rep"))])
    own, sent, low = project(
        after(places, up_other), out_first - len(blocks), blocks, *weights, (*sums, slot)
    )

    low = (low + shift(low, "core", 1)).astype(jnp.bfloat16)
    received = shift(sent, "core", 1)
    if sides == 2:
        low = low + shift(low, "y", 1)
    low = sum([shift(low, "z", k) for k in range(1, layers)], low)
    output_weight_other = shift(after(output_weight, low), "core", 1)

    query = make_query(half.astype(jnp.int32).reshape(1), own, received, low, slot, up, up_other)
    query_local = lax.all_to_all(query, ADP, split_axis=0, concat_axis=1, tiled=True)

    context = attention(
        query_local, cache_length, key_cache, value_cache, new_token_key, new_token_value
    )
    context = jnp.swapaxes(context.reshape(context.shape[0], -1, depth), 0, 1)
    context = lax.all_to_all(context, ADP, split_axis=0, concat_axis=0, tiled=True)
    context = context.reshape(rows, depth)
    context_other = shift(context, "core", 1)

    made = {}
    for first, count in ((0, 1), (1, len(out_keys) - 1)):
        outs = output_partial(
            places,
            out_first + first,
            count,
            context,
            context_other,
            output_weight,
            output_weight_other,
            width,
        )
        made.update(zip(out_keys[first : first + count], outs))
    other_side = {k: shift(made[k, 1], "y", 1) for k in out_order if sides == 2}
    parts = [None] * layers
    for k in out_order:
        parts[k] = after(made[k, 0], made[out_keys[-1]]).astype(jnp.float32)
        if sides == 2:
            parts[k] = parts[k] + other_side[k].astype(jnp.float32)
    return scatter_layers(parts).astype(jnp.bfloat16)


def solution(mesh):
    reps, adp = mesh.shape["rep"], mesh.shape["adp"]
    sides = 2 if adp == 16 else 1
    mesh = Mesh(mesh.devices.reshape(reps, adp // (2 * sides), sides, 2), ("rep",) + ADP)
    in_specs = (
        P("rep", ADP),
        P("rep", None),
        P(),
        P(("rep",) + ADP),
        P(None, ADP),
        P(ADP, None, None),
        P(ADP, None, None),
        P(None, ("rep",) + ADP, None, None),
        P(None, ("rep",) + ADP, None, None),
        P(("rep",) + ADP, None),
        P(("rep",) + ADP, None),
        P(ADP, None),
    )
    return jax.shard_map(
        shards, mesh=mesh, in_specs=in_specs, out_specs=P("rep", ADP), check_vma=False
    )
```

```python
import jax
import jax.numpy as jnp
from jax import lax
from jax.experimental import pallas as pl
from jax.experimental.pallas import tpu as pltpu
from jax.sharding import Mesh
from jax.sharding import PartitionSpec as P

HEADS = 64
HEAD_DIM = 128
ADP = ("z", "y", "core")
GATHERED = ((0, 0), (0, 1), (3, 0), (1, 0), (3, 1), (1, 1), (2, 0), (2, 1))
NT = (((1,), (1,)), ((), ()))
VMEM_LIMIT = 56 << 20
QUICK = pl.CostEstimate(flops=1, bytes_accessed=1, transcendentals=0)


def project_kernel(places, first, count, *refs):
    blocks, w_own, w_other, a_own, a_other = (refs[i * count : (i + 1) * count] for i in range(5))
    ins, outs = refs[5 * count : -3], refs[-3:]
    first_core = places[0] % 2 == 0
    sums = [ref[...] for ref in ins[:3]]
    for i in range(count):
        x = blocks[i][...]
        own, other = a_own[i][0], a_other[i][0]
        pair = jnp.concatenate(
            [jnp.where(first_core, own, other), jnp.where(first_core, other, own)], axis=0
        )
        parts = (
            jnp.dot(x, w_own[i][...], preferred_element_type=jnp.float32),
            jnp.dot(x, w_other[i][...], preferred_element_type=jnp.float32),
            lax.dot_general(x, pair, NT, preferred_element_type=jnp.float32),
        )
        sums = [total + part for total, part in zip(sums, parts)] if sums else parts
    outs[0][...], outs[1][...] = sums[:2]
    low = sums[2]
    if ins:
        slot = ins[3][...]
        rank = low.shape[1] // 2
        mine = places[0] - places[0] % 2
        low = jnp.where(slot == mine, low[:, :rank], 0.0) + jnp.where(
            slot == mine + 1, low[:, rank:], 0.0
        )
        half = low.shape[0] // 2
        low = jnp.concatenate([low[:half], low[half:]], axis=1)
    outs[2][...] = low


def project(places, first, blocks, weight, weight_other, down, down_other, rest):
    count = len(blocks)
    rows, width = blocks[0].shape
    cols, rank = weight.shape[1], down.shape[1]
    flat = lambda shape: pl.BlockSpec(shape, lambda j, p: (0, 0))
    low_rows = rows // 2 if rest else rows
    shapes = [(rows, cols), (rows, cols), (low_rows, 2 * rank)]
    weights = [pl.BlockSpec((width, cols), lambda j, p, i=i: (p[first + i], 0)) for i in range(count)]
    maps = [
        pl.BlockSpec((1, rank, width), lambda j, p, i=i: (0, 0, p[first + i])) for i in range(count)
    ]

    def kernel(places, *refs):
        project_kernel(places, first, count, *refs)

    return pl.pallas_call(
        kernel,
        grid_spec=pltpu.PrefetchScalarGridSpec(
            num_scalar_prefetch=1,
            grid=(1,),
            in_specs=[flat((rows, width))] * count
            + weights * 2
            + maps * 2
            + [flat(array.shape) for array in rest],
            out_specs=[flat(shape) for shape in shapes],
        ),
        out_shape=[jax.ShapeDtypeStruct(shape, jnp.float32) for shape in shapes],
        compiler_params=pltpu.CompilerParams(vmem_limit_bytes=VMEM_LIMIT),
        cost_estimate=QUICK,
    )(
        places,
        *blocks,
        *[weight] * count,
        *[weight_other] * count,
        *[down] * count,
        *[down_other] * count,
        *rest,
    )


def query_kernel(half, own, received, low, slot, up_own, up_other, out):
    step = pl.program_id(0)
    lanes = low.shape[1]
    rank = lanes // 2
    part = rank // 2
    depth = up_own.shape[0]
    shape = (lanes, depth)
    lane = lax.broadcasted_iota(jnp.int32, shape, 1) % part
    row = lax.broadcasted_iota(jnp.int32, shape, 0)
    owner = lax.broadcasted_iota(jnp.int32, (own.shape[0], depth), 1) // part
    live = slot[...] == owner
    total = own[...] + received[...]
    for h, up in ((half[0], up_own), (1 - half[0], up_other)):
        copies = (row == lane + rank * step + part * h).astype(jnp.bfloat16)
        spread = jnp.dot(low[...], copies, preferred_element_type=jnp.float32)
        spread = jnp.where(live, spread, 0.0).astype(jnp.bfloat16)
        total += jnp.dot(spread, up[...], preferred_element_type=jnp.float32)
    out[...] = (total * HEAD_DIM ** (-0.5)).astype(out.dtype)


def make_query(half, own, received, low, slot, up_own, up_other):
    rows, cols = own.shape
    tile = rows // 2
    depth = up_own.shape[0]
    by_rows = lambda width: pl.BlockSpec((tile, width), lambda j, h: (j, 0))
    whole = lambda array: pl.BlockSpec(array.shape, lambda j, h: (0, 0))
    return pl.pallas_call(
        query_kernel,
        grid_spec=pltpu.PrefetchScalarGridSpec(
            num_scalar_prefetch=1,
            grid=(2,),
            in_specs=[
                by_rows(cols),
                by_rows(received.shape[1]),
                whole(low),
                by_rows(1),
                whole(up_own),
                whole(up_other),
            ],
            out_specs=by_rows(cols),
        ),
        out_shape=jax.ShapeDtypeStruct((rows, cols), jnp.bfloat16),
        compiler_params=pltpu.CompilerParams(vmem_limit_bytes=VMEM_LIMIT),
        cost_estimate=QUICK,
    )(half, own, received, low, slot, up_own, up_other)


def output_kernel(places, count, own, other, *refs):
    for w_own, w_other, out in zip(refs[:count], refs[count : 2 * count], refs[2 * count :]):
        total = jnp.dot(own[...], w_own[...], preferred_element_type=jnp.float32)
        total += jnp.dot(other[...], w_other[...], preferred_element_type=jnp.float32)
        out[...] = total.astype(out.dtype)


def output_partial(places, first, count, own, other, weight, weight_other, width):
    rows, depth = own.shape
    tile = width // 2 if width % 256 == 0 else width
    steps = width // tile
    whole = pl.BlockSpec((rows, depth), lambda j, p: (0, 0))
    weights = [
        pl.BlockSpec((depth, tile), lambda j, p, i=i: (0, p[first + i] * steps + j))
        for i in range(count)
    ]

    def kernel(places, *refs):
        output_kernel(places, count, *refs)

    return pl.pallas_call(
        kernel,
        grid_spec=pltpu.PrefetchScalarGridSpec(
            num_scalar_prefetch=1,
            grid=(steps,),
            in_specs=[whole, whole] + weights * 2,
            out_specs=[pl.BlockSpec((rows, tile), lambda j, p: (0, j))] * count,
        ),
        out_shape=[jax.ShapeDtypeStruct((rows, width), jnp.bfloat16)] * count,
        compiler_params=pltpu.CompilerParams(vmem_limit_bytes=VMEM_LIMIT),
        cost_estimate=QUICK,
    )(places, own, other, *[weight] * count, *[weight_other] * count)


def attention(query, cache_length, key_cache, value_cache, k_new, v_new):
    local_reqs = query.shape[0]
    kv_count, _, span, dim = key_cache.shape
    group = HEADS // kv_count
    query = query.reshape(local_reqs, kv_count, group, dim)
    k_new = k_new.reshape(local_reqs, kv_count, dim)
    v_new = v_new.reshape(local_reqs, kv_count, dim)
    live = (jnp.arange(span)[None, :] < cache_length[:, None])[None, :, None, :]
    scores = jnp.einsum("rkge,krje->krgj", query, key_cache, preferred_element_type=jnp.float32)
    fresh = jnp.einsum("rkge,rke->krg", query, k_new, preferred_element_type=jnp.float32)
    scores = jnp.where(live, scores, -jnp.inf)
    top = jnp.maximum(jnp.max(scores, axis=3), fresh)
    expd = jnp.where(live, jnp.exp(scores - top[:, :, :, None]), 0.0)
    expf = jnp.exp(fresh - top)
    total = jnp.sum(expd, axis=3) + expf
    probs = (expd / total[:, :, :, None]).astype(jnp.bfloat16)
    probf = (expf / total).astype(jnp.bfloat16)
    context = jnp.einsum("krgj,krje->rkge", probs, value_cache, preferred_element_type=jnp.float32)
    fresh_part = jnp.einsum("krg,rke->rkge", probf.astype(jnp.float32), v_new.astype(jnp.float32))
    return (context + fresh_part).astype(jnp.bfloat16).reshape(local_reqs, HEADS * dim)


def shift(value, axis, by):
    size = lax.axis_size(axis)
    return lax.ppermute(value, axis, [(i, (i + by) % size) for i in range(size)])


def after(value, *others):
    return lax.optimization_barrier((value, *others))[0]


def gathered_chips():
    layers, sides = lax.axis_size("z"), lax.axis_size("y")
    z, y = lax.axis_index("z"), lax.axis_index("y")
    steps = GATHERED
    if layers != 4 or sides != 2:
        steps = [(-k, side) for k in range(layers) for side in range(sides)]
    return [((z + k) % layers) * sides + (y + side) % sides for k, side in steps]


def gather_features(tokens, down_other, begin):
    layers, sides = lax.axis_size("z"), lax.axis_size("y")
    z = lax.axis_index("z")
    if layers != 4 or sides != 2:
        blocks = [shift(tokens, "z", k) if k else tokens for k in range(layers)]
        blocks = [[block, shift(block, "y", 1)][:sides] for block in blocks]
        blocks = [block for pair in blocks for block in pair]
        return begin(blocks[:-1]), blocks[-1:]
    side = shift(tokens, "y", 1)
    below, above = shift(tokens, "z", 1), shift(tokens, "z", 3)
    below, side, _ = lax.optimization_barrier((below, side, down_other))
    below_side = shift(below, "y", 1)
    from_below = lax.ppermute(below, "z", [(1, 2), (2, 3)])
    above = after(above, below_side)
    above_side = shift(above, "y", 1)
    from_above = lax.ppermute(above, "z", [(2, 1), (1, 0)])
    sums = begin([tokens, side, below, above])
    from_above, from_below, sums = lax.optimization_barrier((from_above, from_below, sums))
    two = jnp.where(z >= 2, from_below, from_above)
    return sums, [below_side, above_side, two, shift(two, "y", 1)]


def scatter_layers(parts):
    layers = lax.axis_size("z")
    wide = lambda value: value.astype(jnp.float32)
    narrow = lambda value: value.astype(jnp.bfloat16)
    if layers != 4:
        return sum([wide(shift(narrow(parts[k]), "z", k)) for k in range(1, layers)], parts[0])
    two = narrow(parts[2])
    up = lax.ppermute(two, "z", [(0, 1), (1, 2)])
    down = lax.ppermute(two, "z", [(3, 2), (2, 1)])
    above = shift(narrow(parts[1] + wide(up)), "z", 1)
    below = shift(narrow(parts[3] + wide(down)), "z", 3)
    return parts[0] + wide(above) + wide(below)


def shards(
    tokens,
    request_adapter,
    adapter_storage_slot,
    cache_length,
    query_weight,
    adapter_down_maps,
    adapter_up_maps,
    key_cache,
    value_cache,
    new_token_key,
    new_token_value,
    output_weight,
):
    layers, sides = lax.axis_size("z"), lax.axis_size("y")
    z, y, core = lax.axis_index("z"), lax.axis_index("y"), lax.axis_index("core")
    rows, width = tokens.shape
    total_adapters = adapter_storage_slot.shape[0]
    rank = adapter_down_maps.shape[2]
    depth = output_weight.shape[0]
    chips_of = lambda layer: [
        (layer % layers) * sides + (y + side) % sides for side in range(sides)
    ]

    down = jnp.swapaxes(adapter_down_maps, 1, 2)
    down_other = shift(down, "core", 1)
    query_weight_other = shift(query_weight, "core", 1)

    ids = request_adapter[:, 0]
    numbers = jnp.arange(total_adapters, dtype=jnp.int32)
    slot = jnp.sum(
        jnp.where(ids[:, None] == numbers[None, :], adapter_storage_slot[None, :], 0), axis=1
    )[:, None]

    out_order = [2, 1, 3, 0] if layers == 4 else list(range(1, layers)) + [0]
    out_keys = [(k, side) for k in out_order for side in reversed(range(sides))]
    chips = gathered_chips()
    out_first = len(chips)
    chips += [chips_of(z + k)[side] for k, side in out_keys]
    places = jnp.stack([2 * chip + core for chip in chips]).astype(jnp.int32)

    weights = query_weight, query_weight_other, down, down_other
    sums, blocks = gather_features(
        tokens, down_other, lambda blocks: project(places, 0, blocks, *weights, ())
    )

    half = lax.axis_index("rep") % 2
    up = jnp.swapaxes(adapter_up_maps, 1, 2)[0]
    up = lax.dynamic_slice_in_dim(up, half * (rank // 2), rank // 2, 0)
    up = after(up, sums[2])
    up = lax.all_to_all(up, ADP, split_axis=1, concat_axis=0, tiled=True)
    up_other = lax.ppermute(up, "rep", [(i, i ^ 1) for i in range(lax.axis_size("rep"))])

    own, sent, low = project(places, out_first - len(blocks), blocks, *weights, (*sums, slot))

    low = (low + shift(low, "core", 1)).astype(jnp.bfloat16)
    received = shift(sent, "core", 1)
    if sides == 2:
        low = low + shift(low, "y", 1)
    low, received, up_other = lax.optimization_barrier((low, received, up_other))
    low = sum([shift(low, "z", k) for k in range(1, layers)], low)

    query = make_query(half.astype(jnp.int32).reshape(1), own, received, low, slot, up, up_other)
    output_weight_other = shift(after(output_weight, query), "core", 1)
    query_local = lax.all_to_all(query, ADP, split_axis=0, concat_axis=1, tiled=True)

    context = attention(
        query_local, cache_length, key_cache, value_cache, new_token_key, new_token_value
    )
    context = jnp.swapaxes(context.reshape(context.shape[0], -1, depth), 0, 1)
    context = lax.all_to_all(context, ADP, split_axis=0, concat_axis=0, tiled=True)
    context = context.reshape(rows, depth)
    context_other = shift(context, "core", 1)

    made = {}
    for first, count in ((0, 1), (1, len(out_keys) - 1)):
        outs = output_partial(
            places,
            out_first + first,
            count,
            context,
            context_other,
            output_weight,
            output_weight_other,
            width,
        )
        made.update(zip(out_keys[first : first + count], outs))
    other_side = {k: shift(made[k, 1], "y", 1) for k in out_order if sides == 2}
    parts = [None] * layers
    for k in out_order:
        parts[k] = after(made[k, 0], made[out_keys[-1]]).astype(jnp.float32)
        if sides == 2:
            parts[k] = parts[k] + other_side[k].astype(jnp.float32)
    return scatter_layers(parts).astype(jnp.bfloat16)


def solution(mesh):
    reps, adp = mesh.shape["rep"], mesh.shape["adp"]
    sides = 2 if adp == 16 else 1
    mesh = Mesh(mesh.devices.reshape(reps, adp // (2 * sides), sides, 2), ("rep",) + ADP)
    in_specs = (
        P("rep", ADP),
        P("rep", None),
        P(),
        P(("rep",) + ADP),
        P(None, ADP),
        P(ADP, None, None),
        P(ADP, None, None),
        P(None, ("rep",) + ADP, None, None),
        P(None, ("rep",) + ADP, None, None),
        P(("rep",) + ADP, None),
        P(("rep",) + ADP, None),
        P(ADP, None),
    )
    return jax.shard_map(
        shards, mesh=mesh, in_specs=in_specs, out_specs=P("rep", ADP), check_vma=False
    )
```

```python
import jax
import jax.numpy as jnp
from jax import lax
from jax.experimental import pallas as pl
from jax.experimental.pallas import tpu as pltpu
from jax.sharding import Mesh
from jax.sharding import PartitionSpec as P

HEADS = 64
HEAD_DIM = 128
ADP = ("z", "y", "core")
GATHERED = ((0, 0), (0, 1), (3, 0), (1, 0), (3, 1), (1, 1), (2, 0), (2, 1))
NT = (((1,), (1,)), ((), ()))
VMEM_LIMIT = 56 << 20
QUICK = pl.CostEstimate(flops=1, bytes_accessed=1, transcendentals=0)


def project_kernel(places, first, count, *refs):
    blocks, w_own, w_other, a_own, a_other = (refs[i * count : (i + 1) * count] for i in range(5))
    ins, outs = refs[5 * count : -3], refs[-3:]
    first_core = places[0] % 2 == 0
    sums = [ref[...] for ref in ins[:3]]
    for i in range(count):
        x = blocks[i][...]
        own, other = a_own[i][0], a_other[i][0]
        pair = jnp.concatenate(
            [jnp.where(first_core, own, other), jnp.where(first_core, other, own)], axis=0
        )
        parts = (
            jnp.dot(x, w_own[i][...], preferred_element_type=jnp.float32),
            jnp.dot(x, w_other[i][...], preferred_element_type=jnp.float32),
            lax.dot_general(x, pair, NT, preferred_element_type=jnp.float32),
        )
        sums = [total + part for total, part in zip(sums, parts)] if sums else parts
    outs[0][...], outs[1][...] = sums[:2]
    low = sums[2]
    if ins:
        slot = ins[3][...]
        rank = low.shape[1] // 2
        mine = places[0] - places[0] % 2
        low = jnp.where(slot == mine, low[:, :rank], 0.0) + jnp.where(
            slot == mine + 1, low[:, rank:], 0.0
        )
        half = low.shape[0] // 2
        low = jnp.concatenate([low[:half], low[half:]], axis=1)
    outs[2][...] = low


def project(places, first, blocks, weight, weight_other, down, down_other, rest):
    count = len(blocks)
    rows, width = blocks[0].shape
    cols, rank = weight.shape[1], down.shape[1]
    flat = lambda shape: pl.BlockSpec(shape, lambda j, p: (0, 0))
    low_rows = rows // 2 if rest else rows
    shapes = [(rows, cols), (rows, cols), (low_rows, 2 * rank)]
    weights = [pl.BlockSpec((width, cols), lambda j, p, i=i: (p[first + i], 0)) for i in range(count)]
    maps = [
        pl.BlockSpec((1, rank, width), lambda j, p, i=i: (0, 0, p[first + i])) for i in range(count)
    ]

    def kernel(places, *refs):
        project_kernel(places, first, count, *refs)

    return pl.pallas_call(
        kernel,
        grid_spec=pltpu.PrefetchScalarGridSpec(
            num_scalar_prefetch=1,
            grid=(1,),
            in_specs=[flat((rows, width))] * count
            + weights * 2
            + maps * 2
            + [flat(array.shape) for array in rest],
            out_specs=[flat(shape) for shape in shapes],
        ),
        out_shape=[jax.ShapeDtypeStruct(shape, jnp.float32) for shape in shapes],
        compiler_params=pltpu.CompilerParams(vmem_limit_bytes=VMEM_LIMIT),
        cost_estimate=QUICK,
    )(
        places,
        *blocks,
        *[weight] * count,
        *[weight_other] * count,
        *[down] * count,
        *[down_other] * count,
        *rest,
    )


def query_kernel(half, own, received, low, slot, up_own, up_other, out):
    step = pl.program_id(0)
    lanes = low.shape[1]
    rank = lanes // 2
    part = rank // 2
    depth = up_own.shape[0]
    shape = (lanes, depth)
    lane = lax.broadcasted_iota(jnp.int32, shape, 1) % part
    row = lax.broadcasted_iota(jnp.int32, shape, 0)
    owner = lax.broadcasted_iota(jnp.int32, (own.shape[0], depth), 1) // part
    live = slot[...] == owner
    total = own[...] + received[...]
    for h, up in ((half[0], up_own), (1 - half[0], up_other)):
        copies = (row == lane + rank * step + part * h).astype(jnp.bfloat16)
        spread = jnp.dot(low[...], copies, preferred_element_type=jnp.float32)
        spread = jnp.where(live, spread, 0.0).astype(jnp.bfloat16)
        total += jnp.dot(spread, up[...], preferred_element_type=jnp.float32)
    out[...] = (total * HEAD_DIM ** (-0.5)).astype(out.dtype)


def make_query(half, own, received, low, slot, up_own, up_other):
    rows, cols = own.shape
    tile = rows // 2
    depth = up_own.shape[0]
    by_rows = lambda width: pl.BlockSpec((tile, width), lambda j, h: (j, 0))
    whole = lambda array: pl.BlockSpec(array.shape, lambda j, h: (0, 0))
    return pl.pallas_call(
        query_kernel,
        grid_spec=pltpu.PrefetchScalarGridSpec(
            num_scalar_prefetch=1,
            grid=(2,),
            in_specs=[
                by_rows(cols),
                by_rows(received.shape[1]),
                whole(low),
                by_rows(1),
                whole(up_own),
                whole(up_other),
            ],
            out_specs=by_rows(cols),
        ),
        out_shape=jax.ShapeDtypeStruct((rows, cols), jnp.bfloat16),
        compiler_params=pltpu.CompilerParams(vmem_limit_bytes=VMEM_LIMIT),
        cost_estimate=QUICK,
    )(half, own, received, low, slot, up_own, up_other)


def output_kernel(places, count, own, other, *refs):
    for w_own, w_other, out in zip(refs[:count], refs[count : 2 * count], refs[2 * count :]):
        total = jnp.dot(own[...], w_own[...], preferred_element_type=jnp.float32)
        total += jnp.dot(other[...], w_other[...], preferred_element_type=jnp.float32)
        out[...] = total.astype(out.dtype)


def output_partial(places, first, count, own, other, weight, weight_other, width):
    rows, depth = own.shape
    tile = width // 2 if width % 256 == 0 else width
    steps = width // tile
    whole = pl.BlockSpec((rows, depth), lambda j, p: (0, 0))
    weights = [
        pl.BlockSpec((depth, tile), lambda j, p, i=i: (0, p[first + i] * steps + j))
        for i in range(count)
    ]

    def kernel(places, *refs):
        output_kernel(places, count, *refs)

    return pl.pallas_call(
        kernel,
        grid_spec=pltpu.PrefetchScalarGridSpec(
            num_scalar_prefetch=1,
            grid=(steps,),
            in_specs=[whole, whole] + weights * 2,
            out_specs=[pl.BlockSpec((rows, tile), lambda j, p: (0, j))] * count,
        ),
        out_shape=[jax.ShapeDtypeStruct((rows, width), jnp.bfloat16)] * count,
        compiler_params=pltpu.CompilerParams(vmem_limit_bytes=VMEM_LIMIT),
        cost_estimate=QUICK,
    )(places, own, other, *[weight] * count, *[weight_other] * count)


def attention(query, cache_length, key_cache, value_cache, k_new, v_new):
    local_reqs = query.shape[0]
    kv_count, _, span, dim = key_cache.shape
    group = HEADS // kv_count
    query = query.reshape(local_reqs, kv_count, group, dim)
    k_new = k_new.reshape(local_reqs, kv_count, dim)
    v_new = v_new.reshape(local_reqs, kv_count, dim)
    live = (jnp.arange(span)[None, :] < cache_length[:, None])[None, :, None, :]
    scores = jnp.einsum("rkge,krje->krgj", query, key_cache, preferred_element_type=jnp.float32)
    fresh = jnp.einsum("rkge,rke->krg", query, k_new, preferred_element_type=jnp.float32)
    scores = jnp.where(live, scores, -jnp.inf)
    top = jnp.maximum(jnp.max(scores, axis=3), fresh)
    expd = jnp.where(live, jnp.exp(scores - top[:, :, :, None]), 0.0)
    expf = jnp.exp(fresh - top)
    total = jnp.sum(expd, axis=3) + expf
    probs = (expd / total[:, :, :, None]).astype(jnp.bfloat16)
    probf = (expf / total).astype(jnp.bfloat16)
    context = jnp.einsum("krgj,krje->rkge", probs, value_cache, preferred_element_type=jnp.float32)
    fresh_part = jnp.einsum("krg,rke->rkge", probf.astype(jnp.float32), v_new.astype(jnp.float32))
    return (context + fresh_part).astype(jnp.bfloat16).reshape(local_reqs, HEADS * dim)


def shift(value, axis, by):
    size = lax.axis_size(axis)
    return lax.ppermute(value, axis, [(i, (i + by) % size) for i in range(size)])


def after(value, *others):
    return lax.optimization_barrier((value, *others))[0]


def gathered_chips():
    layers, sides = lax.axis_size("z"), lax.axis_size("y")
    z, y = lax.axis_index("z"), lax.axis_index("y")
    steps = GATHERED
    if layers != 4 or sides != 2:
        steps = [(-k, side) for k in range(layers) for side in range(sides)]
    return [((z + k) % layers) * sides + (y + side) % sides for k, side in steps]


def gather_features(tokens, down_other, up, begin):
    layers, sides = lax.axis_size("z"), lax.axis_size("y")
    z = lax.axis_index("z")
    if layers != 4 or sides != 2:
        blocks = [shift(tokens, "z", k) if k else tokens for k in range(layers)]
        blocks = [[block, shift(block, "y", 1)][:sides] for block in blocks]
        blocks = [block for pair in blocks for block in pair]
        return begin(blocks[:-1]), blocks[-1:], up
    side = shift(tokens, "y", 1)
    below, above = shift(tokens, "z", 1), shift(tokens, "z", 3)
    below, side, _ = lax.optimization_barrier((below, side, down_other))
    below_side = shift(below, "y", 1)
    from_below = lax.ppermute(below, "z", [(1, 2), (2, 3)])
    above_side = shift(above, "y", 1)
    from_above = lax.ppermute(above, "z", [(2, 1), (1, 0)])
    sums = begin([tokens, side, below, above])
    two = jnp.where(z >= 2, from_below, from_above)
    two, _, up, sums = lax.optimization_barrier((two, below_side, up, sums))
    return sums, [below_side, above_side, two, shift(two, "y", 1)], up


def scatter_layers(parts):
    layers = lax.axis_size("z")
    wide = lambda value: value.astype(jnp.float32)
    narrow = lambda value: value.astype(jnp.bfloat16)
    if layers != 4:
        return sum([wide(shift(narrow(parts[k]), "z", k)) for k in range(1, layers)], parts[0])
    two = narrow(parts[2])
    up = lax.ppermute(two, "z", [(0, 1), (1, 2)])
    down = lax.ppermute(two, "z", [(3, 2), (2, 1)])
    above = shift(narrow(parts[1] + wide(up)), "z", 1)
    below = shift(narrow(parts[3] + wide(down)), "z", 3)
    return parts[0] + wide(above) + wide(below)


def shards(
    tokens,
    request_adapter,
    adapter_storage_slot,
    cache_length,
    query_weight,
    adapter_down_maps,
    adapter_up_maps,
    key_cache,
    value_cache,
    new_token_key,
    new_token_value,
    output_weight,
):
    layers, sides = lax.axis_size("z"), lax.axis_size("y")
    z, y, core = lax.axis_index("z"), lax.axis_index("y"), lax.axis_index("core")
    rows, width = tokens.shape
    total_adapters = adapter_storage_slot.shape[0]
    rank = adapter_down_maps.shape[2]
    depth = output_weight.shape[0]
    chips_of = lambda layer: [
        (layer % layers) * sides + (y + side) % sides for side in range(sides)
    ]

    down = jnp.swapaxes(adapter_down_maps, 1, 2)
    down_other = shift(down, "core", 1)
    query_weight_other = shift(query_weight, "core", 1)

    ids = request_adapter[:, 0]
    numbers = jnp.arange(total_adapters, dtype=jnp.int32)
    slot = jnp.sum(
        jnp.where(ids[:, None] == numbers[None, :], adapter_storage_slot[None, :], 0), axis=1
    )[:, None]

    out_order = [2, 1, 3, 0] if layers == 4 else list(range(1, layers)) + [0]
    out_keys = [(k, side) for k in out_order for side in reversed(range(sides))]
    chips = gathered_chips()
    out_first = len(chips)
    chips += [chips_of(z + k)[side] for k, side in out_keys]
    places = jnp.stack([2 * chip + core for chip in chips]).astype(jnp.int32)

    weights = query_weight, query_weight_other, down, down_other
    half = lax.axis_index("rep") % 2
    up = jnp.swapaxes(adapter_up_maps, 1, 2)[0]
    up = lax.dynamic_slice_in_dim(up, half * (rank // 2), rank // 2, 0)
    up = lax.all_to_all(up, ADP, split_axis=1, concat_axis=0, tiled=True)
    sums, blocks, up = gather_features(
        tokens, down_other, up, lambda blocks: project(places, 0, blocks, *weights, ())
    )
    up_other = lax.ppermute(up, "rep", [(i, i ^ 1) for i in range(lax.axis_size("rep"))])

    own, sent, low = project(places, out_first - len(blocks), blocks, *weights, (*sums, slot))

    low = (low + shift(low, "core", 1)).astype(jnp.bfloat16)
    received = shift(sent, "core", 1)
    if sides == 2:
        low = low + shift(low, "y", 1)
    low, received, up_other = lax.optimization_barrier((low, received, up_other))
    low = sum([shift(low, "z", k) for k in range(1, layers)], low)

    query = make_query(half.astype(jnp.int32).reshape(1), own, received, low, slot, up, up_other)
    output_weight_other = shift(after(output_weight, query), "core", 1)
    query_local = lax.all_to_all(query, ADP, split_axis=0, concat_axis=1, tiled=True)

    context = attention(
        query_local, cache_length, key_cache, value_cache, new_token_key, new_token_value
    )
    context = jnp.swapaxes(context.reshape(context.shape[0], -1, depth), 0, 1)
    context = lax.all_to_all(context, ADP, split_axis=0, concat_axis=0, tiled=True)
    context = context.reshape(rows, depth)
    context_other = shift(context, "core", 1)

    made = {}
    for first, count in ((0, 1), (1, len(out_keys) - 1)):
        outs = output_partial(
            places,
            out_first + first,
            count,
            context,
            context_other,
            output_weight,
            output_weight_other,
            width,
        )
        made.update(zip(out_keys[first : first + count], outs))
    other_side = {k: shift(made[k, 1], "y", 1) for k in out_order if sides == 2}
    parts = [None] * layers
    for k in out_order:
        parts[k] = after(made[k, 0], made[out_keys[-1]]).astype(jnp.float32)
        if sides == 2:
            parts[k] = parts[k] + other_side[k].astype(jnp.float32)
    return scatter_layers(parts).astype(jnp.bfloat16)


def solution(mesh):
    reps, adp = mesh.shape["rep"], mesh.shape["adp"]
    sides = 2 if adp == 16 else 1
    mesh = Mesh(mesh.devices.reshape(reps, adp // (2 * sides), sides, 2), ("rep",) + ADP)
    in_specs = (
        P("rep", ADP),
        P("rep", None),
        P(),
        P(("rep",) + ADP),
        P(None, ADP),
        P(ADP, None, None),
        P(ADP, None, None),
        P(None, ("rep",) + ADP, None, None),
        P(None, ("rep",) + ADP, None, None),
        P(("rep",) + ADP, None),
        P(("rep",) + ADP, None),
        P(ADP, None),
    )
    return jax.shard_map(
        shards, mesh=mesh, in_specs=in_specs, out_specs=P("rep", ADP), check_vma=False
    )
```

```python
import jax
import jax.numpy as jnp
from jax import lax
from jax.experimental import pallas as pl
from jax.experimental.pallas import tpu as pltpu
from jax.sharding import Mesh
from jax.sharding import PartitionSpec as P

HEADS = 64
HEAD_DIM = 128
ADP = ("z", "y", "core")
GATHERED = ((0, 0), (0, 1), (3, 0), (1, 0), (3, 1), (1, 1), (2, 0), (2, 1))
NT = (((1,), (1,)), ((), ()))
VMEM_LIMIT = 56 << 20
QUICK = pl.CostEstimate(flops=1, bytes_accessed=1, transcendentals=0)


def project_kernel(places, first, count, *refs):
    blocks, w_own, w_other, a_own, a_other = (refs[i * count : (i + 1) * count] for i in range(5))
    ins, outs = refs[5 * count : -3], refs[-3:]
    first_core = places[0] % 2 == 0
    sums = [ref[...] for ref in ins[:3]]
    for i in range(count):
        x = blocks[i][...]
        own, other = a_own[i][0], a_other[i][0]
        pair = jnp.concatenate(
            [jnp.where(first_core, own, other), jnp.where(first_core, other, own)], axis=0
        )
        parts = (
            jnp.dot(x, w_own[i][...], preferred_element_type=jnp.float32),
            jnp.dot(x, w_other[i][...], preferred_element_type=jnp.float32),
            lax.dot_general(x, pair, NT, preferred_element_type=jnp.float32),
        )
        sums = [total + part for total, part in zip(sums, parts)] if sums else parts
    outs[0][...], outs[1][...] = sums[:2]
    low = sums[2]
    if ins:
        slot = ins[3][...]
        rank = low.shape[1] // 2
        mine = places[0] - places[0] % 2
        low = jnp.where(slot == mine, low[:, :rank], 0.0) + jnp.where(
            slot == mine + 1, low[:, rank:], 0.0
        )
        half = low.shape[0] // 2
        low = jnp.concatenate([low[:half], low[half:]], axis=1)
    outs[2][...] = low


def project(places, first, blocks, weight, weight_other, down, down_other, rest):
    count = len(blocks)
    rows, width = blocks[0].shape
    cols, rank = weight.shape[1], down.shape[1]
    flat = lambda shape: pl.BlockSpec(shape, lambda j, p: (0, 0))
    low_rows = rows // 2 if rest else rows
    shapes = [(rows, cols), (rows, cols), (low_rows, 2 * rank)]
    weights = [pl.BlockSpec((width, cols), lambda j, p, i=i: (p[first + i], 0)) for i in range(count)]
    maps = [
        pl.BlockSpec((1, rank, width), lambda j, p, i=i: (0, 0, p[first + i])) for i in range(count)
    ]

    def kernel(places, *refs):
        project_kernel(places, first, count, *refs)

    return pl.pallas_call(
        kernel,
        grid_spec=pltpu.PrefetchScalarGridSpec(
            num_scalar_prefetch=1,
            grid=(1,),
            in_specs=[flat((rows, width))] * count
            + weights * 2
            + maps * 2
            + [flat(array.shape) for array in rest],
            out_specs=[flat(shape) for shape in shapes],
        ),
        out_shape=[jax.ShapeDtypeStruct(shape, jnp.float32) for shape in shapes],
        compiler_params=pltpu.CompilerParams(vmem_limit_bytes=VMEM_LIMIT),
        cost_estimate=QUICK,
    )(
        places,
        *blocks,
        *[weight] * count,
        *[weight_other] * count,
        *[down] * count,
        *[down_other] * count,
        *rest,
    )


def query_kernel(half, own, received, low, slot, up_own, up_other, out):
    step = pl.program_id(0)
    lanes = low.shape[1]
    rank = lanes // 2
    part = rank // 2
    depth = up_own.shape[0]
    shape = (lanes, depth)
    lane = lax.broadcasted_iota(jnp.int32, shape, 1) % part
    row = lax.broadcasted_iota(jnp.int32, shape, 0)
    owner = lax.broadcasted_iota(jnp.int32, (own.shape[0], depth), 1) // part
    live = slot[...] == owner
    total = own[...] + received[...]
    for h, up in ((half[0], up_own), (1 - half[0], up_other)):
        copies = (row == lane + rank * step + part * h).astype(jnp.bfloat16)
        spread = jnp.dot(low[...], copies, preferred_element_type=jnp.float32)
        spread = jnp.where(live, spread, 0.0).astype(jnp.bfloat16)
        total += jnp.dot(spread, up[...], preferred_element_type=jnp.float32)
    out[...] = (total * HEAD_DIM ** (-0.5)).astype(out.dtype)


def make_query(half, own, received, low, slot, up_own, up_other):
    rows, cols = own.shape
    tile = rows // 2
    depth = up_own.shape[0]
    by_rows = lambda width: pl.BlockSpec((tile, width), lambda j, h: (j, 0))
    whole = lambda array: pl.BlockSpec(array.shape, lambda j, h: (0, 0))
    return pl.pallas_call(
        query_kernel,
        grid_spec=pltpu.PrefetchScalarGridSpec(
            num_scalar_prefetch=1,
            grid=(2,),
            in_specs=[
                by_rows(cols),
                by_rows(received.shape[1]),
                whole(low),
                by_rows(1),
                whole(up_own),
                whole(up_other),
            ],
            out_specs=by_rows(cols),
        ),
        out_shape=jax.ShapeDtypeStruct((rows, cols), jnp.bfloat16),
        compiler_params=pltpu.CompilerParams(vmem_limit_bytes=VMEM_LIMIT),
        cost_estimate=QUICK,
    )(half, own, received, low, slot, up_own, up_other)


def output_kernel(places, count, own, other, *refs):
    for w_own, w_other, out in zip(refs[:count], refs[count : 2 * count], refs[2 * count :]):
        total = jnp.dot(own[...], w_own[...], preferred_element_type=jnp.float32)
        total += jnp.dot(other[...], w_other[...], preferred_element_type=jnp.float32)
        out[...] = total.astype(out.dtype)


def output_partial(places, first, count, own, other, weight, weight_other, width):
    rows, depth = own.shape
    tile = width // 2 if width % 256 == 0 else width
    steps = width // tile
    whole = pl.BlockSpec((rows, depth), lambda j, p: (0, 0))
    weights = [
        pl.BlockSpec((depth, tile), lambda j, p, i=i: (0, p[first + i] * steps + j))
        for i in range(count)
    ]

    def kernel(places, *refs):
        output_kernel(places, count, *refs)

    return pl.pallas_call(
        kernel,
        grid_spec=pltpu.PrefetchScalarGridSpec(
            num_scalar_prefetch=1,
            grid=(steps,),
            in_specs=[whole, whole] + weights * 2,
            out_specs=[pl.BlockSpec((rows, tile), lambda j, p: (0, j))] * count,
        ),
        out_shape=[jax.ShapeDtypeStruct((rows, width), jnp.bfloat16)] * count,
        compiler_params=pltpu.CompilerParams(vmem_limit_bytes=VMEM_LIMIT),
        cost_estimate=QUICK,
    )(places, own, other, *[weight] * count, *[weight_other] * count)


def attention(query, cache_length, key_cache, value_cache, k_new, v_new):
    local_reqs = query.shape[0]
    kv_count, _, span, dim = key_cache.shape
    group = HEADS // kv_count
    query = query.reshape(local_reqs, kv_count, group, dim)
    k_new = k_new.reshape(local_reqs, kv_count, dim)
    v_new = v_new.reshape(local_reqs, kv_count, dim)
    live = (jnp.arange(span)[None, :] < cache_length[:, None])[None, :, None, :]
    scores = jnp.einsum("rkge,krje->krgj", query, key_cache, preferred_element_type=jnp.float32)
    fresh = jnp.einsum("rkge,rke->krg", query, k_new, preferred_element_type=jnp.float32)
    scores = jnp.where(live, scores, -jnp.inf)
    top = jnp.maximum(jnp.max(scores, axis=3), fresh)
    expd = jnp.where(live, jnp.exp(scores - top[:, :, :, None]), 0.0)
    expf = jnp.exp(fresh - top)
    total = jnp.sum(expd, axis=3) + expf
    probs = (expd / total[:, :, :, None]).astype(jnp.bfloat16)
    probf = (expf / total).astype(jnp.bfloat16)
    context = jnp.einsum("krgj,krje->rkge", probs, value_cache, preferred_element_type=jnp.float32)
    fresh_part = jnp.einsum("krg,rke->rkge", probf.astype(jnp.float32), v_new.astype(jnp.float32))
    return (context + fresh_part).astype(jnp.bfloat16).reshape(local_reqs, HEADS * dim)


def shift(value, axis, by):
    size = lax.axis_size(axis)
    return lax.ppermute(value, axis, [(i, (i + by) % size) for i in range(size)])


def after(value, *others):
    return lax.optimization_barrier((value, *others))[0]


def gathered_chips():
    layers, sides = lax.axis_size("z"), lax.axis_size("y")
    z, y = lax.axis_index("z"), lax.axis_index("y")
    steps = GATHERED
    if layers != 4 or sides != 2:
        steps = [(-k, side) for k in range(layers) for side in range(sides)]
    return [((z + k) % layers) * sides + (y + side) % sides for k, side in steps]


def gather_features(tokens, down_other, up, begin):
    layers, sides = lax.axis_size("z"), lax.axis_size("y")
    z = lax.axis_index("z")
    if layers != 4 or sides != 2:
        blocks = [shift(tokens, "z", k) if k else tokens for k in range(layers)]
        blocks = [[block, shift(block, "y", 1)][:sides] for block in blocks]
        blocks = [block for pair in blocks for block in pair]
        return begin(blocks[:-1]), blocks[-1:], up
    side = shift(tokens, "y", 1)
    below, above = shift(tokens, "z", 1), shift(tokens, "z", 3)
    below, side, _ = lax.optimization_barrier((below, side, down_other))
    below_side = shift(below, "y", 1)
    from_below = lax.ppermute(below, "z", [(1, 2), (2, 3)])
    above_side = shift(above, "y", 1)
    from_above = lax.ppermute(above, "z", [(2, 1), (1, 0)])
    sums = begin([tokens, side, below, above])
    from_below, from_above, _, up, sums = lax.optimization_barrier(
        (from_below, from_above, below_side, up, sums)
    )
    two = jnp.where(z >= 2, from_below, from_above)
    return sums, [below_side, above_side, two, shift(two, "y", 1)], up


def scatter_layers(parts):
    layers = lax.axis_size("z")
    wide = lambda value: value.astype(jnp.float32)
    narrow = lambda value: value.astype(jnp.bfloat16)
    if layers != 4:
        return sum([wide(shift(narrow(parts[k]), "z", k)) for k in range(1, layers)], parts[0])
    two = narrow(parts[2])
    up = lax.ppermute(two, "z", [(0, 1), (1, 2)])
    down = lax.ppermute(two, "z", [(3, 2), (2, 1)])
    above = shift(narrow(parts[1] + wide(up)), "z", 1)
    below = shift(narrow(parts[3] + wide(down)), "z", 3)
    return parts[0] + wide(above) + wide(below)


def shards(
    tokens,
    request_adapter,
    adapter_storage_slot,
    cache_length,
    query_weight,
    adapter_down_maps,
    adapter_up_maps,
    key_cache,
    value_cache,
    new_token_key,
    new_token_value,
    output_weight,
):
    layers, sides = lax.axis_size("z"), lax.axis_size("y")
    z, y, core = lax.axis_index("z"), lax.axis_index("y"), lax.axis_index("core")
    rows, width = tokens.shape
    total_adapters = adapter_storage_slot.shape[0]
    rank = adapter_down_maps.shape[2]
    depth = output_weight.shape[0]
    chips_of = lambda layer: [
        (layer % layers) * sides + (y + side) % sides for side in range(sides)
    ]

    down = jnp.swapaxes(adapter_down_maps, 1, 2)
    down_other = shift(down, "core", 1)
    query_weight_other = shift(query_weight, "core", 1)

    ids = request_adapter[:, 0]
    numbers = jnp.arange(total_adapters, dtype=jnp.int32)
    slot = jnp.sum(
        jnp.where(ids[:, None] == numbers[None, :], adapter_storage_slot[None, :], 0), axis=1
    )[:, None]

    out_order = [2, 1, 3, 0] if layers == 4 else list(range(1, layers)) + [0]
    out_keys = [(k, side) for k in out_order for side in reversed(range(sides))]
    chips = gathered_chips()
    out_first = len(chips)
    chips += [chips_of(z + k)[side] for k, side in out_keys]
    places = jnp.stack([2 * chip + core for chip in chips]).astype(jnp.int32)

    weights = query_weight, query_weight_other, down, down_other
    half = lax.axis_index("rep") % 2
    up = jnp.swapaxes(adapter_up_maps, 1, 2)[0]
    up = lax.dynamic_slice_in_dim(up, half * (rank // 2), rank // 2, 0)
    up = lax.all_to_all(up, ADP, split_axis=1, concat_axis=0, tiled=True)
    sums, blocks, up = gather_features(
        tokens, down_other, up, lambda blocks: project(places, 0, blocks, *weights, ())
    )
    up_other = lax.ppermute(up, "rep", [(i, i ^ 1) for i in range(lax.axis_size("rep"))])

    own, sent, low = project(
        after(places, up_other), out_first - len(blocks), blocks, *weights, (*sums, slot)
    )

    low = (low + shift(low, "core", 1)).astype(jnp.bfloat16)
    received = shift(sent, "core", 1)
    if sides == 2:
        low = low + shift(low, "y", 1)
    low, received = lax.optimization_barrier((low, received))
    low = sum([shift(low, "z", k) for k in range(1, layers)], low)

    query = make_query(half.astype(jnp.int32).reshape(1), own, received, low, slot, up, up_other)
    output_weight_other = shift(after(output_weight, query), "core", 1)
    query_local = lax.all_to_all(query, ADP, split_axis=0, concat_axis=1, tiled=True)

    context = attention(
        query_local, cache_length, key_cache, value_cache, new_token_key, new_token_value
    )
    context = jnp.swapaxes(context.reshape(context.shape[0], -1, depth), 0, 1)
    context = lax.all_to_all(context, ADP, split_axis=0, concat_axis=0, tiled=True)
    context = context.reshape(rows, depth)
    context_other = shift(context, "core", 1)

    made = {}
    for first, count in ((0, 1), (1, len(out_keys) - 1)):
        outs = output_partial(
            places,
            out_first + first,
            count,
            context,
            context_other,
            output_weight,
            output_weight_other,
            width,
        )
        made.update(zip(out_keys[first : first + count], outs))
    other_side = {k: shift(made[k, 1], "y", 1) for k in out_order if sides == 2}
    parts = [None] * layers
    for k in out_order:
        parts[k] = after(made[k, 0], made[out_keys[-1]]).astype(jnp.float32)
        if sides == 2:
            parts[k] = parts[k] + other_side[k].astype(jnp.float32)
    return scatter_layers(parts).astype(jnp.bfloat16)


def solution(mesh):
    reps, adp = mesh.shape["rep"], mesh.shape["adp"]
    sides = 2 if adp == 16 else 1
    mesh = Mesh(mesh.devices.reshape(reps, adp // (2 * sides), sides, 2), ("rep",) + ADP)
    in_specs = (
        P("rep", ADP),
        P("rep", None),
        P(),
        P(("rep",) + ADP),
        P(None, ADP),
        P(ADP, None, None),
        P(ADP, None, None),
        P(None, ("rep",) + ADP, None, None),
        P(None, ("rep",) + ADP, None, None),
        P(("rep",) + ADP, None),
        P(("rep",) + ADP, None),
        P(ADP, None),
    )
    return jax.shard_map(
        shards, mesh=mesh, in_specs=in_specs, out_specs=P("rep", ADP), check_vma=False
    )
```

```python
import jax
import jax.numpy as jnp
from jax import lax
from jax.experimental import pallas as pl
from jax.experimental.pallas import tpu as pltpu
from jax.sharding import Mesh
from jax.sharding import PartitionSpec as P

HEADS = 64
HEAD_DIM = 128
ADP = ("z", "y", "core")
GATHERED = ((0, 0), (0, 1), (3, 0), (1, 0), (3, 1), (1, 1), (2, 0), (2, 1))
NT = (((1,), (1,)), ((), ()))
VMEM_LIMIT = 56 << 20
QUICK = pl.CostEstimate(flops=1, bytes_accessed=1, transcendentals=0)


def project_kernel(places, first, count, *refs):
    blocks, w_own, w_other, a_own, a_other = (refs[i * count : (i + 1) * count] for i in range(5))
    ins, outs = refs[5 * count : -3], refs[-3:]
    first_core = places[0] % 2 == 0
    sums = [ref[...] for ref in ins[:3]]
    for i in range(count):
        x = blocks[i][...]
        own, other = a_own[i][0], a_other[i][0]
        pair = jnp.concatenate(
            [jnp.where(first_core, own, other), jnp.where(first_core, other, own)], axis=0
        )
        parts = (
            jnp.dot(x, w_own[i][...], preferred_element_type=jnp.float32),
            jnp.dot(x, w_other[i][...], preferred_element_type=jnp.float32),
            lax.dot_general(x, pair, NT, preferred_element_type=jnp.float32),
        )
        sums = [total + part for total, part in zip(sums, parts)] if sums else parts
    outs[0][...], outs[1][...] = sums[:2]
    low = sums[2]
    if ins:
        slot = ins[3][...]
        rank = low.shape[1] // 2
        mine = places[0] - places[0] % 2
        low = jnp.where(slot == mine, low[:, :rank], 0.0) + jnp.where(
            slot == mine + 1, low[:, rank:], 0.0
        )
        half = low.shape[0] // 2
        low = jnp.concatenate([low[:half], low[half:]], axis=1)
    outs[2][...] = low


def project(places, first, blocks, weight, weight_other, down, down_other, rest):
    count = len(blocks)
    rows, width = blocks[0].shape
    cols, rank = weight.shape[1], down.shape[1]
    flat = lambda shape: pl.BlockSpec(shape, lambda j, p: (0, 0))
    low_rows = rows // 2 if rest else rows
    shapes = [(rows, cols), (rows, cols), (low_rows, 2 * rank)]
    weights = [pl.BlockSpec((width, cols), lambda j, p, i=i: (p[first + i], 0)) for i in range(count)]
    maps = [
        pl.BlockSpec((1, rank, width), lambda j, p, i=i: (0, 0, p[first + i])) for i in range(count)
    ]

    def kernel(places, *refs):
        project_kernel(places, first, count, *refs)

    return pl.pallas_call(
        kernel,
        grid_spec=pltpu.PrefetchScalarGridSpec(
            num_scalar_prefetch=1,
            grid=(1,),
            in_specs=[flat((rows, width))] * count
            + weights * 2
            + maps * 2
            + [flat(array.shape) for array in rest],
            out_specs=[flat(shape) for shape in shapes],
        ),
        out_shape=[jax.ShapeDtypeStruct(shape, jnp.float32) for shape in shapes],
        compiler_params=pltpu.CompilerParams(vmem_limit_bytes=VMEM_LIMIT),
        cost_estimate=QUICK,
    )(
        places,
        *blocks,
        *[weight] * count,
        *[weight_other] * count,
        *[down] * count,
        *[down_other] * count,
        *rest,
    )


def query_kernel(half, own, received, low, slot, up_own, up_other, out):
    step = pl.program_id(0)
    lanes = low.shape[1]
    rank = lanes // 2
    part = rank // 2
    depth = up_own.shape[0]
    shape = (lanes, depth)
    lane = lax.broadcasted_iota(jnp.int32, shape, 1) % part
    row = lax.broadcasted_iota(jnp.int32, shape, 0)
    owner = lax.broadcasted_iota(jnp.int32, (own.shape[0], depth), 1) // part
    live = slot[...] == owner
    total = own[...] + received[...]
    for h, up in ((half[0], up_own), (1 - half[0], up_other)):
        copies = (row == lane + rank * step + part * h).astype(jnp.bfloat16)
        spread = jnp.dot(low[...], copies, preferred_element_type=jnp.float32)
        spread = jnp.where(live, spread, 0.0).astype(jnp.bfloat16)
        total += jnp.dot(spread, up[...], preferred_element_type=jnp.float32)
    out[...] = (total * HEAD_DIM ** (-0.5)).astype(out.dtype)


def make_query(half, own, received, low, slot, up_own, up_other):
    rows, cols = own.shape
    tile = rows // 2
    depth = up_own.shape[0]
    by_rows = lambda width: pl.BlockSpec((tile, width), lambda j, h: (j, 0))
    whole = lambda array: pl.BlockSpec(array.shape, lambda j, h: (0, 0))
    return pl.pallas_call(
        query_kernel,
        grid_spec=pltpu.PrefetchScalarGridSpec(
            num_scalar_prefetch=1,
            grid=(2,),
            in_specs=[
                by_rows(cols),
                by_rows(received.shape[1]),
                whole(low),
                by_rows(1),
                whole(up_own),
                whole(up_other),
            ],
            out_specs=by_rows(cols),
        ),
        out_shape=jax.ShapeDtypeStruct((rows, cols), jnp.bfloat16),
        compiler_params=pltpu.CompilerParams(vmem_limit_bytes=VMEM_LIMIT),
        cost_estimate=QUICK,
    )(half, own, received, low, slot, up_own, up_other)


def output_kernel(places, count, own, other, *refs):
    for w_own, w_other, out in zip(refs[:count], refs[count : 2 * count], refs[2 * count :]):
        total = jnp.dot(own[...], w_own[...], preferred_element_type=jnp.float32)
        total += jnp.dot(other[...], w_other[...], preferred_element_type=jnp.float32)
        out[...] = total.astype(out.dtype)


def output_partial(places, first, count, own, other, weight, weight_other, width):
    rows, depth = own.shape
    tile = width // 2 if width % 256 == 0 else width
    steps = width // tile
    whole = pl.BlockSpec((rows, depth), lambda j, p: (0, 0))
    weights = [
        pl.BlockSpec((depth, tile), lambda j, p, i=i: (0, p[first + i] * steps + j))
        for i in range(count)
    ]

    def kernel(places, *refs):
        output_kernel(places, count, *refs)

    return pl.pallas_call(
        kernel,
        grid_spec=pltpu.PrefetchScalarGridSpec(
            num_scalar_prefetch=1,
            grid=(steps,),
            in_specs=[whole, whole] + weights * 2,
            out_specs=[pl.BlockSpec((rows, tile), lambda j, p: (0, j))] * count,
        ),
        out_shape=[jax.ShapeDtypeStruct((rows, width), jnp.bfloat16)] * count,
        compiler_params=pltpu.CompilerParams(vmem_limit_bytes=VMEM_LIMIT),
        cost_estimate=QUICK,
    )(places, own, other, *[weight] * count, *[weight_other] * count)


def attention(query, cache_length, key_cache, value_cache, k_new, v_new):
    local_reqs = query.shape[0]
    kv_count, _, span, dim = key_cache.shape
    group = HEADS // kv_count
    query = query.reshape(local_reqs, kv_count, group, dim)
    k_new = k_new.reshape(local_reqs, kv_count, dim)
    v_new = v_new.reshape(local_reqs, kv_count, dim)
    live = (jnp.arange(span)[None, :] < cache_length[:, None])[None, :, None, :]
    scores = jnp.einsum("rkge,krje->krgj", query, key_cache, preferred_element_type=jnp.float32)
    fresh = jnp.einsum("rkge,rke->krg", query, k_new, preferred_element_type=jnp.float32)
    scores = jnp.where(live, scores, -jnp.inf)
    top = jnp.maximum(jnp.max(scores, axis=3), fresh)
    expd = jnp.where(live, jnp.exp(scores - top[:, :, :, None]), 0.0)
    expf = jnp.exp(fresh - top)
    total = jnp.sum(expd, axis=3) + expf
    probs = (expd / total[:, :, :, None]).astype(jnp.bfloat16)
    probf = (expf / total).astype(jnp.bfloat16)
    context = jnp.einsum("krgj,krje->rkge", probs, value_cache, preferred_element_type=jnp.float32)
    fresh_part = jnp.einsum("krg,rke->rkge", probf.astype(jnp.float32), v_new.astype(jnp.float32))
    return (context + fresh_part).astype(jnp.bfloat16).reshape(local_reqs, HEADS * dim)


def shift(value, axis, by):
    size = lax.axis_size(axis)
    return lax.ppermute(value, axis, [(i, (i + by) % size) for i in range(size)])


def after(value, *others):
    return lax.optimization_barrier((value, *others))[0]


def gathered_chips():
    layers, sides = lax.axis_size("z"), lax.axis_size("y")
    z, y = lax.axis_index("z"), lax.axis_index("y")
    steps = GATHERED
    if layers != 4 or sides != 2:
        steps = [(-k, side) for k in range(layers) for side in range(sides)]
    return [((z + k) % layers) * sides + (y + side) % sides for k, side in steps]


def gather_features(tokens, down_other, up, begin):
    layers, sides = lax.axis_size("z"), lax.axis_size("y")
    z = lax.axis_index("z")
    if layers != 4 or sides != 2:
        blocks = [shift(tokens, "z", k) if k else tokens for k in range(layers)]
        blocks = [[block, shift(block, "y", 1)][:sides] for block in blocks]
        blocks = [block for pair in blocks for block in pair]
        return begin(blocks[:-1]), blocks[-1:], up
    side = shift(tokens, "y", 1)
    below, above = shift(tokens, "z", 1), shift(tokens, "z", 3)
    below, side, _ = lax.optimization_barrier((below, side, down_other))
    below_side = shift(below, "y", 1)
    from_below = lax.ppermute(below, "z", [(1, 2), (2, 3)])
    above_side = shift(above, "y", 1)
    from_above = lax.ppermute(above, "z", [(2, 1), (1, 0)])
    sums = begin([tokens, side, below, above])
    two = jnp.where(z >= 2, from_below, from_above)
    two, _, up = lax.optimization_barrier((two, below_side, up))
    return sums, [below_side, above_side, two, shift(two, "y", 1)], up


def scatter_layers(parts):
    layers = lax.axis_size("z")
    wide = lambda value: value.astype(jnp.float32)
    narrow = lambda value: value.astype(jnp.bfloat16)
    if layers != 4:
        return sum([wide(shift(narrow(parts[k]), "z", k)) for k in range(1, layers)], parts[0])
    two = narrow(parts[2])
    up = lax.ppermute(two, "z", [(0, 1), (1, 2)])
    down = lax.ppermute(two, "z", [(3, 2), (2, 1)])
    above = shift(narrow(parts[1] + wide(up)), "z", 1)
    below = shift(narrow(parts[3] + wide(down)), "z", 3)
    return parts[0] + wide(above) + wide(below)


def shards(
    tokens,
    request_adapter,
    adapter_storage_slot,
    cache_length,
    query_weight,
    adapter_down_maps,
    adapter_up_maps,
    key_cache,
    value_cache,
    new_token_key,
    new_token_value,
    output_weight,
):
    layers, sides = lax.axis_size("z"), lax.axis_size("y")
    z, y, core = lax.axis_index("z"), lax.axis_index("y"), lax.axis_index("core")
    rows, width = tokens.shape
    total_adapters = adapter_storage_slot.shape[0]
    rank = adapter_down_maps.shape[2]
    depth = output_weight.shape[0]
    chips_of = lambda layer: [
        (layer % layers) * sides + (y + side) % sides for side in range(sides)
    ]

    down = jnp.swapaxes(adapter_down_maps, 1, 2)
    down_other = shift(down, "core", 1)
    query_weight_other = shift(query_weight, "core", 1)

    ids = request_adapter[:, 0]
    numbers = jnp.arange(total_adapters, dtype=jnp.int32)
    slot = jnp.sum(
        jnp.where(ids[:, None] == numbers[None, :], adapter_storage_slot[None, :], 0), axis=1
    )[:, None]

    out_order = [2, 1, 3, 0] if layers == 4 else list(range(1, layers)) + [0]
    out_keys = [(k, side) for k in out_order for side in reversed(range(sides))]
    chips = gathered_chips()
    out_first = len(chips)
    chips += [chips_of(z + k)[side] for k, side in out_keys]
    places = jnp.stack([2 * chip + core for chip in chips]).astype(jnp.int32)

    weights = query_weight, query_weight_other, down, down_other
    half = lax.axis_index("rep") % 2
    up = jnp.swapaxes(adapter_up_maps, 1, 2)[0]
    up = lax.dynamic_slice_in_dim(up, half * (rank // 2), rank // 2, 0)
    up = lax.all_to_all(up, ADP, split_axis=1, concat_axis=0, tiled=True)
    sums, blocks, up = gather_features(
        tokens, down_other, up, lambda blocks: project(places, 0, blocks, *weights, ())
    )
    up_other = lax.ppermute(up, "rep", [(i, i ^ 1) for i in range(lax.axis_size("rep"))])

    own, sent, low = project(places, out_first - len(blocks), blocks, *weights, (*sums, slot))

    low = (low + shift(low, "core", 1)).astype(jnp.bfloat16)
    received = shift(sent, "core", 1)
    low, up_other = lax.optimization_barrier((low, up_other))
    if sides == 2:
        low = low + shift(low, "y", 1)
    low, received = lax.optimization_barrier((low, received))
    low = sum([shift(low, "z", k) for k in range(1, layers)], low)

    query = make_query(half.astype(jnp.int32).reshape(1), own, received, low, slot, up, up_other)
    output_weight_other = shift(after(output_weight, query), "core", 1)
    query_local = lax.all_to_all(query, ADP, split_axis=0, concat_axis=1, tiled=True)

    context = attention(
        query_local, cache_length, key_cache, value_cache, new_token_key, new_token_value
    )
    context = jnp.swapaxes(context.reshape(context.shape[0], -1, depth), 0, 1)
    context = lax.all_to_all(context, ADP, split_axis=0, concat_axis=0, tiled=True)
    context = context.reshape(rows, depth)
    context_other = shift(context, "core", 1)

    made = {}
    for first, count in ((0, 1), (1, len(out_keys) - 1)):
        outs = output_partial(
            places,
            out_first + first,
            count,
            context,
            context_other,
            output_weight,
            output_weight_other,
            width,
        )
        made.update(zip(out_keys[first : first + count], outs))
    other_side = {k: shift(made[k, 1], "y", 1) for k in out_order if sides == 2}
    parts = [None] * layers
    for k in out_order:
        parts[k] = after(made[k, 0], made[out_keys[-1]]).astype(jnp.float32)
        if sides == 2:
            parts[k] = parts[k] + other_side[k].astype(jnp.float32)
    return scatter_layers(parts).astype(jnp.bfloat16)


def solution(mesh):
    reps, adp = mesh.shape["rep"], mesh.shape["adp"]
    sides = 2 if adp == 16 else 1
    mesh = Mesh(mesh.devices.reshape(reps, adp // (2 * sides), sides, 2), ("rep",) + ADP)
    in_specs = (
        P("rep", ADP),
        P("rep", None),
        P(),
        P(("rep",) + ADP),
        P(None, ADP),
        P(ADP, None, None),
        P(ADP, None, None),
        P(None, ("rep",) + ADP, None, None),
        P(None, ("rep",) + ADP, None, None),
        P(("rep",) + ADP, None),
        P(("rep",) + ADP, None),
        P(ADP, None),
    )
    return jax.shard_map(
        shards, mesh=mesh, in_specs=in_specs, out_specs=P("rep", ADP), check_vma=False
    )
```

```python
import jax
import jax.numpy as jnp
from jax import lax
from jax.experimental import pallas as pl
from jax.experimental.pallas import tpu as pltpu
from jax.sharding import Mesh
from jax.sharding import PartitionSpec as P

HEADS = 64
HEAD_DIM = 128
ADP = ("z", "y", "core")
GATHERED = ((0, 0), (0, 1), (3, 0), (1, 0), (3, 1), (1, 1), (2, 0), (2, 1))
NT = (((1,), (1,)), ((), ()))
VMEM_LIMIT = 56 << 20
QUICK = pl.CostEstimate(flops=1, bytes_accessed=1, transcendentals=0)


def project_kernel(places, first, count, *refs):
    blocks, w_own, w_other, a_own, a_other = (refs[i * count : (i + 1) * count] for i in range(5))
    ins, outs = refs[5 * count : -3], refs[-3:]
    first_core = places[0] % 2 == 0
    sums = [ref[...] for ref in ins[:3]]
    for i in range(count):
        x = blocks[i][...]
        own, other = a_own[i][0], a_other[i][0]
        pair = jnp.concatenate(
            [jnp.where(first_core, own, other), jnp.where(first_core, other, own)], axis=0
        )
        parts = (
            jnp.dot(x, w_own[i][...], preferred_element_type=jnp.float32),
            jnp.dot(x, w_other[i][...], preferred_element_type=jnp.float32),
            lax.dot_general(x, pair, NT, preferred_element_type=jnp.float32),
        )
        sums = [total + part for total, part in zip(sums, parts)] if sums else parts
    outs[0][...], outs[1][...] = sums[:2]
    low = sums[2]
    if ins:
        slot = ins[3][...]
        rank = low.shape[1] // 2
        mine = places[0] - places[0] % 2
        low = jnp.where(slot == mine, low[:, :rank], 0.0) + jnp.where(
            slot == mine + 1, low[:, rank:], 0.0
        )
        half = low.shape[0] // 2
        low = jnp.concatenate([low[:half], low[half:]], axis=1)
    outs[2][...] = low


def project(places, first, blocks, weight, weight_other, down, down_other, rest):
    count = len(blocks)
    rows, width = blocks[0].shape
    cols, rank = weight.shape[1], down.shape[1]
    flat = lambda shape: pl.BlockSpec(shape, lambda j, p: (0, 0))
    low_rows = rows // 2 if rest else rows
    shapes = [(rows, cols), (rows, cols), (low_rows, 2 * rank)]
    weights = [pl.BlockSpec((width, cols), lambda j, p, i=i: (p[first + i], 0)) for i in range(count)]
    maps = [
        pl.BlockSpec((1, rank, width), lambda j, p, i=i: (0, 0, p[first + i])) for i in range(count)
    ]

    def kernel(places, *refs):
        project_kernel(places, first, count, *refs)

    return pl.pallas_call(
        kernel,
        grid_spec=pltpu.PrefetchScalarGridSpec(
            num_scalar_prefetch=1,
            grid=(1,),
            in_specs=[flat((rows, width))] * count
            + weights * 2
            + maps * 2
            + [flat(array.shape) for array in rest],
            out_specs=[flat(shape) for shape in shapes],
        ),
        out_shape=[jax.ShapeDtypeStruct(shape, jnp.float32) for shape in shapes],
        compiler_params=pltpu.CompilerParams(vmem_limit_bytes=VMEM_LIMIT),
        cost_estimate=QUICK,
    )(
        places,
        *blocks,
        *[weight] * count,
        *[weight_other] * count,
        *[down] * count,
        *[down_other] * count,
        *rest,
    )


def query_kernel(half, own, received, low, slot, up_own, up_other, out):
    step = pl.program_id(0)
    lanes = low.shape[1]
    rank = lanes // 2
    part = rank // 2
    depth = up_own.shape[0]
    shape = (lanes, depth)
    lane = lax.broadcasted_iota(jnp.int32, shape, 1) % part
    row = lax.broadcasted_iota(jnp.int32, shape, 0)
    owner = lax.broadcasted_iota(jnp.int32, (own.shape[0], depth), 1) // part
    live = slot[...] == owner
    total = own[...] + received[...]
    for h, up in ((half[0], up_own), (1 - half[0], up_other)):
        copies = (row == lane + rank * step + part * h).astype(jnp.bfloat16)
        spread = jnp.dot(low[...], copies, preferred_element_type=jnp.float32)
        spread = jnp.where(live, spread, 0.0).astype(jnp.bfloat16)
        total += jnp.dot(spread, up[...], preferred_element_type=jnp.float32)
    out[...] = (total * HEAD_DIM ** (-0.5)).astype(out.dtype)


def make_query(half, own, received, low, slot, up_own, up_other):
    rows, cols = own.shape
    tile = rows // 2
    depth = up_own.shape[0]
    by_rows = lambda width: pl.BlockSpec((tile, width), lambda j, h: (j, 0))
    whole = lambda array: pl.BlockSpec(array.shape, lambda j, h: (0, 0))
    return pl.pallas_call(
        query_kernel,
        grid_spec=pltpu.PrefetchScalarGridSpec(
            num_scalar_prefetch=1,
            grid=(2,),
            in_specs=[
                by_rows(cols),
                by_rows(received.shape[1]),
                whole(low),
                by_rows(1),
                whole(up_own),
                whole(up_other),
            ],
            out_specs=by_rows(cols),
        ),
        out_shape=jax.ShapeDtypeStruct((rows, cols), jnp.bfloat16),
        compiler_params=pltpu.CompilerParams(vmem_limit_bytes=VMEM_LIMIT),
        cost_estimate=QUICK,
    )(half, own, received, low, slot, up_own, up_other)


def output_kernel(places, count, own, other, *refs):
    for w_own, w_other, out in zip(refs[:count], refs[count : 2 * count], refs[2 * count :]):
        total = jnp.dot(own[...], w_own[...], preferred_element_type=jnp.float32)
        total += jnp.dot(other[...], w_other[...], preferred_element_type=jnp.float32)
        out[...] = total.astype(out.dtype)


def output_partial(places, first, count, own, other, weight, weight_other, width):
    rows, depth = own.shape
    tile = width // 2 if width % 256 == 0 else width
    steps = width // tile
    whole = pl.BlockSpec((rows, depth), lambda j, p: (0, 0))
    weights = [
        pl.BlockSpec((depth, tile), lambda j, p, i=i: (0, p[first + i] * steps + j))
        for i in range(count)
    ]

    def kernel(places, *refs):
        output_kernel(places, count, *refs)

    return pl.pallas_call(
        kernel,
        grid_spec=pltpu.PrefetchScalarGridSpec(
            num_scalar_prefetch=1,
            grid=(steps,),
            in_specs=[whole, whole] + weights * 2,
            out_specs=[pl.BlockSpec((rows, tile), lambda j, p: (0, j))] * count,
        ),
        out_shape=[jax.ShapeDtypeStruct((rows, width), jnp.bfloat16)] * count,
        compiler_params=pltpu.CompilerParams(vmem_limit_bytes=VMEM_LIMIT),
        cost_estimate=QUICK,
    )(places, own, other, *[weight] * count, *[weight_other] * count)


def attention_kernel(query, lengths, keys, values, k_new, v_new, out):
    pairs, span = keys.shape[1] // 2, keys.shape[2]
    group = out.shape[1] // keys.shape[1]
    columns = query.shape[1]
    half = columns // 2
    q = query[0]
    first = lax.broadcasted_iota(jnp.int32, q.shape, 0) < half
    zero = jnp.zeros_like(q)
    apart = jnp.concatenate([jnp.where(first, q, zero), jnp.where(first, zero, q)], axis=1)
    beside = [
        jnp.concatenate([keys[0, 2 * p], keys[0, 2 * p + 1]], axis=1) for p in range(pairs)
    ]
    every = lax.dot_general(
        jnp.concatenate(beside, axis=0), apart, NT, preferred_element_type=jnp.float32
    )
    column = lax.broadcasted_iota(jnp.int32, (span, columns), 1)
    pair = column % half // group
    scores = every[:span]
    for p in range(1, pairs):
        scores = jnp.where(pair == p, every[p * span : (p + 1) * span], scores)

    request = 2 * pair + column // half
    row = lax.broadcasted_iota(jnp.int32, (span, columns), 0)
    fresh = lax.dot_general(k_new[...], q, NT, preferred_element_type=jnp.float32)
    fresh = jnp.sum(jnp.where(row == request, fresh, 0.0), axis=0, keepdims=True)
    live = row < lengths[...]
    top = jnp.maximum(
        jnp.max(jnp.where(live, scores, -jnp.inf), axis=0, keepdims=True), fresh
    )
    expd = jnp.where(live, jnp.exp(scores - top), 0.0)
    expf = jnp.exp(fresh - top)
    total = jnp.sum(expd, axis=0, keepdims=True) + expf
    probs = jnp.transpose(expd / total)
    probf = jnp.transpose(jnp.where(row == request, expf / total, 0.0)).astype(jnp.bfloat16)
    fresh_part = jnp.dot(probf, v_new[...], preferred_element_type=jnp.float32)

    none = jnp.zeros((group, span), jnp.float32)
    wide = 2 if pairs % 2 == 0 else 1
    for p in range(0, pairs, wide):
        left, right = [], []
        for i in range(p, p + wide):
            left += [
                jnp.concatenate([probs[i * group : (i + 1) * group], none], axis=1),
                jnp.concatenate([none, probs[half + i * group : half + (i + 1) * group]], axis=1),
            ]
            right.append(values[0, 2 * i : 2 * i + 2].reshape(2 * span, values.shape[3]))
        both = jnp.dot(
            jnp.concatenate(left, axis=0).astype(jnp.bfloat16),
            jnp.concatenate(right, axis=1),
            preferred_element_type=jnp.float32,
        )
        for i in range(p, p + wide):
            j = i - p
            context = both[2 * group * j : 2 * group * (j + 1), 128 * j : 128 * (j + 1)]
            context += jnp.concatenate(
                [
                    fresh_part[i * group : (i + 1) * group],
                    fresh_part[half + i * group : half + (i + 1) * group],
                ],
                axis=0,
            )
            out[0, 2 * group * i : 2 * group * (i + 1), :] = context.astype(out.dtype)


def attention(query, cache_length, key_cache, value_cache, k_new, v_new):
    devices, requests, width = query.shape
    kv_count, _, span, dim = key_cache.shape
    group = HEADS // kv_count
    pairs = requests // 2
    half = 128
    query = query.reshape(kv_count, devices // kv_count, pairs, 2, width // dim, dim)
    query = query.transpose(0, 3, 2, 1, 4, 5).reshape(kv_count, 2, pairs * group, dim)
    query = jnp.pad(query, ((0, 0), (0, 0), (0, half - pairs * group), (0, 0)))
    query = query.reshape(kv_count, 2 * half, dim)
    lengths = jnp.repeat(cache_length.reshape(pairs, 2).T, group, axis=1)
    lengths = jnp.pad(lengths, ((0, 0), (0, half - pairs * group))).reshape(1, 2 * half)
    k_new, v_new = (jnp.pad(new, ((0, span - requests), (0, 0))) for new in (k_new, v_new))
    cache_spec = pl.BlockSpec((1, requests, span, dim), lambda g: (g, 0, 0, 0))
    new_spec = pl.BlockSpec((span, dim), lambda g: (0, g))
    context = pl.pallas_call(
        attention_kernel,
        grid=(kv_count,),
        in_specs=[
            pl.BlockSpec((1, 2 * half, dim), lambda g: (g, 0, 0)),
            pl.BlockSpec((1, 2 * half), lambda g: (0, 0)),
            cache_spec,
            cache_spec,
            new_spec,
            new_spec,
        ],
        out_specs=pl.BlockSpec((1, requests * group, dim), lambda g: (g, 0, 0)),
        out_shape=jax.ShapeDtypeStruct((kv_count, requests * group, dim), jnp.bfloat16),
        compiler_params=pltpu.CompilerParams(vmem_limit_bytes=VMEM_LIMIT),
        cost_estimate=QUICK,
    )(query, lengths, key_cache, value_cache, k_new, v_new)
    context = context.reshape(kv_count, requests, devices // kv_count, width // dim, dim)
    return context.transpose(0, 2, 1, 3, 4).reshape(devices, requests, width)


def shift(value, axis, by):
    size = lax.axis_size(axis)
    return lax.ppermute(value, axis, [(i, (i + by) % size) for i in range(size)])


def after(value, *others):
    return lax.optimization_barrier((value, *others))[0]


def gathered_chips():
    layers, sides = lax.axis_size("z"), lax.axis_size("y")
    z, y = lax.axis_index("z"), lax.axis_index("y")
    steps = GATHERED
    if layers != 4 or sides != 2:
        steps = [(-k, side) for k in range(layers) for side in range(sides)]
    return [((z + k) % layers) * sides + (y + side) % sides for k, side in steps]


def gather_features(tokens, down_other, up, begin):
    layers, sides = lax.axis_size("z"), lax.axis_size("y")
    z = lax.axis_index("z")
    if layers != 4 or sides != 2:
        blocks = [shift(tokens, "z", k) if k else tokens for k in range(layers)]
        blocks = [[block, shift(block, "y", 1)][:sides] for block in blocks]
        blocks = [block for pair in blocks for block in pair]
        return begin(blocks[:-1]), blocks[-1:], up
    side = shift(tokens, "y", 1)
    below, above = shift(tokens, "z", 1), shift(tokens, "z", 3)
    below, side, _ = lax.optimization_barrier((below, side, down_other))
    below_side = shift(below, "y", 1)
    from_below = lax.ppermute(below, "z", [(1, 2), (2, 3)])
    above_side = shift(above, "y", 1)
    from_above = lax.ppermute(above, "z", [(2, 1), (1, 0)])
    sums = begin([tokens, side, below, above])
    two = jnp.where(z >= 2, from_below, from_above)
    two, _, up = lax.optimization_barrier((two, below_side, up))
    return sums, [below_side, above_side, two, shift(two, "y", 1)], up


def scatter_layers(parts):
    layers = lax.axis_size("z")
    wide = lambda value: value.astype(jnp.float32)
    narrow = lambda value: value.astype(jnp.bfloat16)
    if layers != 4:
        return sum([wide(shift(narrow(parts[k]), "z", k)) for k in range(1, layers)], parts[0])
    two = narrow(parts[2])
    up = lax.ppermute(two, "z", [(0, 1), (1, 2)])
    down = lax.ppermute(two, "z", [(3, 2), (2, 1)])
    above = shift(narrow(parts[1] + wide(up)), "z", 1)
    below = shift(narrow(parts[3] + wide(down)), "z", 3)
    return parts[0] + wide(above) + wide(below)


def shards(
    tokens,
    request_adapter,
    adapter_storage_slot,
    cache_length,
    query_weight,
    adapter_down_maps,
    adapter_up_maps,
    key_cache,
    value_cache,
    new_token_key,
    new_token_value,
    output_weight,
):
    layers, sides = lax.axis_size("z"), lax.axis_size("y")
    z, y, core = lax.axis_index("z"), lax.axis_index("y"), lax.axis_index("core")
    rows, width = tokens.shape
    total_adapters = adapter_storage_slot.shape[0]
    rank = adapter_down_maps.shape[2]
    depth = output_weight.shape[0]
    chips_of = lambda layer: [
        (layer % layers) * sides + (y + side) % sides for side in range(sides)
    ]

    down = jnp.swapaxes(adapter_down_maps, 1, 2)
    down_other = shift(down, "core", 1)
    query_weight_other = shift(query_weight, "core", 1)

    ids = request_adapter[:, 0]
    numbers = jnp.arange(total_adapters, dtype=jnp.int32)
    slot = jnp.sum(
        jnp.where(ids[:, None] == numbers[None, :], adapter_storage_slot[None, :], 0), axis=1
    )[:, None]

    out_order = [2, 1, 3, 0] if layers == 4 else list(range(1, layers)) + [0]
    out_keys = [(k, side) for k in out_order for side in reversed(range(sides))]
    chips = gathered_chips()
    out_first = len(chips)
    chips += [chips_of(z + k)[side] for k, side in out_keys]
    places = jnp.stack([2 * chip + core for chip in chips]).astype(jnp.int32)

    weights = query_weight, query_weight_other, down, down_other
    half = lax.axis_index("rep") % 2
    up = jnp.swapaxes(adapter_up_maps, 1, 2)[0]
    up = lax.dynamic_slice_in_dim(up, half * (rank // 2), rank // 2, 0)
    up = lax.all_to_all(up, ADP, split_axis=1, concat_axis=0, tiled=True)
    sums, blocks, up = gather_features(
        tokens, down_other, up, lambda blocks: project(places, 0, blocks, *weights, ())
    )
    up_other = lax.ppermute(up, "rep", [(i, i ^ 1) for i in range(lax.axis_size("rep"))])

    own, sent, low = project(
        after(places, up_other), out_first - len(blocks), blocks, *weights, (*sums, slot)
    )

    low = (low + shift(low, "core", 1)).astype(jnp.bfloat16)
    received = shift(sent, "core", 1)
    if sides == 2:
        low = low + shift(low, "y", 1)
    low, received = lax.optimization_barrier((low, received))
    low = sum([shift(low, "z", k) for k in range(1, layers)], low)

    query = make_query(half.astype(jnp.int32).reshape(1), own, received, low, slot, up, up_other)
    output_weight_other = shift(after(output_weight, query), "core", 1)
    query = query.reshape(rows // cache_length.shape[0], cache_length.shape[0], depth)
    query = lax.all_to_all(query, ADP, split_axis=0, concat_axis=0, tiled=True)
    context = attention(
        query, cache_length, key_cache, value_cache, new_token_key, new_token_value
    )
    context = lax.all_to_all(context, ADP, split_axis=0, concat_axis=0, tiled=True)
    context = context.reshape(rows, depth)
    context_other = shift(context, "core", 1)

    made = {}
    for first, count in ((0, 1), (1, len(out_keys) - 1)):
        outs = output_partial(
            places,
            out_first + first,
            count,
            context,
            context_other,
            output_weight,
            output_weight_other,
            width,
        )
        made.update(zip(out_keys[first : first + count], outs))
    other_side = {k: shift(made[k, 1], "y", 1) for k in out_order if sides == 2}
    parts = [None] * layers
    for k in out_order:
        parts[k] = after(made[k, 0], made[out_keys[-1]]).astype(jnp.float32)
        if sides == 2:
            parts[k] = parts[k] + other_side[k].astype(jnp.float32)
    return scatter_layers(parts).astype(jnp.bfloat16)


def solution(mesh):
    reps, adp = mesh.shape["rep"], mesh.shape["adp"]
    sides = 2 if adp == 16 else 1
    mesh = Mesh(mesh.devices.reshape(reps, adp // (2 * sides), sides, 2), ("rep",) + ADP)
    in_specs = (
        P("rep", ADP),
        P("rep", None),
        P(),
        P(("rep",) + ADP),
        P(None, ADP),
        P(ADP, None, None),
        P(ADP, None, None),
        P(None, ("rep",) + ADP, None, None),
        P(None, ("rep",) + ADP, None, None),
        P(("rep",) + ADP, None),
        P(("rep",) + ADP, None),
        P(ADP, None),
    )
    return jax.shard_map(
        shards, mesh=mesh, in_specs=in_specs, out_specs=P("rep", ADP), check_vma=False
    )
```

```python
import jax
import jax.numpy as jnp
from jax import lax
from jax.experimental import pallas as pl
from jax.experimental.pallas import tpu as pltpu
from jax.sharding import Mesh
from jax.sharding import PartitionSpec as P

HEADS = 64
HEAD_DIM = 128
ADP = ("z", "y", "core")
GATHERED = ((0, 0), (0, 1), (3, 0), (1, 0), (3, 1), (1, 1), (2, 0), (2, 1))
NT = (((1,), (1,)), ((), ()))
VMEM_LIMIT = 56 << 20
QUICK = pl.CostEstimate(flops=1, bytes_accessed=1, transcendentals=0)


def project_kernel(places, first, count, *refs):
    blocks, w_own, w_other, a_own, a_other = (refs[i * count : (i + 1) * count] for i in range(5))
    ins, outs = refs[5 * count : -3], refs[-3:]
    first_core = places[0] % 2 == 0
    sums = [ref[...] for ref in ins[:3]]
    for i in range(count):
        x = blocks[i][...]
        own, other = a_own[i][0], a_other[i][0]
        pair = jnp.concatenate(
            [jnp.where(first_core, own, other), jnp.where(first_core, other, own)], axis=0
        )
        parts = (
            jnp.dot(x, w_own[i][...], preferred_element_type=jnp.float32),
            jnp.dot(x, w_other[i][...], preferred_element_type=jnp.float32),
            lax.dot_general(x, pair, NT, preferred_element_type=jnp.float32),
        )
        sums = [total + part for total, part in zip(sums, parts)] if sums else parts
    outs[0][...], outs[1][...] = sums[:2]
    low = sums[2]
    if ins:
        slot = ins[3][...]
        rank = low.shape[1] // 2
        mine = places[0] - places[0] % 2
        low = jnp.where(slot == mine, low[:, :rank], 0.0) + jnp.where(
            slot == mine + 1, low[:, rank:], 0.0
        )
        half = low.shape[0] // 2
        low = jnp.concatenate([low[:half], low[half:]], axis=1)
    outs[2][...] = low


def project(places, first, blocks, weight, weight_other, down, down_other, rest):
    count = len(blocks)
    rows, width = blocks[0].shape
    cols, rank = weight.shape[1], down.shape[1]
    flat = lambda shape: pl.BlockSpec(shape, lambda j, p: (0, 0))
    low_rows = rows // 2 if rest else rows
    shapes = [(rows, cols), (rows, cols), (low_rows, 2 * rank)]
    weights = [pl.BlockSpec((width, cols), lambda j, p, i=i: (p[first + i], 0)) for i in range(count)]
    maps = [
        pl.BlockSpec((1, rank, width), lambda j, p, i=i: (0, 0, p[first + i])) for i in range(count)
    ]

    def kernel(places, *refs):
        project_kernel(places, first, count, *refs)

    return pl.pallas_call(
        kernel,
        grid_spec=pltpu.PrefetchScalarGridSpec(
            num_scalar_prefetch=1,
            grid=(1,),
            in_specs=[flat((rows, width))] * count
            + weights * 2
            + maps * 2
            + [flat(array.shape) for array in rest],
            out_specs=[flat(shape) for shape in shapes],
        ),
        out_shape=[jax.ShapeDtypeStruct(shape, jnp.float32) for shape in shapes],
        compiler_params=pltpu.CompilerParams(vmem_limit_bytes=VMEM_LIMIT),
        cost_estimate=pl.CostEstimate(
            flops=4 * count * rows * width * (cols + rank),
            bytes_accessed=2 * count * width * (rows + 2 * cols) + 8 * rows * cols,
            transcendentals=0,
        ),
    )(
        places,
        *blocks,
        *[weight] * count,
        *[weight_other] * count,
        *[down] * count,
        *[down_other] * count,
        *rest,
    )


def query_kernel(half, own, received, low, slot, up_own, up_other, out):
    step = pl.program_id(0)
    lanes = low.shape[1]
    rank = lanes // 2
    part = rank // 2
    depth = up_own.shape[0]
    shape = (lanes, depth)
    lane = lax.broadcasted_iota(jnp.int32, shape, 1) % part
    row = lax.broadcasted_iota(jnp.int32, shape, 0)
    owner = lax.broadcasted_iota(jnp.int32, (own.shape[0], depth), 1) // part
    live = slot[...] == owner
    total = own[...] + received[...]
    for h, up in ((half[0], up_own), (1 - half[0], up_other)):
        copies = (row == lane + rank * step + part * h).astype(jnp.bfloat16)
        spread = jnp.dot(low[...], copies, preferred_element_type=jnp.float32)
        spread = jnp.where(live, spread, 0.0).astype(jnp.bfloat16)
        total += jnp.dot(spread, up[...], preferred_element_type=jnp.float32)
    out[...] = (total * HEAD_DIM ** (-0.5)).astype(out.dtype)


def make_query(half, own, received, low, slot, up_own, up_other):
    rows, cols = own.shape
    tile = rows // 2
    depth = up_own.shape[0]
    by_rows = lambda width: pl.BlockSpec((tile, width), lambda j, h: (j, 0))
    whole = lambda array: pl.BlockSpec(array.shape, lambda j, h: (0, 0))
    return pl.pallas_call(
        query_kernel,
        grid_spec=pltpu.PrefetchScalarGridSpec(
            num_scalar_prefetch=1,
            grid=(2,),
            in_specs=[
                by_rows(cols),
                by_rows(received.shape[1]),
                whole(low),
                by_rows(1),
                whole(up_own),
                whole(up_other),
            ],
            out_specs=by_rows(cols),
        ),
        out_shape=jax.ShapeDtypeStruct((rows, cols), jnp.bfloat16),
        compiler_params=pltpu.CompilerParams(vmem_limit_bytes=VMEM_LIMIT),
        cost_estimate=QUICK,
    )(half, own, received, low, slot, up_own, up_other)


def output_kernel(places, count, own, other, *refs):
    for w_own, w_other, out in zip(refs[:count], refs[count : 2 * count], refs[2 * count :]):
        total = jnp.dot(own[...], w_own[...], preferred_element_type=jnp.float32)
        total += jnp.dot(other[...], w_other[...], preferred_element_type=jnp.float32)
        out[...] = total.astype(out.dtype)


def output_partial(places, first, count, own, other, weight, weight_other, width):
    rows, depth = own.shape
    tile = width // 2 if width % 256 == 0 else width
    steps = width // tile
    whole = pl.BlockSpec((rows, depth), lambda j, p: (0, 0))
    weights = [
        pl.BlockSpec((depth, tile), lambda j, p, i=i: (0, p[first + i] * steps + j))
        for i in range(count)
    ]

    def kernel(places, *refs):
        output_kernel(places, count, *refs)

    return pl.pallas_call(
        kernel,
        grid_spec=pltpu.PrefetchScalarGridSpec(
            num_scalar_prefetch=1,
            grid=(steps,),
            in_specs=[whole, whole] + weights * 2,
            out_specs=[pl.BlockSpec((rows, tile), lambda j, p: (0, j))] * count,
        ),
        out_shape=[jax.ShapeDtypeStruct((rows, width), jnp.bfloat16)] * count,
        compiler_params=pltpu.CompilerParams(vmem_limit_bytes=VMEM_LIMIT),
        cost_estimate=QUICK,
    )(places, own, other, *[weight] * count, *[weight_other] * count)


def attention(query, cache_length, key_cache, value_cache, k_new, v_new):
    local_reqs = query.shape[0]
    kv_count, _, span, dim = key_cache.shape
    group = HEADS // kv_count
    query = query.reshape(local_reqs, kv_count, group, dim)
    k_new = k_new.reshape(local_reqs, kv_count, dim)
    v_new = v_new.reshape(local_reqs, kv_count, dim)
    live = (jnp.arange(span)[None, :] < cache_length[:, None])[None, :, None, :]
    scores = jnp.einsum("rkge,krje->krgj", query, key_cache, preferred_element_type=jnp.float32)
    fresh = jnp.einsum("rkge,rke->krg", query, k_new, preferred_element_type=jnp.float32)
    scores = jnp.where(live, scores, -jnp.inf)
    top = jnp.maximum(jnp.max(scores, axis=3), fresh)
    expd = jnp.where(live, jnp.exp(scores - top[:, :, :, None]), 0.0)
    expf = jnp.exp(fresh - top)
    total = jnp.sum(expd, axis=3) + expf
    probs = (expd / total[:, :, :, None]).astype(jnp.bfloat16)
    probf = (expf / total).astype(jnp.bfloat16)
    context = jnp.einsum("krgj,krje->rkge", probs, value_cache, preferred_element_type=jnp.float32)
    fresh_part = jnp.einsum("krg,rke->rkge", probf.astype(jnp.float32), v_new.astype(jnp.float32))
    return (context + fresh_part).astype(jnp.bfloat16).reshape(local_reqs, HEADS * dim)


def shift(value, axis, by):
    size = lax.axis_size(axis)
    return lax.ppermute(value, axis, [(i, (i + by) % size) for i in range(size)])


def after(value, *others):
    return lax.optimization_barrier((value, *others))[0]


def gathered_chips():
    layers, sides = lax.axis_size("z"), lax.axis_size("y")
    z, y = lax.axis_index("z"), lax.axis_index("y")
    steps = GATHERED
    if layers != 4 or sides != 2:
        steps = [(-k, side) for k in range(layers) for side in range(sides)]
    return [((z + k) % layers) * sides + (y + side) % sides for k, side in steps]


def gather_features(tokens, down_other, up, begin):
    layers, sides = lax.axis_size("z"), lax.axis_size("y")
    z = lax.axis_index("z")
    if layers != 4 or sides != 2:
        blocks = [shift(tokens, "z", k) if k else tokens for k in range(layers)]
        blocks = [[block, shift(block, "y", 1)][:sides] for block in blocks]
        blocks = [block for pair in blocks for block in pair]
        return begin(blocks[:-1]), blocks[-1:], up
    side = shift(tokens, "y", 1)
    below, above = shift(tokens, "z", 1), shift(tokens, "z", 3)
    below, side, _ = lax.optimization_barrier((below, side, down_other))
    below_side = shift(below, "y", 1)
    from_below = lax.ppermute(below, "z", [(1, 2), (2, 3)])
    above_side = shift(above, "y", 1)
    from_above = lax.ppermute(above, "z", [(2, 1), (1, 0)])
    sums = begin([tokens, side, below, above])
    two = jnp.where(z >= 2, from_below, from_above)
    two, _, up = lax.optimization_barrier((two, below_side, up))
    return sums, [below_side, above_side, two, shift(two, "y", 1)], up


def scatter_layers(parts):
    layers = lax.axis_size("z")
    wide = lambda value: value.astype(jnp.float32)
    narrow = lambda value: value.astype(jnp.bfloat16)
    if layers != 4:
        return sum([wide(shift(narrow(parts[k]), "z", k)) for k in range(1, layers)], parts[0])
    two = narrow(parts[2])
    up = lax.ppermute(two, "z", [(0, 1), (1, 2)])
    down = lax.ppermute(two, "z", [(3, 2), (2, 1)])
    above = shift(narrow(parts[1] + wide(up)), "z", 1)
    below = shift(narrow(parts[3] + wide(down)), "z", 3)
    return parts[0] + wide(above) + wide(below)


def shards(
    tokens,
    request_adapter,
    adapter_storage_slot,
    cache_length,
    query_weight,
    adapter_down_maps,
    adapter_up_maps,
    key_cache,
    value_cache,
    new_token_key,
    new_token_value,
    output_weight,
):
    layers, sides = lax.axis_size("z"), lax.axis_size("y")
    z, y, core = lax.axis_index("z"), lax.axis_index("y"), lax.axis_index("core")
    rows, width = tokens.shape
    total_adapters = adapter_storage_slot.shape[0]
    rank = adapter_down_maps.shape[2]
    depth = output_weight.shape[0]
    chips_of = lambda layer: [
        (layer % layers) * sides + (y + side) % sides for side in range(sides)
    ]

    down = jnp.swapaxes(adapter_down_maps, 1, 2)
    down_other = shift(down, "core", 1)
    query_weight_other = shift(query_weight, "core", 1)

    ids = request_adapter[:, 0]
    numbers = jnp.arange(total_adapters, dtype=jnp.int32)
    slot = jnp.sum(
        jnp.where(ids[:, None] == numbers[None, :], adapter_storage_slot[None, :], 0), axis=1
    )[:, None]

    out_order = [2, 1, 3, 0] if layers == 4 else list(range(1, layers)) + [0]
    out_keys = [(k, side) for k in out_order for side in reversed(range(sides))]
    chips = gathered_chips()
    out_first = len(chips)
    chips += [chips_of(z + k)[side] for k, side in out_keys]
    places = jnp.stack([2 * chip + core for chip in chips]).astype(jnp.int32)

    weights = query_weight, query_weight_other, down, down_other
    half = lax.axis_index("rep") % 2
    up = jnp.swapaxes(adapter_up_maps, 1, 2)[0]
    up = lax.dynamic_slice_in_dim(up, half * (rank // 2), rank // 2, 0)
    up = lax.all_to_all(up, ADP, split_axis=1, concat_axis=0, tiled=True)
    sums, blocks, up = gather_features(
        tokens, down_other, up, lambda blocks: project(places, 0, blocks, *weights, ())
    )
    up_other = lax.ppermute(up, "rep", [(i, i ^ 1) for i in range(lax.axis_size("rep"))])

    own, sent, low = project(
        after(places, up_other), out_first - len(blocks), blocks, *weights, (*sums, slot)
    )

    low = (low + shift(low, "core", 1)).astype(jnp.bfloat16)
    received = shift(sent, "core", 1)
    if sides == 2:
        low = low + shift(low, "y", 1)
    low, received = lax.optimization_barrier((low, received))
    low = sum([shift(low, "z", k) for k in range(1, layers)], low)

    query = make_query(half.astype(jnp.int32).reshape(1), own, received, low, slot, up, up_other)
    output_weight_other = shift(after(output_weight, query), "core", 1)
    query_local = lax.all_to_all(query, ADP, split_axis=0, concat_axis=1, tiled=True)

    context = attention(
        query_local, cache_length, key_cache, value_cache, new_token_key, new_token_value
    )
    context = jnp.swapaxes(context.reshape(context.shape[0], -1, depth), 0, 1)
    context = lax.all_to_all(context, ADP, split_axis=0, concat_axis=0, tiled=True)
    context = context.reshape(rows, depth)
    context_other = shift(context, "core", 1)

    made = {}
    for first, count in ((0, 1), (1, len(out_keys) - 1)):
        outs = output_partial(
            places,
            out_first + first,
            count,
            context,
            context_other,
            output_weight,
            output_weight_other,
            width,
        )
        made.update(zip(out_keys[first : first + count], outs))
    other_side = {k: shift(made[k, 1], "y", 1) for k in out_order if sides == 2}
    parts = [None] * layers
    for k in out_order:
        parts[k] = after(made[k, 0], made[out_keys[-1]]).astype(jnp.float32)
        if sides == 2:
            parts[k] = parts[k] + other_side[k].astype(jnp.float32)
    return scatter_layers(parts).astype(jnp.bfloat16)


def solution(mesh):
    reps, adp = mesh.shape["rep"], mesh.shape["adp"]
    sides = 2 if adp == 16 else 1
    mesh = Mesh(mesh.devices.reshape(reps, adp // (2 * sides), sides, 2), ("rep",) + ADP)
    in_specs = (
        P("rep", ADP),
        P("rep", None),
        P(),
        P(("rep",) + ADP),
        P(None, ADP),
        P(ADP, None, None),
        P(ADP, None, None),
        P(None, ("rep",) + ADP, None, None),
        P(None, ("rep",) + ADP, None, None),
        P(("rep",) + ADP, None),
        P(("rep",) + ADP, None),
        P(ADP, None),
    )
    return jax.shard_map(
        shards, mesh=mesh, in_specs=in_specs, out_specs=P("rep", ADP), check_vma=False
    )
```

```python
import jax
import jax.numpy as jnp
from jax import lax
from jax.experimental import pallas as pl
from jax.experimental.pallas import tpu as pltpu
from jax.sharding import Mesh
from jax.sharding import PartitionSpec as P

HEADS = 64
HEAD_DIM = 128
ADP = ("z", "y", "core")
GATHERED = ((0, 0), (0, 1), (3, 0), (1, 0), (3, 1), (1, 1), (2, 0), (2, 1))
NT = (((1,), (1,)), ((), ()))
VMEM_LIMIT = 56 << 20
QUICK = pl.CostEstimate(flops=1, bytes_accessed=1, transcendentals=0)


def project_kernel(places, first, count, *refs):
    blocks, w_own, w_other, a_own, a_other = (refs[i * count : (i + 1) * count] for i in range(5))
    ins, outs = refs[5 * count : -3], refs[-3:]
    first_core = places[0] % 2 == 0
    sums = [ref[...] for ref in ins[:3]]
    for i in range(count):
        x = blocks[i][...]
        own, other = a_own[i][0], a_other[i][0]
        pair = jnp.concatenate(
            [jnp.where(first_core, own, other), jnp.where(first_core, other, own)], axis=0
        )
        parts = (
            jnp.dot(x, w_own[i][...], preferred_element_type=jnp.float32),
            jnp.dot(x, w_other[i][...], preferred_element_type=jnp.float32),
            lax.dot_general(x, pair, NT, preferred_element_type=jnp.float32),
        )
        sums = [total + part for total, part in zip(sums, parts)] if sums else parts
    outs[0][...], outs[1][...] = sums[:2]
    low = sums[2]
    if ins:
        slot = ins[3][...]
        rank = low.shape[1] // 2
        mine = places[0] - places[0] % 2
        low = jnp.where(slot == mine, low[:, :rank], 0.0) + jnp.where(
            slot == mine + 1, low[:, rank:], 0.0
        )
        half = low.shape[0] // 2
        low = jnp.concatenate([low[:half], low[half:]], axis=1)
    outs[2][...] = low


def project(places, first, blocks, weight, weight_other, down, down_other, rest):
    count = len(blocks)
    rows, width = blocks[0].shape
    cols, rank = weight.shape[1], down.shape[1]
    flat = lambda shape: pl.BlockSpec(shape, lambda j, p: (0, 0))
    low_rows = rows // 2 if rest else rows
    shapes = [(rows, cols), (rows, cols), (low_rows, 2 * rank)]
    weights = [pl.BlockSpec((width, cols), lambda j, p, i=i: (p[first + i], 0)) for i in range(count)]
    maps = [
        pl.BlockSpec((1, rank, width), lambda j, p, i=i: (0, 0, p[first + i])) for i in range(count)
    ]

    def kernel(places, *refs):
        project_kernel(places, first, count, *refs)

    return pl.pallas_call(
        kernel,
        grid_spec=pltpu.PrefetchScalarGridSpec(
            num_scalar_prefetch=1,
            grid=(1,),
            in_specs=[flat((rows, width))] * count
            + weights * 2
            + maps * 2
            + [flat(array.shape) for array in rest],
            out_specs=[flat(shape) for shape in shapes],
        ),
        out_shape=[jax.ShapeDtypeStruct(shape, jnp.float32) for shape in shapes],
        compiler_params=pltpu.CompilerParams(vmem_limit_bytes=VMEM_LIMIT),
        cost_estimate=pl.CostEstimate(
            flops=4 * count * rows * width * (cols + rank),
            bytes_accessed=2 * count * width * (rows + 2 * cols) + 8 * rows * cols,
            transcendentals=0,
        ),
    )(
        places,
        *blocks,
        *[weight] * count,
        *[weight_other] * count,
        *[down] * count,
        *[down_other] * count,
        *rest,
    )


def query_kernel(half, own, received, low, slot, up_own, up_other, out):
    step = pl.program_id(0)
    lanes = low.shape[1]
    rank = lanes // 2
    part = rank // 2
    depth = up_own.shape[0]
    shape = (lanes, depth)
    lane = lax.broadcasted_iota(jnp.int32, shape, 1) % part
    row = lax.broadcasted_iota(jnp.int32, shape, 0)
    owner = lax.broadcasted_iota(jnp.int32, (own.shape[0], depth), 1) // part
    live = slot[...] == owner
    total = own[...] + received[...]
    for h, up in ((half[0], up_own), (1 - half[0], up_other)):
        copies = (row == lane + rank * step + part * h).astype(jnp.bfloat16)
        spread = jnp.dot(low[...], copies, preferred_element_type=jnp.float32)
        spread = jnp.where(live, spread, 0.0).astype(jnp.bfloat16)
        total += jnp.dot(spread, up[...], preferred_element_type=jnp.float32)
    out[...] = (total * HEAD_DIM ** (-0.5)).astype(out.dtype)


def make_query(half, own, received, low, slot, up_own, up_other):
    rows, cols = own.shape
    tile = rows // 2
    depth = up_own.shape[0]
    by_rows = lambda width: pl.BlockSpec((tile, width), lambda j, h: (j, 0))
    whole = lambda array: pl.BlockSpec(array.shape, lambda j, h: (0, 0))
    return pl.pallas_call(
        query_kernel,
        grid_spec=pltpu.PrefetchScalarGridSpec(
            num_scalar_prefetch=1,
            grid=(2,),
            in_specs=[
                by_rows(cols),
                by_rows(received.shape[1]),
                whole(low),
                by_rows(1),
                whole(up_own),
                whole(up_other),
            ],
            out_specs=by_rows(cols),
        ),
        out_shape=jax.ShapeDtypeStruct((rows, cols), jnp.bfloat16),
        compiler_params=pltpu.CompilerParams(vmem_limit_bytes=VMEM_LIMIT),
        cost_estimate=QUICK,
    )(half, own, received, low, slot, up_own, up_other)


def output_kernel(places, count, own, other, *refs):
    for w_own, w_other, out in zip(refs[:count], refs[count : 2 * count], refs[2 * count :]):
        total = jnp.dot(own[...], w_own[...], preferred_element_type=jnp.float32)
        total += jnp.dot(other[...], w_other[...], preferred_element_type=jnp.float32)
        out[...] = total.astype(out.dtype)


def output_partial(places, first, count, own, other, weight, weight_other, width):
    rows, depth = own.shape
    tile = width // 2 if width % 256 == 0 else width
    steps = width // tile
    whole = pl.BlockSpec((rows, depth), lambda j, p: (0, 0))
    weights = [
        pl.BlockSpec((depth, tile), lambda j, p, i=i: (0, p[first + i] * steps + j))
        for i in range(count)
    ]

    def kernel(places, *refs):
        output_kernel(places, count, *refs)

    return pl.pallas_call(
        kernel,
        grid_spec=pltpu.PrefetchScalarGridSpec(
            num_scalar_prefetch=1,
            grid=(steps,),
            in_specs=[whole, whole] + weights * 2,
            out_specs=[pl.BlockSpec((rows, tile), lambda j, p: (0, j))] * count,
        ),
        out_shape=[jax.ShapeDtypeStruct((rows, width), jnp.bfloat16)] * count,
        compiler_params=pltpu.CompilerParams(vmem_limit_bytes=VMEM_LIMIT),
        cost_estimate=QUICK,
    )(places, own, other, *[weight] * count, *[weight_other] * count)


def attention(query, cache_length, key_cache, value_cache, k_new, v_new):
    local_reqs = query.shape[0]
    kv_count, _, span, dim = key_cache.shape
    group = HEADS // kv_count
    query = query.reshape(local_reqs, kv_count, group, dim)
    k_new = k_new.reshape(local_reqs, kv_count, dim)
    v_new = v_new.reshape(local_reqs, kv_count, dim)
    live = (jnp.arange(span)[None, :] < cache_length[:, None])[None, :, None, :]
    scores = jnp.einsum("rkge,krje->krgj", query, key_cache, preferred_element_type=jnp.float32)
    fresh = jnp.einsum("rkge,rke->krg", query, k_new, preferred_element_type=jnp.float32)
    scores = jnp.where(live, scores, -jnp.inf)
    top = jnp.maximum(jnp.max(scores, axis=3), fresh)
    expd = jnp.where(live, jnp.exp(scores - top[:, :, :, None]), 0.0)
    expf = jnp.exp(fresh - top)
    total = jnp.sum(expd, axis=3) + expf
    probs = (expd / total[:, :, :, None]).astype(jnp.bfloat16)
    probf = (expf / total).astype(jnp.bfloat16)
    context = jnp.einsum("krgj,krje->rkge", probs, value_cache, preferred_element_type=jnp.float32)
    fresh_part = jnp.einsum("krg,rke->rkge", probf.astype(jnp.float32), v_new.astype(jnp.float32))
    return (context + fresh_part).astype(jnp.bfloat16).reshape(local_reqs, HEADS * dim)


def shift(value, axis, by):
    size = lax.axis_size(axis)
    return lax.ppermute(value, axis, [(i, (i + by) % size) for i in range(size)])


def after(value, *others):
    return lax.optimization_barrier((value, *others))[0]


def gathered_chips():
    layers, sides = lax.axis_size("z"), lax.axis_size("y")
    z, y = lax.axis_index("z"), lax.axis_index("y")
    steps = GATHERED
    if layers != 4 or sides != 2:
        steps = [(-k, side) for k in range(layers) for side in range(sides)]
    return [((z + k) % layers) * sides + (y + side) % sides for k, side in steps]


def gather_features(tokens, down_other, up, begin):
    layers, sides = lax.axis_size("z"), lax.axis_size("y")
    z = lax.axis_index("z")
    if layers != 4 or sides != 2:
        blocks = [shift(tokens, "z", k) if k else tokens for k in range(layers)]
        blocks = [[block, shift(block, "y", 1)][:sides] for block in blocks]
        blocks = [block for pair in blocks for block in pair]
        return begin(blocks[:-1]), blocks[-1:], up
    side = shift(tokens, "y", 1)
    below, above = shift(tokens, "z", 1), shift(tokens, "z", 3)
    below, side, _ = lax.optimization_barrier((below, side, down_other))
    below_side = shift(below, "y", 1)
    from_below = lax.ppermute(below, "z", [(1, 2), (2, 3)])
    above_side = shift(above, "y", 1)
    from_above = lax.ppermute(above, "z", [(2, 1), (1, 0)])
    sums = begin([tokens, side, below, above])
    from_below, from_above, sums = lax.optimization_barrier((from_below, from_above, sums))
    two = jnp.where(z >= 2, from_below, from_above)
    two, _, above_side, up = lax.optimization_barrier((two, below_side, above_side, up))
    return sums, [below_side, above_side, two, shift(two, "y", 1)], up


def scatter_layers(parts):
    layers = lax.axis_size("z")
    wide = lambda value: value.astype(jnp.float32)
    narrow = lambda value: value.astype(jnp.bfloat16)
    if layers != 4:
        return sum([wide(shift(narrow(parts[k]), "z", k)) for k in range(1, layers)], parts[0])
    two = narrow(parts[2])
    up = lax.ppermute(two, "z", [(0, 1), (1, 2)])
    down = lax.ppermute(two, "z", [(3, 2), (2, 1)])
    above = shift(narrow(parts[1] + wide(up)), "z", 1)
    below = shift(narrow(parts[3] + wide(down)), "z", 3)
    return parts[0] + wide(above) + wide(below)


def shards(
    tokens,
    request_adapter,
    adapter_storage_slot,
    cache_length,
    query_weight,
    adapter_down_maps,
    adapter_up_maps,
    key_cache,
    value_cache,
    new_token_key,
    new_token_value,
    output_weight,
):
    layers, sides = lax.axis_size("z"), lax.axis_size("y")
    z, y, core = lax.axis_index("z"), lax.axis_index("y"), lax.axis_index("core")
    rows, width = tokens.shape
    total_adapters = adapter_storage_slot.shape[0]
    rank = adapter_down_maps.shape[2]
    depth = output_weight.shape[0]
    chips_of = lambda layer: [
        (layer % layers) * sides + (y + side) % sides for side in range(sides)
    ]

    down = jnp.swapaxes(adapter_down_maps, 1, 2)
    down_other = shift(down, "core", 1)
    query_weight_other = shift(query_weight, "core", 1)

    ids = request_adapter[:, 0]
    numbers = jnp.arange(total_adapters, dtype=jnp.int32)
    slot = jnp.sum(
        jnp.where(ids[:, None] == numbers[None, :], adapter_storage_slot[None, :], 0), axis=1
    )[:, None]

    out_order = [2, 1, 3, 0] if layers == 4 else list(range(1, layers)) + [0]
    out_keys = [(k, side) for k in out_order for side in reversed(range(sides))]
    chips = gathered_chips()
    out_first = len(chips)
    chips += [chips_of(z + k)[side] for k, side in out_keys]
    places = jnp.stack([2 * chip + core for chip in chips]).astype(jnp.int32)

    weights = query_weight, query_weight_other, down, down_other
    half = lax.axis_index("rep") % 2
    up = jnp.swapaxes(adapter_up_maps, 1, 2)[0]
    up = lax.dynamic_slice_in_dim(up, half * (rank // 2), rank // 2, 0)
    up = lax.all_to_all(up, ADP, split_axis=1, concat_axis=0, tiled=True)
    sums, blocks, up = gather_features(
        tokens, down_other, up, lambda blocks: project(places, 0, blocks, *weights, ())
    )
    up_other = lax.ppermute(up, "rep", [(i, i ^ 1) for i in range(lax.axis_size("rep"))])

    own, sent, low = project(
        after(places, up_other), out_first - len(blocks), blocks, *weights, (*sums, slot)
    )

    low = (low + shift(low, "core", 1)).astype(jnp.bfloat16)
    received = shift(sent, "core", 1)
    if sides == 2:
        low = low + shift(low, "y", 1)
    low, received = lax.optimization_barrier((low, received))
    low = sum([shift(low, "z", k) for k in range(1, layers)], low)

    query = make_query(half.astype(jnp.int32).reshape(1), own, received, low, slot, up, up_other)
    output_weight_other = shift(after(output_weight, query), "core", 1)
    query_local = lax.all_to_all(query, ADP, split_axis=0, concat_axis=1, tiled=True)

    context = attention(
        query_local, cache_length, key_cache, value_cache, new_token_key, new_token_value
    )
    context = jnp.swapaxes(context.reshape(context.shape[0], -1, depth), 0, 1)
    context = lax.all_to_all(context, ADP, split_axis=0, concat_axis=0, tiled=True)
    context = context.reshape(rows, depth)
    context_other = shift(context, "core", 1)

    made = {}
    for first, count in ((0, 1), (1, len(out_keys) - 1)):
        outs = output_partial(
            places,
            out_first + first,
            count,
            context,
            context_other,
            output_weight,
            output_weight_other,
            width,
        )
        made.update(zip(out_keys[first : first + count], outs))
    other_side = {k: shift(made[k, 1], "y", 1) for k in out_order if sides == 2}
    parts = [None] * layers
    for k in out_order:
        parts[k] = after(made[k, 0], made[out_keys[-1]]).astype(jnp.float32)
        if sides == 2:
            parts[k] = parts[k] + other_side[k].astype(jnp.float32)
    return scatter_layers(parts).astype(jnp.bfloat16)


def solution(mesh):
    reps, adp = mesh.shape["rep"], mesh.shape["adp"]
    sides = 2 if adp == 16 else 1
    mesh = Mesh(mesh.devices.reshape(reps, adp // (2 * sides), sides, 2), ("rep",) + ADP)
    in_specs = (
        P("rep", ADP),
        P("rep", None),
        P(),
        P(("rep",) + ADP),
        P(None, ADP),
        P(ADP, None, None),
        P(ADP, None, None),
        P(None, ("rep",) + ADP, None, None),
        P(None, ("rep",) + ADP, None, None),
        P(("rep",) + ADP, None),
        P(("rep",) + ADP, None),
        P(ADP, None),
    )
    return jax.shard_map(
        shards, mesh=mesh, in_specs=in_specs, out_specs=P("rep", ADP), check_vma=False
    )
```

```python
import jax
import jax.numpy as jnp
from jax import lax
from jax.experimental import pallas as pl
from jax.experimental.pallas import tpu as pltpu
from jax.sharding import Mesh
from jax.sharding import PartitionSpec as P

HEADS = 64
HEAD_DIM = 128
ADP = ("z", "y", "core")
GATHERED = ((0, 0), (0, 1), (3, 0), (1, 0), (3, 1), (1, 1), (2, 0), (2, 1))
NT = (((1,), (1,)), ((), ()))
VMEM_LIMIT = 63 << 20
QUICK = pl.CostEstimate(flops=1, bytes_accessed=1, transcendentals=0)


def project_kernel(places, first, count, *refs):
    blocks, w_own, w_other, a_own, a_other = (refs[i * count : (i + 1) * count] for i in range(5))
    ins, outs = refs[5 * count : -3], refs[-3:]
    first_core = places[0] % 2 == 0
    sums = [ref[...] for ref in ins[:3]]
    for i in range(count):
        x = blocks[i][...]
        own, other = a_own[i][0], a_other[i][0]
        pair = jnp.concatenate(
            [jnp.where(first_core, own, other), jnp.where(first_core, other, own)], axis=0
        )
        parts = (
            jnp.dot(x, w_own[i][...], preferred_element_type=jnp.float32),
            jnp.dot(x, w_other[i][...], preferred_element_type=jnp.float32),
            lax.dot_general(x, pair, NT, preferred_element_type=jnp.float32),
        )
        sums = [total + part for total, part in zip(sums, parts)] if sums else parts
    outs[0][...], outs[1][...] = sums[:2]
    low = sums[2]
    if ins:
        slot = ins[3][...]
        rank = low.shape[1] // 2
        mine = places[0] - places[0] % 2
        low = jnp.where(slot == mine, low[:, :rank], 0.0) + jnp.where(
            slot == mine + 1, low[:, rank:], 0.0
        )
        half = low.shape[0] // 2
        low = jnp.concatenate([low[:half], low[half:]], axis=1)
    outs[2][...] = low


def project(places, first, blocks, weight, weight_other, down, down_other, rest):
    count = len(blocks)
    rows, width = blocks[0].shape
    cols, rank = weight.shape[1], down.shape[1]
    flat = lambda shape: pl.BlockSpec(shape, lambda j, p: (0, 0))
    low_rows = rows // 2 if rest else rows
    shapes = [(rows, cols), (rows, cols), (low_rows, 2 * rank)]
    weights = [pl.BlockSpec((width, cols), lambda j, p, i=i: (p[first + i], 0)) for i in range(count)]
    maps = [
        pl.BlockSpec((1, rank, width), lambda j, p, i=i: (0, 0, p[first + i])) for i in range(count)
    ]

    def kernel(places, *refs):
        project_kernel(places, first, count, *refs)

    return pl.pallas_call(
        kernel,
        grid_spec=pltpu.PrefetchScalarGridSpec(
            num_scalar_prefetch=1,
            grid=(1,),
            in_specs=[flat((rows, width))] * count
            + weights * 2
            + maps * 2
            + [flat(array.shape) for array in rest],
            out_specs=[flat(shape) for shape in shapes],
        ),
        out_shape=[jax.ShapeDtypeStruct(shape, jnp.float32) for shape in shapes],
        compiler_params=pltpu.CompilerParams(vmem_limit_bytes=VMEM_LIMIT),
        cost_estimate=pl.CostEstimate(
            flops=4 * count * rows * width * (cols + rank),
            bytes_accessed=2 * count * width * (rows + 2 * cols) + 8 * rows * cols,
            transcendentals=0,
        ),
    )(
        places,
        *blocks,
        *[weight] * count,
        *[weight_other] * count,
        *[down] * count,
        *[down_other] * count,
        *rest,
    )


def query_kernel(half, own, received, low, slot, up_own, up_other, out):
    step = pl.program_id(0)
    lanes = low.shape[1]
    rank = lanes // 2
    part = rank // 2
    depth = up_own.shape[0]
    shape = (lanes, depth)
    lane = lax.broadcasted_iota(jnp.int32, shape, 1) % part
    row = lax.broadcasted_iota(jnp.int32, shape, 0)
    owner = lax.broadcasted_iota(jnp.int32, (own.shape[0], depth), 1) // part
    live = slot[...] == owner
    total = own[...] + received[...]
    for h, up in ((half[0], up_own), (1 - half[0], up_other)):
        copies = (row == lane + rank * step + part * h).astype(jnp.bfloat16)
        spread = jnp.dot(low[...], copies, preferred_element_type=jnp.float32)
        spread = jnp.where(live, spread, 0.0).astype(jnp.bfloat16)
        total += jnp.dot(spread, up[...], preferred_element_type=jnp.float32)
    out[...] = (total * HEAD_DIM ** (-0.5)).astype(out.dtype)


def make_query(half, own, received, low, slot, up_own, up_other):
    rows, cols = own.shape
    tile = rows // 2
    depth = up_own.shape[0]
    by_rows = lambda width: pl.BlockSpec((tile, width), lambda j, h: (j, 0))
    whole = lambda array: pl.BlockSpec(array.shape, lambda j, h: (0, 0))
    return pl.pallas_call(
        query_kernel,
        grid_spec=pltpu.PrefetchScalarGridSpec(
            num_scalar_prefetch=1,
            grid=(2,),
            in_specs=[
                by_rows(cols),
                by_rows(received.shape[1]),
                whole(low),
                by_rows(1),
                whole(up_own),
                whole(up_other),
            ],
            out_specs=by_rows(cols),
        ),
        out_shape=jax.ShapeDtypeStruct((rows, cols), jnp.bfloat16),
        compiler_params=pltpu.CompilerParams(vmem_limit_bytes=VMEM_LIMIT),
        cost_estimate=QUICK,
    )(half, own, received, low, slot, up_own, up_other)


def output_kernel(places, count, own, other, *refs):
    for w_own, w_other, out in zip(refs[:count], refs[count : 2 * count], refs[2 * count :]):
        total = jnp.dot(own[...], w_own[...], preferred_element_type=jnp.float32)
        total += jnp.dot(other[...], w_other[...], preferred_element_type=jnp.float32)
        out[...] = total.astype(out.dtype)


def output_partial(places, first, count, own, other, weight, weight_other, width):
    rows, depth = own.shape
    tile = width // 2 if width % 256 == 0 else width
    steps = width // tile
    whole = pl.BlockSpec((rows, depth), lambda j, p: (0, 0))
    weights = [
        pl.BlockSpec((depth, tile), lambda j, p, i=i: (0, p[first + i] * steps + j))
        for i in range(count)
    ]

    def kernel(places, *refs):
        output_kernel(places, count, *refs)

    return pl.pallas_call(
        kernel,
        grid_spec=pltpu.PrefetchScalarGridSpec(
            num_scalar_prefetch=1,
            grid=(steps,),
            in_specs=[whole, whole] + weights * 2,
            out_specs=[pl.BlockSpec((rows, tile), lambda j, p: (0, j))] * count,
        ),
        out_shape=[jax.ShapeDtypeStruct((rows, width), jnp.bfloat16)] * count,
        compiler_params=pltpu.CompilerParams(vmem_limit_bytes=VMEM_LIMIT),
        cost_estimate=QUICK,
    )(places, own, other, *[weight] * count, *[weight_other] * count)


def attention(query, cache_length, key_cache, value_cache, k_new, v_new):
    local_reqs = query.shape[0]
    kv_count, _, span, dim = key_cache.shape
    group = HEADS // kv_count
    query = query.reshape(local_reqs, kv_count, group, dim)
    k_new = k_new.reshape(local_reqs, kv_count, dim)
    v_new = v_new.reshape(local_reqs, kv_count, dim)
    live = (jnp.arange(span)[None, :] < cache_length[:, None])[None, :, None, :]
    scores = jnp.einsum("rkge,krje->krgj", query, key_cache, preferred_element_type=jnp.float32)
    fresh = jnp.einsum("rkge,rke->krg", query, k_new, preferred_element_type=jnp.float32)
    scores = jnp.where(live, scores, -jnp.inf)
    top = jnp.maximum(jnp.max(scores, axis=3), fresh)
    expd = jnp.where(live, jnp.exp(scores - top[:, :, :, None]), 0.0)
    expf = jnp.exp(fresh - top)
    total = jnp.sum(expd, axis=3) + expf
    probs = (expd / total[:, :, :, None]).astype(jnp.bfloat16)
    probf = (expf / total).astype(jnp.bfloat16)
    context = jnp.einsum("krgj,krje->rkge", probs, value_cache, preferred_element_type=jnp.float32)
    fresh_part = jnp.einsum("krg,rke->rkge", probf.astype(jnp.float32), v_new.astype(jnp.float32))
    return (context + fresh_part).astype(jnp.bfloat16).reshape(local_reqs, HEADS * dim)


def shift(value, axis, by):
    size = lax.axis_size(axis)
    return lax.ppermute(value, axis, [(i, (i + by) % size) for i in range(size)])


def after(value, *others):
    return lax.optimization_barrier((value, *others))[0]


def gathered_chips():
    layers, sides = lax.axis_size("z"), lax.axis_size("y")
    z, y = lax.axis_index("z"), lax.axis_index("y")
    steps = GATHERED
    if layers != 4 or sides != 2:
        steps = [(-k, side) for k in range(layers) for side in range(sides)]
    return [((z + k) % layers) * sides + (y + side) % sides for k, side in steps]


def gather_features(tokens, down_other, up, begin):
    layers, sides = lax.axis_size("z"), lax.axis_size("y")
    z = lax.axis_index("z")
    if layers != 4 or sides != 2:
        blocks = [shift(tokens, "z", k) if k else tokens for k in range(layers)]
        blocks = [[block, shift(block, "y", 1)][:sides] for block in blocks]
        blocks = [block for pair in blocks for block in pair]
        return begin(blocks[:-1]), blocks[-1:], up
    side = shift(tokens, "y", 1)
    below, above = shift(tokens, "z", 1), shift(tokens, "z", 3)
    below, side, _ = lax.optimization_barrier((below, side, down_other))
    below_side = shift(below, "y", 1)
    from_below = lax.ppermute(below, "z", [(1, 2), (2, 3)])
    above_side = shift(above, "y", 1)
    from_above = lax.ppermute(above, "z", [(2, 1), (1, 0)])
    sums = begin([tokens, side, below, above])
    from_below, from_above, sums = lax.optimization_barrier((from_below, from_above, sums))
    two = jnp.where(z >= 2, from_below, from_above)
    two, _, up = lax.optimization_barrier((two, below_side, up))
    two, above_side = lax.optimization_barrier((two, above_side))
    return sums, [below_side, above_side, two, shift(two, "y", 1)], up


def scatter_layers(parts):
    layers = lax.axis_size("z")
    wide = lambda value: value.astype(jnp.float32)
    narrow = lambda value: value.astype(jnp.bfloat16)
    if layers != 4:
        return sum([wide(shift(narrow(parts[k]), "z", k)) for k in range(1, layers)], parts[0])
    two = narrow(parts[2])
    up = lax.ppermute(two, "z", [(0, 1), (1, 2)])
    down = lax.ppermute(two, "z", [(3, 2), (2, 1)])
    above = shift(narrow(parts[1] + wide(up)), "z", 1)
    below = shift(narrow(parts[3] + wide(down)), "z", 3)
    return parts[0] + wide(above) + wide(below)


def shards(
    tokens,
    request_adapter,
    adapter_storage_slot,
    cache_length,
    query_weight,
    adapter_down_maps,
    adapter_up_maps,
    key_cache,
    value_cache,
    new_token_key,
    new_token_value,
    output_weight,
):
    layers, sides = lax.axis_size("z"), lax.axis_size("y")
    z, y, core = lax.axis_index("z"), lax.axis_index("y"), lax.axis_index("core")
    rows, width = tokens.shape
    total_adapters = adapter_storage_slot.shape[0]
    rank = adapter_down_maps.shape[2]
    depth = output_weight.shape[0]
    chips_of = lambda layer: [
        (layer % layers) * sides + (y + side) % sides for side in range(sides)
    ]

    down = jnp.swapaxes(adapter_down_maps, 1, 2)
    down_other = shift(down, "core", 1)
    query_weight_other = shift(query_weight, "core", 1)

    ids = request_adapter[:, 0]
    numbers = jnp.arange(total_adapters, dtype=jnp.int32)
    slot = jnp.sum(
        jnp.where(ids[:, None] == numbers[None, :], adapter_storage_slot[None, :], 0), axis=1
    )[:, None]

    out_order = [2, 1, 3, 0] if layers == 4 else list(range(1, layers)) + [0]
    out_keys = [(k, side) for k in out_order for side in reversed(range(sides))]
    chips = gathered_chips()
    out_first = len(chips)
    chips += [chips_of(z + k)[side] for k, side in out_keys]
    places = jnp.stack([2 * chip + core for chip in chips]).astype(jnp.int32)

    weights = query_weight, query_weight_other, down, down_other
    half = lax.axis_index("rep") % 2
    up = jnp.swapaxes(adapter_up_maps, 1, 2)[0]
    up = lax.dynamic_slice_in_dim(up, half * (rank // 2), rank // 2, 0)
    up = lax.all_to_all(up, ADP, split_axis=1, concat_axis=0, tiled=True)
    sums, blocks, up = gather_features(
        tokens, down_other, up, lambda blocks: project(places, 0, blocks, *weights, ())
    )
    up_other = lax.ppermute(up, "rep", [(i, i ^ 1) for i in range(lax.axis_size("rep"))])

    own, sent, low = project(
        after(places, up_other), out_first - len(blocks), blocks, *weights, (*sums, slot)
    )

    low = (low + shift(low, "core", 1)).astype(jnp.bfloat16)
    received = shift(sent, "core", 1)
    if sides == 2:
        low = low + shift(low, "y", 1)
    low, received = lax.optimization_barrier((low, received))
    low = sum([shift(low, "z", k) for k in range(1, layers)], low)

    query = make_query(half.astype(jnp.int32).reshape(1), own, received, low, slot, up, up_other)
    output_weight_other = shift(after(output_weight, query), "core", 1)
    query_local = lax.all_to_all(query, ADP, split_axis=0, concat_axis=1, tiled=True)

    context = attention(
        query_local, cache_length, key_cache, value_cache, new_token_key, new_token_value
    )
    context = jnp.swapaxes(context.reshape(context.shape[0], -1, depth), 0, 1)
    context = lax.all_to_all(context, ADP, split_axis=0, concat_axis=0, tiled=True)
    context = context.reshape(rows, depth)
    context_other = shift(context, "core", 1)

    made = {}
    for first, count in ((0, 1), (1, len(out_keys) - 1)):
        outs = output_partial(
            places,
            out_first + first,
            count,
            context,
            context_other,
            output_weight,
            output_weight_other,
            width,
        )
        made.update(zip(out_keys[first : first + count], outs))
    other_side = {k: shift(made[k, 1], "y", 1) for k in out_order if sides == 2}
    parts = [None] * layers
    for k in out_order:
        parts[k] = after(made[k, 0], made[out_keys[-1]]).astype(jnp.float32)
        if sides == 2:
            parts[k] = parts[k] + other_side[k].astype(jnp.float32)
    return scatter_layers(parts).astype(jnp.bfloat16)


def solution(mesh):
    reps, adp = mesh.shape["rep"], mesh.shape["adp"]
    sides = 2 if adp == 16 else 1
    mesh = Mesh(mesh.devices.reshape(reps, adp // (2 * sides), sides, 2), ("rep",) + ADP)
    in_specs = (
        P("rep", ADP),
        P("rep", None),
        P(),
        P(("rep",) + ADP),
        P(None, ADP),
        P(ADP, None, None),
        P(ADP, None, None),
        P(None, ("rep",) + ADP, None, None),
        P(None, ("rep",) + ADP, None, None),
        P(("rep",) + ADP, None),
        P(("rep",) + ADP, None),
        P(ADP, None),
    )
    return jax.shard_map(
        shards, mesh=mesh, in_specs=in_specs, out_specs=P("rep", ADP), check_vma=False
    )
```

```python
import jax
import jax.numpy as jnp
from jax import lax
from jax.experimental import pallas as pl
from jax.experimental.pallas import tpu as pltpu
from jax.sharding import Mesh
from jax.sharding import PartitionSpec as P

HEADS = 64
HEAD_DIM = 128
ADP = ("z", "y", "core")
GATHERED = ((0, 0), (0, 1), (3, 0), (1, 0), (3, 1), (1, 1), (2, 0), (2, 1))
NT = (((1,), (1,)), ((), ()))
VMEM_LIMIT = 63 << 20
QUICK = pl.CostEstimate(flops=1, bytes_accessed=1, transcendentals=0)


def project_kernel(places, first, count, *refs):
    blocks, w_own, w_other, a_own, a_other = (refs[i * count : (i + 1) * count] for i in range(5))
    ins, outs = refs[5 * count : -3], refs[-3:]
    first_core = places[0] % 2 == 0
    sums = [ref[...] for ref in ins[:3]]
    for i in range(count):
        x = blocks[i][...]
        own, other = a_own[i][0], a_other[i][0]
        pair = jnp.concatenate(
            [jnp.where(first_core, own, other), jnp.where(first_core, other, own)], axis=0
        )
        parts = (
            jnp.dot(x, w_own[i][...], preferred_element_type=jnp.float32),
            jnp.dot(x, w_other[i][...], preferred_element_type=jnp.float32),
            lax.dot_general(x, pair, NT, preferred_element_type=jnp.float32),
        )
        sums = [total + part for total, part in zip(sums, parts)] if sums else parts
    outs[0][...], outs[1][...] = sums[:2]
    low = sums[2]
    if ins:
        slot = ins[3][...]
        rank = low.shape[1] // 2
        mine = places[0] - places[0] % 2
        low = jnp.where(slot == mine, low[:, :rank], 0.0) + jnp.where(
            slot == mine + 1, low[:, rank:], 0.0
        )
        half = low.shape[0] // 2
        low = jnp.concatenate([low[:half], low[half:]], axis=1)
    outs[2][...] = low


def project(places, first, blocks, weight, weight_other, down, down_other, rest):
    count = len(blocks)
    rows, width = blocks[0].shape
    cols, rank = weight.shape[1], down.shape[1]
    flat = lambda shape: pl.BlockSpec(shape, lambda j, p: (0, 0))
    low_rows = rows // 2 if rest else rows
    shapes = [(rows, cols), (rows, cols), (low_rows, 2 * rank)]
    weights = [pl.BlockSpec((width, cols), lambda j, p, i=i: (p[first + i], 0)) for i in range(count)]
    maps = [
        pl.BlockSpec((1, rank, width), lambda j, p, i=i: (0, 0, p[first + i])) for i in range(count)
    ]

    def kernel(places, *refs):
        project_kernel(places, first, count, *refs)

    return pl.pallas_call(
        kernel,
        grid_spec=pltpu.PrefetchScalarGridSpec(
            num_scalar_prefetch=1,
            grid=(1,),
            in_specs=[flat((rows, width))] * count
            + weights * 2
            + maps * 2
            + [flat(array.shape) for array in rest],
            out_specs=[flat(shape) for shape in shapes],
        ),
        out_shape=[jax.ShapeDtypeStruct(shape, jnp.float32) for shape in shapes],
        compiler_params=pltpu.CompilerParams(vmem_limit_bytes=VMEM_LIMIT),
        cost_estimate=pl.CostEstimate(
            flops=4 * count * rows * width * (cols + rank),
            bytes_accessed=2 * count * width * (rows + 2 * cols) + 8 * rows * cols,
            transcendentals=0,
        ),
    )(
        places,
        *blocks,
        *[weight] * count,
        *[weight_other] * count,
        *[down] * count,
        *[down_other] * count,
        *rest,
    )


def query_kernel(half, own, received, low, slot, up_own, up_other, out):
    step = pl.program_id(0)
    lanes = low.shape[1]
    rank = lanes // 2
    part = rank // 2
    depth = up_own.shape[0]
    shape = (lanes, depth)
    lane = lax.broadcasted_iota(jnp.int32, shape, 1) % part
    row = lax.broadcasted_iota(jnp.int32, shape, 0)
    owner = lax.broadcasted_iota(jnp.int32, (own.shape[0], depth), 1) // part
    live = slot[...] == owner
    total = own[...] + received[...]
    for h, up in ((half[0], up_own), (1 - half[0], up_other)):
        copies = (row == lane + rank * step + part * h).astype(jnp.bfloat16)
        spread = jnp.dot(low[...], copies, preferred_element_type=jnp.float32)
        spread = jnp.where(live, spread, 0.0).astype(jnp.bfloat16)
        total += jnp.dot(spread, up[...], preferred_element_type=jnp.float32)
    out[...] = (total * HEAD_DIM ** (-0.5)).astype(out.dtype)


def make_query(half, own, received, low, slot, up_own, up_other):
    rows, cols = own.shape
    tile = rows // 2
    depth = up_own.shape[0]
    by_rows = lambda width: pl.BlockSpec((tile, width), lambda j, h: (j, 0))
    whole = lambda array: pl.BlockSpec(array.shape, lambda j, h: (0, 0))
    return pl.pallas_call(
        query_kernel,
        grid_spec=pltpu.PrefetchScalarGridSpec(
            num_scalar_prefetch=1,
            grid=(2,),
            in_specs=[
                by_rows(cols),
                by_rows(received.shape[1]),
                whole(low),
                by_rows(1),
                whole(up_own),
                whole(up_other),
            ],
            out_specs=by_rows(cols),
        ),
        out_shape=jax.ShapeDtypeStruct((rows, cols), jnp.bfloat16),
        compiler_params=pltpu.CompilerParams(vmem_limit_bytes=VMEM_LIMIT),
        cost_estimate=QUICK,
    )(half, own, received, low, slot, up_own, up_other)


def output_kernel(places, count, own, other, *refs):
    for w_own, w_other, out in zip(refs[:count], refs[count : 2 * count], refs[2 * count :]):
        total = jnp.dot(own[...], w_own[...], preferred_element_type=jnp.float32)
        total += jnp.dot(other[...], w_other[...], preferred_element_type=jnp.float32)
        out[...] = total.astype(out.dtype)


def output_partial(places, first, count, own, other, weight, weight_other, width):
    rows, depth = own.shape
    tile = width // 2 if width % 256 == 0 else width
    steps = width // tile
    whole = pl.BlockSpec((rows, depth), lambda j, p: (0, 0))
    weights = [
        pl.BlockSpec((depth, tile), lambda j, p, i=i: (0, p[first + i] * steps + j))
        for i in range(count)
    ]

    def kernel(places, *refs):
        output_kernel(places, count, *refs)

    return pl.pallas_call(
        kernel,
        grid_spec=pltpu.PrefetchScalarGridSpec(
            num_scalar_prefetch=1,
            grid=(steps,),
            in_specs=[whole, whole] + weights * 2,
            out_specs=[pl.BlockSpec((rows, tile), lambda j, p: (0, j))] * count,
        ),
        out_shape=[jax.ShapeDtypeStruct((rows, width), jnp.bfloat16)] * count,
        compiler_params=pltpu.CompilerParams(vmem_limit_bytes=VMEM_LIMIT),
        cost_estimate=QUICK,
    )(places, own, other, *[weight] * count, *[weight_other] * count)


def attention(query, cache_length, key_cache, value_cache, k_new, v_new):
    local_reqs = query.shape[0]
    kv_count, _, span, dim = key_cache.shape
    group = HEADS // kv_count
    query = query.reshape(local_reqs, kv_count, group, dim)
    k_new = k_new.reshape(local_reqs, kv_count, dim)
    v_new = v_new.reshape(local_reqs, kv_count, dim)
    live = (jnp.arange(span)[None, :] < cache_length[:, None])[None, :, None, :]
    scores = jnp.einsum("rkge,krje->krgj", query, key_cache, preferred_element_type=jnp.float32)
    fresh = jnp.einsum("rkge,rke->krg", query, k_new, preferred_element_type=jnp.float32)
    scores = jnp.where(live, scores, -jnp.inf)
    top = jnp.maximum(jnp.max(scores, axis=3), fresh)
    expd = jnp.where(live, jnp.exp(scores - top[:, :, :, None]), 0.0)
    expf = jnp.exp(fresh - top)
    total = jnp.sum(expd, axis=3) + expf
    probs = (expd / total[:, :, :, None]).astype(jnp.bfloat16)
    probf = (expf / total).astype(jnp.bfloat16)
    context = jnp.einsum("krgj,krje->rkge", probs, value_cache, preferred_element_type=jnp.float32)
    fresh_part = jnp.einsum("krg,rke->rkge", probf.astype(jnp.float32), v_new.astype(jnp.float32))
    return (context + fresh_part).astype(jnp.bfloat16).reshape(local_reqs, HEADS * dim)


def shift(value, axis, by):
    size = lax.axis_size(axis)
    return lax.ppermute(value, axis, [(i, (i + by) % size) for i in range(size)])


def after(value, *others):
    return lax.optimization_barrier((value, *others))[0]


def gathered_chips():
    layers, sides = lax.axis_size("z"), lax.axis_size("y")
    z, y = lax.axis_index("z"), lax.axis_index("y")
    steps = GATHERED
    if layers != 4 or sides != 2:
        steps = [(-k, side) for k in range(layers) for side in range(sides)]
    return [((z + k) % layers) * sides + (y + side) % sides for k, side in steps]


def gather_features(tokens, down_other, up, begin):
    layers, sides = lax.axis_size("z"), lax.axis_size("y")
    z = lax.axis_index("z")
    if layers != 4 or sides != 2:
        blocks = [shift(tokens, "z", k) if k else tokens for k in range(layers)]
        blocks = [[block, shift(block, "y", 1)][:sides] for block in blocks]
        blocks = [block for pair in blocks for block in pair]
        return begin(blocks[:-1]), blocks[-1:], up
    side = shift(tokens, "y", 1)
    below, above = shift(tokens, "z", 1), shift(tokens, "z", 3)
    below, side, _ = lax.optimization_barrier((below, side, down_other))
    below_side = shift(below, "y", 1)
    from_below = lax.ppermute(after(below, below_side), "z", [(1, 2), (2, 3)])
    above_side = shift(above, "y", 1)
    from_above = lax.ppermute(above, "z", [(2, 1), (1, 0)])
    sums = begin([tokens, side, below, above])
    from_below, from_above, sums = lax.optimization_barrier((from_below, from_above, sums))
    two = jnp.where(z >= 2, from_below, from_above)
    two, _, up = lax.optimization_barrier((two, below_side, up))
    two, above_side = lax.optimization_barrier((two, above_side))
    return sums, [below_side, above_side, two, shift(two, "y", 1)], up


def scatter_layers(parts):
    layers = lax.axis_size("z")
    wide = lambda value: value.astype(jnp.float32)
    narrow = lambda value: value.astype(jnp.bfloat16)
    if layers != 4:
        return sum([wide(shift(narrow(parts[k]), "z", k)) for k in range(1, layers)], parts[0])
    two = narrow(parts[2])
    up = lax.ppermute(two, "z", [(0, 1), (1, 2)])
    down = lax.ppermute(two, "z", [(3, 2), (2, 1)])
    above = shift(narrow(parts[1] + wide(up)), "z", 1)
    below = shift(narrow(parts[3] + wide(down)), "z", 3)
    return parts[0] + wide(above) + wide(below)


def shards(
    tokens,
    request_adapter,
    adapter_storage_slot,
    cache_length,
    query_weight,
    adapter_down_maps,
    adapter_up_maps,
    key_cache,
    value_cache,
    new_token_key,
    new_token_value,
    output_weight,
):
    layers, sides = lax.axis_size("z"), lax.axis_size("y")
    z, y, core = lax.axis_index("z"), lax.axis_index("y"), lax.axis_index("core")
    rows, width = tokens.shape
    total_adapters = adapter_storage_slot.shape[0]
    rank = adapter_down_maps.shape[2]
    depth = output_weight.shape[0]
    chips_of = lambda layer: [
        (layer % layers) * sides + (y + side) % sides for side in range(sides)
    ]

    down = jnp.swapaxes(adapter_down_maps, 1, 2)
    down_other = shift(down, "core", 1)
    query_weight_other = shift(query_weight, "core", 1)

    ids = request_adapter[:, 0]
    numbers = jnp.arange(total_adapters, dtype=jnp.int32)
    slot = jnp.sum(
        jnp.where(ids[:, None] == numbers[None, :], adapter_storage_slot[None, :], 0), axis=1
    )[:, None]

    out_order = [2, 1, 3, 0] if layers == 4 else list(range(1, layers)) + [0]
    out_keys = [(k, side) for k in out_order for side in reversed(range(sides))]
    chips = gathered_chips()
    out_first = len(chips)
    chips += [chips_of(z + k)[side] for k, side in out_keys]
    places = jnp.stack([2 * chip + core for chip in chips]).astype(jnp.int32)

    weights = query_weight, query_weight_other, down, down_other
    half = lax.axis_index("rep") % 2
    up = jnp.swapaxes(adapter_up_maps, 1, 2)[0]
    up = lax.dynamic_slice_in_dim(up, half * (rank // 2), rank // 2, 0)
    up = lax.all_to_all(up, ADP, split_axis=1, concat_axis=0, tiled=True)
    sums, blocks, up = gather_features(
        tokens, down_other, up, lambda blocks: project(places, 0, blocks, *weights, ())
    )
    up_other = lax.ppermute(up, "rep", [(i, i ^ 1) for i in range(lax.axis_size("rep"))])

    own, sent, low = project(
        after(places, up_other), out_first - len(blocks), blocks, *weights, (*sums, slot)
    )

    low = (low + shift(low, "core", 1)).astype(jnp.bfloat16)
    received = shift(sent, "core", 1)
    if sides == 2:
        low = low + shift(low, "y", 1)
    low, received = lax.optimization_barrier((low, received))
    low = sum([shift(low, "z", k) for k in range(1, layers)], low)

    query = make_query(half.astype(jnp.int32).reshape(1), own, received, low, slot, up, up_other)
    output_weight_other = shift(after(output_weight, query), "core", 1)
    query_local = lax.all_to_all(query, ADP, split_axis=0, concat_axis=1, tiled=True)

    context = attention(
        query_local, cache_length, key_cache, value_cache, new_token_key, new_token_value
    )
    context = jnp.swapaxes(context.reshape(context.shape[0], -1, depth), 0, 1)
    context = lax.all_to_all(context, ADP, split_axis=0, concat_axis=0, tiled=True)
    context = context.reshape(rows, depth)
    context_other = shift(context, "core", 1)

    made = {}
    for first, count in ((0, 1), (1, len(out_keys) - 1)):
        outs = output_partial(
            places,
            out_first + first,
            count,
            context,
            context_other,
            output_weight,
            output_weight_other,
            width,
        )
        made.update(zip(out_keys[first : first + count], outs))
    other_side = {k: shift(made[k, 1], "y", 1) for k in out_order if sides == 2}
    parts = [None] * layers
    for k in out_order:
        parts[k] = after(made[k, 0], made[out_keys[-1]]).astype(jnp.float32)
        if sides == 2:
            parts[k] = parts[k] + other_side[k].astype(jnp.float32)
    return scatter_layers(parts).astype(jnp.bfloat16)


def solution(mesh):
    reps, adp = mesh.shape["rep"], mesh.shape["adp"]
    sides = 2 if adp == 16 else 1
    mesh = Mesh(mesh.devices.reshape(reps, adp // (2 * sides), sides, 2), ("rep",) + ADP)
    in_specs = (
        P("rep", ADP),
        P("rep", None),
        P(),
        P(("rep",) + ADP),
        P(None, ADP),
        P(ADP, None, None),
        P(ADP, None, None),
        P(None, ("rep",) + ADP, None, None),
        P(None, ("rep",) + ADP, None, None),
        P(("rep",) + ADP, None),
        P(("rep",) + ADP, None),
        P(ADP, None),
    )
    return jax.shard_map(
        shards, mesh=mesh, in_specs=in_specs, out_specs=P("rep", ADP), check_vma=False
    )
```

```python
import jax
import jax.numpy as jnp
from jax import lax
from jax.experimental import pallas as pl
from jax.experimental.pallas import tpu as pltpu
from jax.sharding import Mesh
from jax.sharding import PartitionSpec as P

HEADS = 64
HEAD_DIM = 128
ADP = ("z", "y", "core")
GATHERED = ((0, 0), (0, 1), (3, 0), (1, 0), (3, 1), (1, 1), (2, 0), (2, 1))
NT = (((1,), (1,)), ((), ()))
VMEM_LIMIT = 63 << 20
QUICK = pl.CostEstimate(flops=1, bytes_accessed=1, transcendentals=0)


def project_kernel(places, first, count, *refs):
    blocks, w_own, w_other, a_own, a_other = (refs[i * count : (i + 1) * count] for i in range(5))
    ins, outs = refs[5 * count : -3], refs[-3:]
    first_core = places[0] % 2 == 0
    sums = [ref[...] for ref in ins[:3]]
    for i in range(count):
        x = blocks[i][...]
        own, other = a_own[i][0], a_other[i][0]
        pair = jnp.concatenate(
            [jnp.where(first_core, own, other), jnp.where(first_core, other, own)], axis=0
        )
        parts = (
            jnp.dot(x, w_own[i][...], preferred_element_type=jnp.float32),
            jnp.dot(x, w_other[i][...], preferred_element_type=jnp.float32),
            lax.dot_general(x, pair, NT, preferred_element_type=jnp.float32),
        )
        sums = [total + part for total, part in zip(sums, parts)] if sums else parts
    outs[0][...], outs[1][...] = sums[:2]
    low = sums[2]
    if ins:
        slot = ins[3][...]
        rank = low.shape[1] // 2
        mine = places[0] - places[0] % 2
        low = jnp.where(slot == mine, low[:, :rank], 0.0) + jnp.where(
            slot == mine + 1, low[:, rank:], 0.0
        )
        half = low.shape[0] // 2
        low = jnp.concatenate([low[:half], low[half:]], axis=1)
    outs[2][...] = low


def project(places, first, blocks, weight, weight_other, down, down_other, rest):
    count = len(blocks)
    rows, width = blocks[0].shape
    cols, rank = weight.shape[1], down.shape[1]
    flat = lambda shape: pl.BlockSpec(shape, lambda j, p: (0, 0))
    low_rows = rows // 2 if rest else rows
    shapes = [(rows, cols), (rows, cols), (low_rows, 2 * rank)]
    weights = [pl.BlockSpec((width, cols), lambda j, p, i=i: (p[first + i], 0)) for i in range(count)]
    maps = [
        pl.BlockSpec((1, rank, width), lambda j, p, i=i: (0, 0, p[first + i])) for i in range(count)
    ]

    def kernel(places, *refs):
        project_kernel(places, first, count, *refs)

    return pl.pallas_call(
        kernel,
        grid_spec=pltpu.PrefetchScalarGridSpec(
            num_scalar_prefetch=1,
            grid=(1,),
            in_specs=[flat((rows, width))] * count
            + weights * 2
            + maps * 2
            + [flat(array.shape) for array in rest],
            out_specs=[flat(shape) for shape in shapes],
        ),
        out_shape=[jax.ShapeDtypeStruct(shape, jnp.float32) for shape in shapes],
        compiler_params=pltpu.CompilerParams(vmem_limit_bytes=VMEM_LIMIT),
        cost_estimate=pl.CostEstimate(
            flops=4 * count * rows * width * (cols + rank),
            bytes_accessed=2 * count * width * (rows + 2 * cols) + 8 * rows * cols,
            transcendentals=0,
        ),
    )(
        places,
        *blocks,
        *[weight] * count,
        *[weight_other] * count,
        *[down] * count,
        *[down_other] * count,
        *rest,
    )


def query_kernel(half, own, received, low, slot, up_own, up_other, out):
    step = pl.program_id(0)
    lanes = low.shape[1]
    rank = lanes // 2
    part = rank // 2
    depth = up_own.shape[0]
    shape = (lanes, depth)
    lane = lax.broadcasted_iota(jnp.int32, shape, 1) % part
    row = lax.broadcasted_iota(jnp.int32, shape, 0)
    owner = lax.broadcasted_iota(jnp.int32, (own.shape[0], depth), 1) // part
    live = slot[...] == owner
    total = own[...] + received[...]
    for h, up in ((half[0], up_own), (1 - half[0], up_other)):
        copies = (row == lane + rank * step + part * h).astype(jnp.bfloat16)
        spread = jnp.dot(low[...], copies, preferred_element_type=jnp.float32)
        spread = jnp.where(live, spread, 0.0).astype(jnp.bfloat16)
        total += jnp.dot(spread, up[...], preferred_element_type=jnp.float32)
    out[...] = (total * HEAD_DIM ** (-0.5)).astype(out.dtype)


def make_query(half, own, received, low, slot, up_own, up_other):
    rows, cols = own.shape
    tile = rows // 2
    depth = up_own.shape[0]
    by_rows = lambda width: pl.BlockSpec((tile, width), lambda j, h: (j, 0))
    whole = lambda array: pl.BlockSpec(array.shape, lambda j, h: (0, 0))
    return pl.pallas_call(
        query_kernel,
        grid_spec=pltpu.PrefetchScalarGridSpec(
            num_scalar_prefetch=1,
            grid=(2,),
            in_specs=[
                by_rows(cols),
                by_rows(received.shape[1]),
                whole(low),
                by_rows(1),
                whole(up_own),
                whole(up_other),
            ],
            out_specs=by_rows(cols),
        ),
        out_shape=jax.ShapeDtypeStruct((rows, cols), jnp.bfloat16),
        compiler_params=pltpu.CompilerParams(vmem_limit_bytes=VMEM_LIMIT),
        cost_estimate=QUICK,
    )(half, own, received, low, slot, up_own, up_other)


def output_kernel(places, count, own, other, *refs):
    for w_own, w_other, out in zip(refs[:count], refs[count : 2 * count], refs[2 * count :]):
        total = jnp.dot(own[...], w_own[...], preferred_element_type=jnp.float32)
        total += jnp.dot(other[...], w_other[...], preferred_element_type=jnp.float32)
        out[...] = total.astype(out.dtype)


def output_partial(places, first, count, own, other, weight, weight_other, width):
    rows, depth = own.shape
    tile = width // 2 if width % 256 == 0 else width
    steps = width // tile
    whole = pl.BlockSpec((rows, depth), lambda j, p: (0, 0))
    weights = [
        pl.BlockSpec((depth, tile), lambda j, p, i=i: (0, p[first + i] * steps + j))
        for i in range(count)
    ]

    def kernel(places, *refs):
        output_kernel(places, count, *refs)

    return pl.pallas_call(
        kernel,
        grid_spec=pltpu.PrefetchScalarGridSpec(
            num_scalar_prefetch=1,
            grid=(steps,),
            in_specs=[whole, whole] + weights * 2,
            out_specs=[pl.BlockSpec((rows, tile), lambda j, p: (0, j))] * count,
        ),
        out_shape=[jax.ShapeDtypeStruct((rows, width), jnp.bfloat16)] * count,
        compiler_params=pltpu.CompilerParams(vmem_limit_bytes=VMEM_LIMIT),
        cost_estimate=QUICK,
    )(places, own, other, *[weight] * count, *[weight_other] * count)


def attention(query, cache_length, key_cache, value_cache, k_new, v_new):
    local_reqs = query.shape[0]
    kv_count, _, span, dim = key_cache.shape
    group = HEADS // kv_count
    query = query.reshape(local_reqs, kv_count, group, dim)
    k_new = k_new.reshape(local_reqs, kv_count, dim)
    v_new = v_new.reshape(local_reqs, kv_count, dim)
    live = (jnp.arange(span)[None, :] < cache_length[:, None])[None, :, None, :]
    scores = jnp.einsum("rkge,krje->krgj", query, key_cache, preferred_element_type=jnp.float32)
    fresh = jnp.einsum("rkge,rke->krg", query, k_new, preferred_element_type=jnp.float32)
    scores = jnp.where(live, scores, -jnp.inf)
    top = jnp.maximum(jnp.max(scores, axis=3), fresh)
    expd = jnp.where(live, jnp.exp(scores - top[:, :, :, None]), 0.0)
    expf = jnp.exp(fresh - top)
    total = jnp.sum(expd, axis=3) + expf
    probs = (expd / total[:, :, :, None]).astype(jnp.bfloat16)
    probf = (expf / total).astype(jnp.bfloat16)
    context = jnp.einsum("krgj,krje->rkge", probs, value_cache, preferred_element_type=jnp.float32)
    fresh_part = jnp.einsum("krg,rke->rkge", probf.astype(jnp.float32), v_new.astype(jnp.float32))
    return (context + fresh_part).astype(jnp.bfloat16).reshape(local_reqs, HEADS * dim)


def shift(value, axis, by):
    size = lax.axis_size(axis)
    return lax.ppermute(value, axis, [(i, (i + by) % size) for i in range(size)])


def after(value, *others):
    return lax.optimization_barrier((value, *others))[0]


def gathered_chips():
    layers, sides = lax.axis_size("z"), lax.axis_size("y")
    z, y = lax.axis_index("z"), lax.axis_index("y")
    steps = GATHERED
    if layers != 4 or sides != 2:
        steps = [(-k, side) for k in range(layers) for side in range(sides)]
    return [((z + k) % layers) * sides + (y + side) % sides for k, side in steps]


def gather_features(tokens, down_other, up, begin):
    layers, sides = lax.axis_size("z"), lax.axis_size("y")
    z = lax.axis_index("z")
    if layers != 4 or sides != 2:
        blocks = [shift(tokens, "z", k) if k else tokens for k in range(layers)]
        blocks = [[block, shift(block, "y", 1)][:sides] for block in blocks]
        blocks = [block for pair in blocks for block in pair]
        return begin(blocks[:-1]), blocks[-1:], up
    side = shift(tokens, "y", 1)
    below, above = shift(tokens, "z", 1), shift(tokens, "z", 3)
    below, side, _ = lax.optimization_barrier((below, side, down_other))
    below_side = shift(below, "y", 1)
    from_below = lax.ppermute(after(below, below_side), "z", [(1, 2), (2, 3)])
    above_side = shift(above, "y", 1)
    from_above = lax.ppermute(above, "z", [(2, 1), (1, 0)])
    sums = begin([after(tokens, up), side, below, above])
    from_below, from_above, sums = lax.optimization_barrier((from_below, from_above, sums))
    two = jnp.where(z >= 2, from_below, from_above)
    two, _, up = lax.optimization_barrier((two, below_side, up))
    two, above_side = lax.optimization_barrier((two, above_side))
    return sums, [below_side, above_side, two, shift(two, "y", 1)], up


def scatter_layers(parts):
    layers = lax.axis_size("z")
    wide = lambda value: value.astype(jnp.float32)
    narrow = lambda value: value.astype(jnp.bfloat16)
    if layers != 4:
        return sum([wide(shift(narrow(parts[k]), "z", k)) for k in range(1, layers)], parts[0])
    two = narrow(parts[2])
    up = lax.ppermute(two, "z", [(0, 1), (1, 2)])
    down = lax.ppermute(two, "z", [(3, 2), (2, 1)])
    above = shift(narrow(parts[1] + wide(up)), "z", 1)
    below = shift(narrow(parts[3] + wide(down)), "z", 3)
    return parts[0] + wide(above) + wide(below)


def shards(
    tokens,
    request_adapter,
    adapter_storage_slot,
    cache_length,
    query_weight,
    adapter_down_maps,
    adapter_up_maps,
    key_cache,
    value_cache,
    new_token_key,
    new_token_value,
    output_weight,
):
    layers, sides = lax.axis_size("z"), lax.axis_size("y")
    z, y, core = lax.axis_index("z"), lax.axis_index("y"), lax.axis_index("core")
    rows, width = tokens.shape
    total_adapters = adapter_storage_slot.shape[0]
    rank = adapter_down_maps.shape[2]
    depth = output_weight.shape[0]
    chips_of = lambda layer: [
        (layer % layers) * sides + (y + side) % sides for side in range(sides)
    ]

    down = jnp.swapaxes(adapter_down_maps, 1, 2)
    down_other = shift(down, "core", 1)
    query_weight_other = shift(query_weight, "core", 1)

    ids = request_adapter[:, 0]
    numbers = jnp.arange(total_adapters, dtype=jnp.int32)
    slot = jnp.sum(
        jnp.where(ids[:, None] == numbers[None, :], adapter_storage_slot[None, :], 0), axis=1
    )[:, None]

    out_order = [2, 1, 3, 0] if layers == 4 else list(range(1, layers)) + [0]
    out_keys = [(k, side) for k in out_order for side in reversed(range(sides))]
    chips = gathered_chips()
    out_first = len(chips)
    chips += [chips_of(z + k)[side] for k, side in out_keys]
    places = jnp.stack([2 * chip + core for chip in chips]).astype(jnp.int32)

    weights = query_weight, query_weight_other, down, down_other
    half = lax.axis_index("rep") % 2
    up = jnp.swapaxes(adapter_up_maps, 1, 2)[0]
    up = lax.dynamic_slice_in_dim(up, half * (rank // 2), rank // 2, 0)
    up = lax.all_to_all(up, ADP, split_axis=1, concat_axis=0, tiled=True)
    sums, blocks, up = gather_features(
        tokens, down_other, up, lambda blocks: project(places, 0, blocks, *weights, ())
    )
    up_other = lax.ppermute(up, "rep", [(i, i ^ 1) for i in range(lax.axis_size("rep"))])

    own, sent, low = project(
        after(places, up_other), out_first - len(blocks), blocks, *weights, (*sums, slot)
    )

    low = (low + shift(low, "core", 1)).astype(jnp.bfloat16)
    received = shift(sent, "core", 1)
    if sides == 2:
        low = low + shift(low, "y", 1)
    low, received = lax.optimization_barrier((low, received))
    low = sum([shift(low, "z", k) for k in range(1, layers)], low)

    query = make_query(half.astype(jnp.int32).reshape(1), own, received, low, slot, up, up_other)
    output_weight_other = shift(after(output_weight, query), "core", 1)
    query_local = lax.all_to_all(query, ADP, split_axis=0, concat_axis=1, tiled=True)

    context = attention(
        query_local, cache_length, key_cache, value_cache, new_token_key, new_token_value
    )
    context = jnp.swapaxes(context.reshape(context.shape[0], -1, depth), 0, 1)
    context = lax.all_to_all(context, ADP, split_axis=0, concat_axis=0, tiled=True)
    context = context.reshape(rows, depth)
    context_other = shift(context, "core", 1)

    made = {}
    for first, count in ((0, 1), (1, len(out_keys) - 1)):
        outs = output_partial(
            places,
            out_first + first,
            count,
            context,
            context_other,
            output_weight,
            output_weight_other,
            width,
        )
        made.update(zip(out_keys[first : first + count], outs))
    other_side = {k: shift(made[k, 1], "y", 1) for k in out_order if sides == 2}
    parts = [None] * layers
    for k in out_order:
        parts[k] = after(made[k, 0], made[out_keys[-1]]).astype(jnp.float32)
        if sides == 2:
            parts[k] = parts[k] + other_side[k].astype(jnp.float32)
    return scatter_layers(parts).astype(jnp.bfloat16)


def solution(mesh):
    reps, adp = mesh.shape["rep"], mesh.shape["adp"]
    sides = 2 if adp == 16 else 1
    mesh = Mesh(mesh.devices.reshape(reps, adp // (2 * sides), sides, 2), ("rep",) + ADP)
    in_specs = (
        P("rep", ADP),
        P("rep", None),
        P(),
        P(("rep",) + ADP),
        P(None, ADP),
        P(ADP, None, None),
        P(ADP, None, None),
        P(None, ("rep",) + ADP, None, None),
        P(None, ("rep",) + ADP, None, None),
        P(("rep",) + ADP, None),
        P(("rep",) + ADP, None),
        P(ADP, None),
    )
    return jax.shard_map(
        shards, mesh=mesh, in_specs=in_specs, out_specs=P("rep", ADP), check_vma=False
    )
```

```python
import jax
import jax.numpy as jnp
from jax import lax
from jax.experimental import pallas as pl
from jax.experimental.pallas import tpu as pltpu
from jax.sharding import Mesh
from jax.sharding import PartitionSpec as P

HEADS = 64
HEAD_DIM = 128
ADP = ("z", "y", "core")
GATHERED = ((0, 0), (0, 1), (3, 0), (1, 0), (3, 1), (1, 1), (2, 0), (2, 1))
NT = (((1,), (1,)), ((), ()))
VMEM_LIMIT = 56 << 20
QUICK = pl.CostEstimate(flops=1, bytes_accessed=1, transcendentals=0)


def project_kernel(places, first, count, *refs):
    blocks, w_own, w_other, a_own, a_other = (refs[i * count : (i + 1) * count] for i in range(5))
    ins, outs = refs[5 * count : -3], refs[-3:]
    first_core = places[0] % 2 == 0
    sums = [ref[...] for ref in ins[:3]]
    for i in range(count):
        x = blocks[i][...]
        own, other = a_own[i][0], a_other[i][0]
        pair = jnp.concatenate(
            [jnp.where(first_core, own, other), jnp.where(first_core, other, own)], axis=0
        )
        parts = (
            jnp.dot(x, w_own[i][...], preferred_element_type=jnp.float32),
            jnp.dot(x, w_other[i][...], preferred_element_type=jnp.float32),
            lax.dot_general(x, pair, NT, preferred_element_type=jnp.float32),
        )
        sums = [total + part for total, part in zip(sums, parts)] if sums else parts
    outs[0][...], outs[1][...] = sums[:2]
    low = sums[2]
    if ins:
        slot = ins[3][...]
        rank = low.shape[1] // 2
        mine = places[0] - places[0] % 2
        low = jnp.where(slot == mine, low[:, :rank], 0.0) + jnp.where(
            slot == mine + 1, low[:, rank:], 0.0
        )
        half = low.shape[0] // 2
        low = jnp.concatenate([low[:half], low[half:]], axis=1)
    outs[2][...] = low


def project(places, first, blocks, weight, weight_other, down, down_other, rest):
    count = len(blocks)
    rows, width = blocks[0].shape
    cols, rank = weight.shape[1], down.shape[1]
    flat = lambda shape: pl.BlockSpec(shape, lambda j, p: (0, 0))
    low_rows = rows // 2 if rest else rows
    shapes = [(rows, cols), (rows, cols), (low_rows, 2 * rank)]
    weights = [pl.BlockSpec((width, cols), lambda j, p, i=i: (p[first + i], 0)) for i in range(count)]
    maps = [
        pl.BlockSpec((1, rank, width), lambda j, p, i=i: (0, 0, p[first + i])) for i in range(count)
    ]

    def kernel(places, *refs):
        project_kernel(places, first, count, *refs)

    return pl.pallas_call(
        kernel,
        grid_spec=pltpu.PrefetchScalarGridSpec(
            num_scalar_prefetch=1,
            grid=(1,),
            in_specs=[flat((rows, width))] * count
            + weights * 2
            + maps * 2
            + [flat(array.shape) for array in rest],
            out_specs=[flat(shape) for shape in shapes],
        ),
        out_shape=[jax.ShapeDtypeStruct(shape, jnp.float32) for shape in shapes],
        compiler_params=pltpu.CompilerParams(vmem_limit_bytes=VMEM_LIMIT),
        cost_estimate=pl.CostEstimate(
            flops=4 * count * rows * width * (cols + rank),
            bytes_accessed=2 * count * width * (rows + 2 * cols) + 8 * rows * cols,
            transcendentals=0,
        ),
    )(
        places,
        *blocks,
        *[weight] * count,
        *[weight_other] * count,
        *[down] * count,
        *[down_other] * count,
        *rest,
    )


def query_kernel(half, own, received, low, slot, up_own, up_other, out):
    step = pl.program_id(0)
    lanes = low.shape[1]
    rank = lanes // 2
    part = rank // 2
    depth = up_own.shape[0]
    shape = (lanes, depth)
    lane = lax.broadcasted_iota(jnp.int32, shape, 1) % part
    row = lax.broadcasted_iota(jnp.int32, shape, 0)
    owner = lax.broadcasted_iota(jnp.int32, (own.shape[0], depth), 1) // part
    live = slot[...] == owner
    total = own[...] + received[...]
    for h, up in ((half[0], up_own), (1 - half[0], up_other)):
        copies = (row == lane + rank * step + part * h).astype(jnp.bfloat16)
        spread = jnp.dot(low[...], copies, preferred_element_type=jnp.float32)
        spread = jnp.where(live, spread, 0.0).astype(jnp.bfloat16)
        total += jnp.dot(spread, up[...], preferred_element_type=jnp.float32)
    out[...] = (total * HEAD_DIM ** (-0.5)).astype(out.dtype)


def make_query(half, own, received, low, slot, up_own, up_other):
    rows, cols = own.shape
    tile = rows // 2
    depth = up_own.shape[0]
    by_rows = lambda width: pl.BlockSpec((tile, width), lambda j, h: (j, 0))
    whole = lambda array: pl.BlockSpec(array.shape, lambda j, h: (0, 0))
    return pl.pallas_call(
        query_kernel,
        grid_spec=pltpu.PrefetchScalarGridSpec(
            num_scalar_prefetch=1,
            grid=(2,),
            in_specs=[
                by_rows(cols),
                by_rows(received.shape[1]),
                whole(low),
                by_rows(1),
                whole(up_own),
                whole(up_other),
            ],
            out_specs=by_rows(cols),
        ),
        out_shape=jax.ShapeDtypeStruct((rows, cols), jnp.bfloat16),
        compiler_params=pltpu.CompilerParams(vmem_limit_bytes=VMEM_LIMIT),
        cost_estimate=QUICK,
    )(half, own, received, low, slot, up_own, up_other)


def output_kernel(places, count, own, other, *refs):
    for w_own, w_other, out in zip(refs[:count], refs[count : 2 * count], refs[2 * count :]):
        total = jnp.dot(own[...], w_own[...], preferred_element_type=jnp.float32)
        total += jnp.dot(other[...], w_other[...], preferred_element_type=jnp.float32)
        out[...] = total.astype(out.dtype)


def output_partial(places, first, count, own, other, weight, weight_other, width):
    rows, depth = own.shape
    tile = width // 2 if width % 256 == 0 else width
    steps = width // tile
    whole = pl.BlockSpec((rows, depth), lambda j, p: (0, 0))
    weights = [
        pl.BlockSpec((depth, tile), lambda j, p, i=i: (0, p[first + i] * steps + j))
        for i in range(count)
    ]

    def kernel(places, *refs):
        output_kernel(places, count, *refs)

    return pl.pallas_call(
        kernel,
        grid_spec=pltpu.PrefetchScalarGridSpec(
            num_scalar_prefetch=1,
            grid=(steps,),
            in_specs=[whole, whole] + weights * 2,
            out_specs=[pl.BlockSpec((rows, tile), lambda j, p: (0, j))] * count,
        ),
        out_shape=[jax.ShapeDtypeStruct((rows, width), jnp.bfloat16)] * count,
        compiler_params=pltpu.CompilerParams(vmem_limit_bytes=VMEM_LIMIT),
        cost_estimate=QUICK,
    )(places, own, other, *[weight] * count, *[weight_other] * count)


def attention(query, cache_length, key_cache, value_cache, k_new, v_new):
    local_reqs = query.shape[0]
    kv_count, _, span, dim = key_cache.shape
    group = HEADS // kv_count
    query = query.reshape(local_reqs, kv_count, group, dim)
    k_new = k_new.reshape(local_reqs, kv_count, dim)
    v_new = v_new.reshape(local_reqs, kv_count, dim)
    live = (jnp.arange(span)[None, :] < cache_length[:, None])[None, :, None, :]
    scores = jnp.einsum("rkge,krje->krgj", query, key_cache, preferred_element_type=jnp.float32)
    fresh = jnp.einsum("rkge,rke->krg", query, k_new, preferred_element_type=jnp.float32)
    scores = jnp.where(live, scores, -jnp.inf)
    top = jnp.maximum(jnp.max(scores, axis=3), fresh)
    expd = jnp.where(live, jnp.exp(scores - top[:, :, :, None]), 0.0)
    expf = jnp.exp(fresh - top)
    total = jnp.sum(expd, axis=3) + expf
    probs = (expd / total[:, :, :, None]).astype(jnp.bfloat16)
    probf = (expf / total).astype(jnp.bfloat16)
    context = jnp.einsum("krgj,krje->rkge", probs, value_cache, preferred_element_type=jnp.float32)
    fresh_part = jnp.einsum("krg,rke->rkge", probf.astype(jnp.float32), v_new.astype(jnp.float32))
    return (context + fresh_part).astype(jnp.bfloat16).reshape(local_reqs, HEADS * dim)


def shift(value, axis, by):
    size = lax.axis_size(axis)
    return lax.ppermute(value, axis, [(i, (i + by) % size) for i in range(size)])


def after(value, *others):
    return lax.optimization_barrier((value, *others))[0]


def gathered_chips():
    layers, sides = lax.axis_size("z"), lax.axis_size("y")
    z, y = lax.axis_index("z"), lax.axis_index("y")
    steps = GATHERED
    if layers != 4 or sides != 2:
        steps = [(-k, side) for k in range(layers) for side in range(sides)]
    return [((z + k) % layers) * sides + (y + side) % sides for k, side in steps]


def gather_features(tokens, down_other, up, begin):
    layers, sides = lax.axis_size("z"), lax.axis_size("y")
    z = lax.axis_index("z")
    if layers != 4 or sides != 2:
        blocks = [shift(tokens, "z", k) if k else tokens for k in range(layers)]
        blocks = [[block, shift(block, "y", 1)][:sides] for block in blocks]
        blocks = [block for pair in blocks for block in pair]
        return begin(blocks[:-1]), blocks[-1:], up
    side = shift(tokens, "y", 1)
    below, above = shift(tokens, "z", 1), shift(tokens, "z", 3)
    below, side, _ = lax.optimization_barrier((below, side, down_other))
    below_side = shift(below, "y", 1)
    from_below = lax.ppermute(below, "z", [(1, 2), (2, 3)])
    above_side = shift(above, "y", 1)
    from_above = lax.ppermute(above, "z", [(2, 1), (1, 0)])
    sums = begin([tokens, side, below, above])
    from_below, from_above, sums = lax.optimization_barrier((from_below, from_above, sums))
    two = jnp.where(z >= 2, from_below, from_above)
    two, _, above_side, up = lax.optimization_barrier((two, below_side, above_side, up))
    return sums, [below_side, above_side, two, shift(two, "y", 1)], up


def scatter_layers(parts):
    layers = lax.axis_size("z")
    wide = lambda value: value.astype(jnp.float32)
    narrow = lambda value: value.astype(jnp.bfloat16)
    if layers != 4:
        return sum([wide(shift(narrow(parts[k]), "z", k)) for k in range(1, layers)], parts[0])
    two = narrow(parts[2])
    up = lax.ppermute(two, "z", [(0, 1), (1, 2)])
    down = lax.ppermute(two, "z", [(3, 2), (2, 1)])
    early = lax.optimization_barrier(parts[1])
    above = shift(narrow(early + wide(up)), "z", 1)
    below = shift(narrow(parts[3] + wide(down)), "z", 3)
    early = lax.optimization_barrier(parts[0] + wide(above))
    return early + wide(below)


def shards(
    tokens,
    request_adapter,
    adapter_storage_slot,
    cache_length,
    query_weight,
    adapter_down_maps,
    adapter_up_maps,
    key_cache,
    value_cache,
    new_token_key,
    new_token_value,
    output_weight,
):
    layers, sides = lax.axis_size("z"), lax.axis_size("y")
    z, y, core = lax.axis_index("z"), lax.axis_index("y"), lax.axis_index("core")
    rows, width = tokens.shape
    total_adapters = adapter_storage_slot.shape[0]
    rank = adapter_down_maps.shape[2]
    depth = output_weight.shape[0]
    chips_of = lambda layer: [
        (layer % layers) * sides + (y + side) % sides for side in range(sides)
    ]

    down = jnp.swapaxes(adapter_down_maps, 1, 2)
    down_other = shift(down, "core", 1)
    query_weight_other = shift(query_weight, "core", 1)

    ids = request_adapter[:, 0]
    numbers = jnp.arange(total_adapters, dtype=jnp.int32)
    slot = jnp.sum(
        jnp.where(ids[:, None] == numbers[None, :], adapter_storage_slot[None, :], 0), axis=1
    )[:, None]

    out_order = [2, 1, 3, 0] if layers == 4 else list(range(1, layers)) + [0]
    out_keys = [(k, side) for k in out_order for side in reversed(range(sides))]
    chips = gathered_chips()
    out_first = len(chips)
    chips += [chips_of(z + k)[side] for k, side in out_keys]
    places = jnp.stack([2 * chip + core for chip in chips]).astype(jnp.int32)

    weights = query_weight, query_weight_other, down, down_other
    half = lax.axis_index("rep") % 2
    up = jnp.swapaxes(adapter_up_maps, 1, 2)[0]
    up = lax.dynamic_slice_in_dim(up, half * (rank // 2), rank // 2, 0)
    up = lax.all_to_all(up, ADP, split_axis=1, concat_axis=0, tiled=True)
    sums, blocks, up = gather_features(
        tokens, down_other, up, lambda blocks: project(places, 0, blocks, *weights, ())
    )
    up_other = lax.ppermute(up, "rep", [(i, i ^ 1) for i in range(lax.axis_size("rep"))])

    own, sent, low = project(
        after(places, up_other), out_first - len(blocks), blocks, *weights, (*sums, slot)
    )

    low = (low + shift(low, "core", 1)).astype(jnp.bfloat16)
    received = shift(sent, "core", 1)
    if sides == 2:
        low = low + shift(low, "y", 1)
    low, received = lax.optimization_barrier((low, received))
    low = sum([shift(low, "z", k) for k in range(1, layers)], low)

    query = make_query(half.astype(jnp.int32).reshape(1), own, received, low, slot, up, up_other)
    output_weight_other = shift(after(output_weight, query), "core", 1)
    query_local = lax.all_to_all(query, ADP, split_axis=0, concat_axis=1, tiled=True)

    context = attention(
        query_local, cache_length, key_cache, value_cache, new_token_key, new_token_value
    )
    context = jnp.swapaxes(context.reshape(context.shape[0], -1, depth), 0, 1)
    context = lax.all_to_all(context, ADP, split_axis=0, concat_axis=0, tiled=True)
    context = context.reshape(rows, depth)
    context_other = shift(context, "core", 1)

    made = {}
    for first, count in ((0, 1), (1, len(out_keys) - 1)):
        outs = output_partial(
            places,
            out_first + first,
            count,
            context,
            context_other,
            output_weight,
            output_weight_other,
            width,
        )
        made.update(zip(out_keys[first : first + count], outs))
    other_side = {k: shift(made[k, 1], "y", 1) for k in out_order if sides == 2}
    parts = [None] * layers
    for k in out_order:
        parts[k] = after(made[k, 0], made[out_keys[-1]]).astype(jnp.float32)
        if sides == 2:
            parts[k] = parts[k] + other_side[k].astype(jnp.float32)
    return scatter_layers(parts).astype(jnp.bfloat16)


def solution(mesh):
    reps, adp = mesh.shape["rep"], mesh.shape["adp"]
    sides = 2 if adp == 16 else 1
    mesh = Mesh(mesh.devices.reshape(reps, adp // (2 * sides), sides, 2), ("rep",) + ADP)
    in_specs = (
        P("rep", ADP),
        P("rep", None),
        P(),
        P(("rep",) + ADP),
        P(None, ADP),
        P(ADP, None, None),
        P(ADP, None, None),
        P(None, ("rep",) + ADP, None, None),
        P(None, ("rep",) + ADP, None, None),
        P(("rep",) + ADP, None),
        P(("rep",) + ADP, None),
        P(ADP, None),
    )
    return jax.shard_map(
        shards, mesh=mesh, in_specs=in_specs, out_specs=P("rep", ADP), check_vma=False
    )
```
